32 devices in a mesh: groups: 2 (over x), lib: 16 (over z, y, core).
Axes of the slice: x: 2, y: 2, z: 4, core: 2. Of those that a mesh axis runs over, the one named last changes fastest.
Arguments:
- spectra: bfloat16 [512, 4096], P(('groups', 'lib')), parts along dimension 0, may hold values from -6 to 6
- library: bfloat16 [8192, 4096], P('lib'), may hold values from -6 to 6
- cand_block: int32 [512, 8], P(('groups', 'lib')), parts along dimension 0, may hold values from 0 to 15, all different within a row; in each aligned block of 16 rows (0 to 15, 16 to 31, ...) at most 12 rows name the same one
- cand_local: int32 [512, 8, 8], P(('groups', 'lib')), parts along dimension 0, may hold values from 0 to 511
Outputs:
- profiles: float32 [512, 64, 1024], P(('groups', 'lib')), parts along dimension 0
The draws below stay inside these ranges and needn't reach their ends.
There are 2 independent parts, one for each index of `groups`. The reference program is written for one: setup_inputs(seed, part) draws one part's arguments, and reference() takes and returns one part's arrays. A program takes and returns all parts, laid end to end along the dimension named above; an argument that names none is the same for every part. Nothing has to cross between parts.
Inputs may be any that keep to these rules, and one draw needn't show every extreme that they name: `cand_block`: each query names 8 different blocks; among the 16 queries of one device no block is named by more than 12 of them, and 12 is reached.
All inputs are finite; a program needn't handle non-finite values.
Results may differ from the reference program's by a relative error of at most 0.0029.
Values may be sent and summed in bfloat16 or wider, within the bound.
No kernel may reach another device: no remote copies, remote signals or barrier semaphores. Data moves between devices by JAX's collectives and lax.ppermute only.
A program may use at most 128 MiB of HBM per device.

```python
import math
import jax
import jax.numpy as jnp
import numpy as np
from jax import lax

BINS = 4096
SHIFTS = 1024
HALF = 512
BG = 32
TOUCH = 8
CB = 8
CANDS = 64
Q_DEV = 16
LIB_DEV = 512
RQ = 12
QUERIES = 256
LIBRARY = 8192
N_LIB = 16


def with_ends(array, rng, low, top_value):
    place = [jax.random.randint(jax.random.fold_in(rng, axis), (), 0, length) for axis, length in enumerate(array.shape)]
    main_axis = array.shape.index(max(array.shape))
    beside = place[:main_axis] + [(place[main_axis] + 1) % array.shape[main_axis]] + place[main_axis + 1:]
    return array.at[tuple(place)].set(low).at[tuple(beside)].set(top_value)


def levels(key, extent, shards, least, largest):
    def one(dim, blocks):
        steps = jax.random.uniform(jax.random.fold_in(jax.random.fold_in(key, 6), dim), (blocks,), jnp.float32, least / len(shards), largest / len(shards))
        return jnp.repeat(jnp.exp(steps), extent[dim] // blocks).reshape((-1,) + (1,) * (len(extent) - dim - 1))

    level = one(*shards[0])
    for cut in shards[1:]:
        level = level * one(*cut)
    return level


def assign_block(rng, own, number, rows, number_of, top, most, skew):
    ranking = jax.random.permutation(rng, number_of)
    heavy_load, usual = portions_of(number_of, rows * top, most, skew, True), portions_of(number_of, rows * top, most, skew, False)
    places = jnp.arange(number_of)

    def named(sizes, turn):
        used = int((sizes > 0).sum())
        fixed = max(1, used // 4)
        passed = fixed + (places - fixed + turn * (used - fixed)) % max(1, number_of - fixed)
        return jnp.zeros((number_of,), jnp.int32).at[ranking[jnp.where(places < fixed, places, passed)]].set(jnp.asarray(sizes, jnp.int32))

    sizes = jnp.where(number % 4 == 0, named(heavy_load, number // 4), named(usual, number - number // 4 - 1))
    mixed = jax.random.permutation(jax.random.fold_in(own, 3), number_of)
    source_of, sink = mixed[0:number_of // 2 * 2:2], mixed[1:number_of // 2 * 2:2]
    room = jnp.minimum(sizes[source_of] - 1, most - sizes[sink]) // 2
    room = jnp.where((source_of == ranking[0]) | (sink == ranking[0]) | (sizes[sink] == 0), 0, jnp.maximum(room, 0))
    passed = jax.random.randint(jax.random.fold_in(own, 4), (number_of // 2,), 0, 1 << 20) % (room + 1)
    sizes = sizes.at[source_of].add(-passed).at[sink].add(passed)
    items = jnp.searchsorted(jnp.cumsum(sizes), jnp.arange(rows * top), side="right").astype(jnp.int32)
    table = items.reshape(top, rows).T
    table = table[jax.random.permutation(jax.random.fold_in(own, 1), rows)]
    turn = jax.random.randint(jax.random.fold_in(own, 2), (rows, 1), 0, top)
    return jnp.take_along_axis(table, (jnp.arange(top)[None, :] + turn) % top, axis=1)


def portions_of(count, total, reach, lean, full):
    weights = [(1 << 20) // math.isqrt(rank ** lean) + 1 for rank in range(1, count + 1)]
    largest = reach if full else min(reach, max(-(-total // count), total * weights[0] // sum(weights)))
    least = 1 if total - largest >= count - 1 else 0
    counts, rest = [largest] + [least] * (count - 1), total - largest - least * (count - 1)
    while rest > 0:
        candidates = [i for i in range(1, count) if counts[i] < largest] or [i for i in range(1, count) if counts[i] < reach]
        pool, left = sum([weights[i] for i in candidates]), rest
        for i in candidates:
            addition = min(reach - counts[i], max(1, left * weights[i] // pool), rest)
            counts[i] = counts[i] + addition
            rest = rest - addition
    return np.array(counts)


def scatter_about(rng, extent, deviation, limit, cuts=(), held_as=jnp.bfloat16):
    values = deviation * jax.random.normal(rng, extent, jnp.float32)
    if cuts:
        values = values * levels(rng, extent, cuts, -0.22, 0.18)
    return jnp.clip(values, -limit, limit).astype(held_as)


def setup_inputs(seed: int = 0, part: int = 0) -> dict:
    key_list = jax.random.split(jax.random.key(seed), 5)
    own_keys = jax.random.split(jax.random.fold_in(key_list[4], part), 5)
    spectra = scatter_about(own_keys[0], (QUERIES, BINS), 1.0, 6.0, ((0, 16),))
    library = scatter_about(key_list[1], (LIBRARY, BINS), 1.0, 6.0, ((0, 16),))
    cand_block_keys = jax.random.split(jax.random.fold_in(own_keys[2], 1), QUERIES // Q_DEV)
    cand_block_turns = jax.random.permutation(jax.random.fold_in(own_keys[2], 3), QUERIES // Q_DEV)
    cand_block = jax.vmap(lambda own, number: assign_block(jax.random.fold_in(own_keys[2], 2), own, number, Q_DEV, N_LIB, TOUCH, RQ, 2))(cand_block_keys, cand_block_turns).reshape((QUERIES, TOUCH))
    cand_local = with_ends(jax.random.randint(own_keys[3], (QUERIES, TOUCH, CB), 0, LIB_DEV), jax.random.fold_in(own_keys[3], 1), 0, LIB_DEV - 1).astype(jnp.int32)
    return dict(spectra=spectra, library=library, cand_block=cand_block, cand_local=cand_local)


EPSILON = 1e-06

def prepare(spectra):
    values = spectra.astype(jnp.float32)
    window_sum = lax.reduce_window(values, jnp.float32(0.0), lax.add, (1, 2 * BG + 1), (1, 1), ((0, 0), (BG, BG)))
    centered = values - window_sum / (2 * BG + 1)
    factor = lax.rsqrt(lax.optimization_barrier(jnp.mean(centered * centered, axis=1, keepdims=True)) + EPSILON)
    return (centered * factor).astype(jnp.bfloat16)

def hankel_of(prepared):
    num_query, num_bins = prepared.shape
    width_ext = num_bins + 128
    extended = jnp.concatenate([prepared, jnp.zeros((num_query, 129), prepared.dtype)], axis=1)
    tiled = jnp.tile(extended, (1, 128))[:, :128 * width_ext]
    return tiled.reshape(num_query, 128, width_ext)

def reference(spectra, library, cand_block, cand_local):
    prepared = prepare(spectra)
    cand_index = (cand_block[:, :, None] * LIB_DEV + cand_local).reshape(cand_block.shape[0], -1).astype(jnp.int32)

    def single(operands):
        prep_row, index_row = operands
        cand_rows = library[index_row].astype(jnp.float32)
        scales = lax.rsqrt(lax.optimization_barrier(jnp.mean(cand_rows * cand_rows, axis=1)) + EPSILON)
        padded = jnp.pad(cand_rows, ((0, 0), (HALF, HALF)))
        hankel = hankel_of(prep_row[None, :].astype(jnp.float32))[0]
        width_ext = hankel.shape[1]
        stacked = jnp.stack([padded[:, 128 * offset:128 * offset + width_ext] for offset in range(SHIFTS // 128)], axis=1)
        stacked = stacked.reshape(-1, width_ext)
        values = jnp.dot(stacked, hankel.T, preferred_element_type=jnp.float32).reshape(CANDS, SHIFTS)
        return values * scales[:, None]
    return lax.map(single, (prepared, cand_index))
```

```python
import functools

import jax
import jax.numpy as jnp
from jax import lax
from jax.experimental import pallas as pl
from jax.experimental.pallas import tpu as pltpu
from jax.sharding import PartitionSpec as P

SHIFTS = 1024
BG = 32
EPSILON = 1e-06
LANES = 128
VMEM_LIMIT = 48 * 1024 * 1024
PARTS = 3


def depth_of(num_query, touches, devices):
    return min(num_query, max(3, 3 * num_query * touches // (2 * devices)))


def prepare_kernel(spectra_ref, out_ref, rows_ref):
    num_query, num_bins = spectra_ref.shape
    blocks = num_bins // LANES
    values = spectra_ref[...].astype(jnp.float32)
    zeros = jnp.zeros((num_query, LANES), jnp.float32)
    wide = jnp.concatenate([values, zeros], axis=1)
    total, length = wide, 1
    while length < 2 * BG:
        total = total + pltpu.roll(total, length, 1)
        length *= 2
    total = total + pltpu.roll(wide, length, 1)
    total = pltpu.roll(total, total.shape[1] - BG, 1)[:, :num_bins]
    centered = values - total / (2 * BG + 1)
    factor = lax.rsqrt(jnp.mean(centered * centered, axis=1, keepdims=True) + EPSILON)
    prepared = (centered * factor).astype(jnp.bfloat16)
    row = lax.broadcasted_iota(jnp.int32, (LANES, LANES), 0)
    col = lax.broadcasted_iota(jnp.int32, (LANES, LANES), 1)
    flip = jnp.where(row + col == LANES - 1, 1.0, 0.0).astype(jnp.bfloat16)
    for block in range(blocks):
        piece = prepared[:, block * LANES : (block + 1) * LANES]
        turned = jnp.dot(piece, flip, preferred_element_type=jnp.float32)
        rows_ref[pl.ds(blocks - 1 - block, num_query, stride=blocks), :] = turned
    out_ref[...] = rows_ref[...].reshape(out_ref.shape).astype(jnp.bfloat16)


def prepare(spectra):
    num_query, num_bins = spectra.shape
    blocks = num_bins // LANES
    return pl.pallas_call(
        prepare_kernel,
        out_shape=jax.ShapeDtypeStruct((num_query, blocks, LANES), jnp.bfloat16),
        scratch_shapes=[pltpu.VMEM((num_query * blocks, LANES), jnp.float32)],
        compiler_params=pltpu.CompilerParams(vmem_limit_bytes=VMEM_LIMIT),
        name="prepare",
    )(spectra)


def route_kernel(num_query, touches, depth, me_ref, named_ref, own_ref, slots_ref, returns_ref):
    me = me_ref[0]
    slots = slots_ref.shape[0] - 1
    devices = slots // depth

    @pl.loop(0, slots + 1)
    def _(i):
        slots_ref[i] = -1
        returns_ref[i] = -1

    @pl.loop(0, devices)
    def _(device):
        first = device * num_query

        def query(q, place):
            for t in range(touches):
                touch = (first + q) * touches + t
                hit = named_ref[touch] == me
                slots_ref[place] = jnp.where(hit, touch, -1)
                place = place + hit.astype(jnp.int32)
            return place

        lax.fori_loop(0, num_query, query, device * depth)

    @pl.loop(0, num_query)
    def _(q):
        for t in range(touches):
            touch = q * touches + t
            base = own_ref[touch] * depth
            taken = jnp.int32(0)
            for s in range(depth):
                taken = taken + (returns_ref[base + s] >= 0).astype(jnp.int32)
            returns_ref[base + taken] = touch


def route(me, named, own, num_query, touches, depth):
    devices = named.shape[0] // (num_query * touches)
    smem = pl.BlockSpec(memory_space=pltpu.SMEM)
    table = jax.ShapeDtypeStruct((devices * depth + 1,), jnp.int32)
    return pl.pallas_call(
        functools.partial(route_kernel, num_query, touches, depth),
        out_shape=(table, table),
        in_specs=[smem] * 3,
        out_specs=(smem, smem),
        name="route",
    )(me, named, own)


def profile_kernel(
    part, depth, touches, slots_ref, local_ref, query_ref, library_ref, out_ref,
    cand_ref, left_ref, right_ref,
):
    per_touch = 8
    blocks = query_ref.shape[1]
    offsets = SHIFTS // LANES
    edge = offsets // 2
    part_depth = depth // PARTS
    part_slots = out_ref.shape[0] // per_touch
    tiles = (blocks + 2) // 2
    row = lax.broadcasted_iota(jnp.int32, (8, LANES), 0)
    lane = lax.broadcasted_iota(jnp.int32, (8, LANES), 1)
    lane16 = lax.broadcasted_iota(jnp.int32, (16, LANES), 1)

    cand_ref[...] = jnp.zeros(cand_ref.shape, cand_ref.dtype)
    right_ref[...] = jnp.zeros(right_ref.shape, right_ref.dtype)

    def one(slot, half):
        place = slot // part_depth * depth + part * part_depth + slot % part_depth
        touch = jnp.maximum(slots_ref[place], 0)
        square = jnp.zeros((per_touch, LANES), jnp.float32)
        for k in range(per_touch):
            wanted = local_ref[touch * per_touch + k]
            cand_ref[half, pl.ds(edge * per_touch + k, blocks, stride=per_touch), :] = (
                library_ref[wanted].astype(jnp.float32)
            )
        for b in range(blocks):
            piece = cand_ref[half, pl.ds((edge + b) * per_touch, per_touch), :]
            square = square + piece * piece
        mean = jnp.sum(square, axis=1, keepdims=True) / (blocks * LANES)
        scale = lax.rsqrt(mean + EPSILON)
        for g in range((blocks + offsets) // 2):
            left_ref[half, pl.ds(16 * g, 16), 0:LANES] = cand_ref[
                half, pl.ds(16 * g, 16), :
            ].astype(jnp.bfloat16)
            left_ref[half, pl.ds(16 * g, 16), LANES : 2 * LANES] = cand_ref[
                half, pl.ds(16 * g + 8, 16), :
            ].astype(jnp.bfloat16)

        spectrum = query_ref[touch // touches].astype(jnp.float32)
        zero = jnp.zeros((8, LANES), jnp.float32)
        before = (zero, zero)
        before_shifted = jnp.zeros((16, LANES), jnp.bfloat16)
        for b in range(blocks + 1):
            if b < blocks:
                wide = jnp.broadcast_to(spectrum[b : b + 1, :], (8, LANES))
                now = tuple(
                    pltpu.roll(wide, 1 + 8 * h, 1, stride=1, stride_axis=0) for h in range(2)
                )
            else:
                now = (zero, zero)
            shifted = jnp.concatenate(
                [jnp.where(lane > row + 8 * h, now[h], before[h]) for h in range(2)], axis=0
            ).astype(jnp.bfloat16)
            for a in range(8):
                if a == 0:
                    tile = shifted
                else:
                    tile = pltpu.roll(
                        jnp.where(lane16 < LANES - 16 * a, shifted, before_shifted), 16 * a, 1
                    )
                right_ref[half, pl.ds((blocks - b) * LANES + 16 * a, 16), :] = tile
            before, before_shifted = now, shifted

        left = jnp.concatenate(
            [left_ref[half, pl.ds(16 * u, 8 * offsets), :] for u in range(tiles)], axis=1
        )
        product = jnp.dot(left, right_ref[half], preferred_element_type=jnp.float32)
        return [product[8 * o : 8 * o + 8, :] * scale for o in range(offsets)]

    @pl.loop(0, part_slots // 2)
    def _(pair):
        first = one(2 * pair, 0)
        second = one(2 * pair + 1, 1)
        for o in range(offsets):
            out_ref[pl.ds(pl.multiple_of(16 * pair, 16), 16), o * LANES : (o + 1) * LANES] = (
                jnp.concatenate([first[o], second[o]], axis=0).astype(jnp.bfloat16)
            )


def profile(part, depth, touches, devices, slots, local, queries, library):
    blocks = queries.shape[1]
    offsets = SHIFTS // LANES
    part_slots = devices * depth // PARTS
    rows = (blocks + offsets + 2) * 8
    smem = pl.BlockSpec(memory_space=pltpu.SMEM)
    vmem = pl.BlockSpec(memory_space=pltpu.VMEM)
    flops = part_slots * 2 * 8 * offsets * (blocks + 2) * LANES * LANES
    return pl.pallas_call(
        functools.partial(profile_kernel, part, depth, touches),
        out_shape=jax.ShapeDtypeStruct((part_slots * 8, SHIFTS), jnp.bfloat16),
        in_specs=[smem, smem, vmem, vmem],
        out_specs=vmem,
        scratch_shapes=[
            pltpu.VMEM((2, rows, LANES), jnp.float32),
            pltpu.VMEM((2, (blocks + offsets) * 8, 2 * LANES), jnp.bfloat16),
            pltpu.VMEM((2, (blocks + 2) * LANES, LANES), jnp.bfloat16),
        ],
        compiler_params=pltpu.CompilerParams(vmem_limit_bytes=VMEM_LIMIT),
        cost_estimate=pl.CostEstimate(
            flops=8 * flops, bytes_accessed=8 * 1024 * 1024, transcendentals=0
        ),
        name=f"profile_{part}",
    )(slots, local, queries, library)


def unpack_kernel(part, depth, returns_ref, got_ref, *rest):
    out_ref, stage_ref, sem_ref = rest[-3:]
    part_depth = depth // PARTS
    slots = got_ref.shape[0]

    def copy(slot, touch):
        return pltpu.make_async_copy(stage_ref.at[slot], out_ref.at[touch], sem_ref.at[slot])

    def touch_of(slot):
        return returns_ref[slot // part_depth * depth + part * part_depth + slot % part_depth]

    @pl.loop(0, slots)
    def _(slot):
        touch = touch_of(slot)

        @pl.when(touch >= 0)
        def _():
            stage_ref[slot] = got_ref[slot].astype(jnp.float32)
            copy(slot, touch).start()

    @pl.loop(0, slots)
    def _(slot):
        touch = touch_of(slot)

        @pl.when(touch >= 0)
        def _():
            copy(slot, touch).wait()


def unpack(part, depth, touched, returns, got, out):
    slots, per_touch, shifts = got.shape
    smem = pl.BlockSpec(memory_space=pltpu.SMEM)
    vmem = pl.BlockSpec(memory_space=pltpu.VMEM)
    hbm = pl.BlockSpec(memory_space=pl.ANY)
    more = () if out is None else (out,)
    return pl.pallas_call(
        functools.partial(unpack_kernel, part, depth),
        out_shape=jax.ShapeDtypeStruct((touched, per_touch, shifts), jnp.float32),
        in_specs=[smem, vmem] + [hbm] * len(more),
        out_specs=hbm,
        scratch_shapes=[
            pltpu.VMEM((slots, per_touch, shifts), jnp.float32),
            pltpu.SemaphoreType.DMA((slots,)),
        ],
        input_output_aliases={2: 0} if more else {},
        compiler_params=pltpu.CompilerParams(vmem_limit_bytes=VMEM_LIMIT),
        cost_estimate=pl.CostEstimate(
            flops=0, bytes_accessed=got.size * 6, transcendentals=0
        ),
        name=f"unpack_{part}",
    )(returns, got, *more)


def local(spectra, library, cand_block, cand_local):
    devices = lax.axis_size("lib")
    num_query, num_bins = spectra.shape
    touches, per_touch = cand_local.shape[1], cand_local.shape[2]
    depth = depth_of(num_query, touches, devices)
    blocks = num_bins // LANES
    me = lax.axis_index("lib").astype(jnp.int32).reshape(1)

    own = cand_block.reshape(-1)
    named = lax.all_gather(
        jnp.concatenate([own, cand_local.reshape(-1)]), "lib", axis=0, tiled=False
    )
    named, wanted = named[:, : own.shape[0]], named[:, own.shape[0] :]
    queries = lax.all_gather(prepare(spectra), "lib", axis=0, tiled=True)
    rows = library.reshape(-1, blocks, LANES)
    slots, returns = route(me, named.reshape(-1), own, num_query, touches, depth)

    out = None
    for part in range(PARTS):
        answer = profile(
            part, depth, touches, devices, slots, wanted.reshape(-1), queries, rows
        )
        answer = answer.reshape(devices, depth // PARTS * per_touch, SHIFTS)
        got = lax.all_to_all(answer, "lib", split_axis=0, concat_axis=0, tiled=True)
        got = got.reshape(-1, per_touch, SHIFTS)
        out = unpack(part, depth, num_query * touches, returns, got, out)
    return out.reshape(num_query, touches * per_touch, SHIFTS)


def solution(mesh):
    placed = (
        P(("groups", "lib"), None),
        P("lib", None),
        P(("groups", "lib"), None),
        P(("groups", "lib"), None, None),
    )
    return jax.shard_map(
        local,
        mesh=mesh,
        in_specs=placed,
        out_specs=P(("groups", "lib"), None, None),
        check_vma=False,
    )
```

```python
import functools

import jax
import jax.numpy as jnp
from jax import lax
from jax.experimental import pallas as pl
from jax.experimental.pallas import tpu as pltpu
from jax.sharding import PartitionSpec as P

SHIFTS = 1024
BG = 32
EPSILON = 1e-06
LANES = 128
VMEM_LIMIT = 48 * 1024 * 1024
PARTS = 3
CHAINS = 4


def depth_of(num_query, touches, devices):
    return min(num_query, max(3, 3 * num_query * touches // (2 * devices)))


def prepare_kernel(spectra_ref, out_ref, rows_ref):
    num_query, num_bins = spectra_ref.shape
    blocks = num_bins // LANES
    values = spectra_ref[...].astype(jnp.float32)
    zeros = jnp.zeros((num_query, LANES), jnp.float32)
    wide = jnp.concatenate([values, zeros], axis=1)
    total, length = wide, 1
    while length < 2 * BG:
        total = total + pltpu.roll(total, length, 1)
        length *= 2
    total = total + pltpu.roll(wide, length, 1)
    total = pltpu.roll(total, total.shape[1] - BG, 1)[:, :num_bins]
    centered = values - total / (2 * BG + 1)
    factor = lax.rsqrt(jnp.mean(centered * centered, axis=1, keepdims=True) + EPSILON)
    prepared = (centered * factor).astype(jnp.bfloat16)
    row = lax.broadcasted_iota(jnp.int32, (LANES, LANES), 0)
    col = lax.broadcasted_iota(jnp.int32, (LANES, LANES), 1)
    flip = jnp.where(row + col == LANES - 1, 1.0, 0.0).astype(jnp.bfloat16)
    for block in range(blocks):
        piece = prepared[:, block * LANES : (block + 1) * LANES]
        turned = jnp.dot(piece, flip, preferred_element_type=jnp.float32)
        rows_ref[pl.ds(blocks - 1 - block, num_query, stride=blocks), :] = turned
    out_ref[...] = rows_ref[...].reshape(out_ref.shape).astype(jnp.bfloat16)


def prepare(spectra):
    num_query, num_bins = spectra.shape
    blocks = num_bins // LANES
    return pl.pallas_call(
        prepare_kernel,
        out_shape=jax.ShapeDtypeStruct((num_query, blocks, LANES), jnp.bfloat16),
        scratch_shapes=[pltpu.VMEM((num_query * blocks, LANES), jnp.float32)],
        compiler_params=pltpu.CompilerParams(vmem_limit_bytes=VMEM_LIMIT),
        name="prepare",
    )(spectra)


def route_kernel(num_query, touches, depth, me_ref, named_ref, own_ref, slots_ref, returns_ref):
    me = me_ref[0]
    slots = slots_ref.shape[0] - 1
    devices = slots // depth

    @pl.loop(0, slots + 1)
    def _(i):
        slots_ref[i] = -1
        returns_ref[i] = -1

    @pl.loop(0, devices)
    def _(device):
        first = device * num_query

        def query(q, place):
            for t in range(touches):
                touch = (first + q) * touches + t
                hit = named_ref[touch] == me
                slots_ref[place] = jnp.where(hit, touch, -1)
                place = place + hit.astype(jnp.int32)
            return place

        lax.fori_loop(0, num_query, query, device * depth)

    @pl.loop(0, num_query)
    def _(q):
        for t in range(touches):
            touch = q * touches + t
            base = own_ref[touch] * depth
            taken = jnp.int32(0)
            for s in range(depth):
                taken = taken + (returns_ref[base + s] >= 0).astype(jnp.int32)
            returns_ref[base + taken] = touch


def route(me, named, own, num_query, touches, depth):
    devices = named.shape[0] // (num_query * touches)
    smem = pl.BlockSpec(memory_space=pltpu.SMEM)
    table = jax.ShapeDtypeStruct((devices * depth + 1,), jnp.int32)
    return pl.pallas_call(
        functools.partial(route_kernel, num_query, touches, depth),
        out_shape=(table, table),
        in_specs=[smem] * 3,
        out_specs=(smem, smem),
        name="route",
    )(me, named, own)


def profile_kernel(
    part, depth, touches, slots_ref, local_ref, query_ref, library_ref, out_ref,
    cand_ref, left_ref, right_ref,
):
    per_touch = 8
    blocks = query_ref.shape[1]
    offsets = SHIFTS // LANES
    edge = offsets // 2
    part_depth = depth // PARTS
    part_slots = out_ref.shape[0] // per_touch
    tiles = (blocks + 2) // 2
    row = lax.broadcasted_iota(jnp.int32, (8, LANES), 0)
    lane = lax.broadcasted_iota(jnp.int32, (8, LANES), 1)
    lane16 = lax.broadcasted_iota(jnp.int32, (16, LANES), 1)

    cand_ref[...] = jnp.zeros(cand_ref.shape, cand_ref.dtype)
    right_ref[...] = jnp.zeros(right_ref.shape, right_ref.dtype)

    def one(slot, half):
        place = slot // part_depth * depth + part * part_depth + slot % part_depth
        touch = jnp.maximum(slots_ref[place], 0)
        square = jnp.zeros((per_touch, LANES), jnp.float32)
        for k in range(per_touch):
            wanted = local_ref[touch * per_touch + k]
            cand_ref[half, pl.ds(edge * per_touch + k, blocks, stride=per_touch), :] = (
                library_ref[wanted].astype(jnp.float32)
            )
        for b in range(blocks):
            piece = cand_ref[half, pl.ds((edge + b) * per_touch, per_touch), :]
            square = square + piece * piece
        mean = jnp.sum(square, axis=1, keepdims=True) / (blocks * LANES)
        scale = lax.rsqrt(mean + EPSILON)
        for g in range((blocks + offsets) // 2):
            left_ref[half, pl.ds(16 * g, 16), 0:LANES] = cand_ref[
                half, pl.ds(16 * g, 16), :
            ].astype(jnp.bfloat16)
            left_ref[half, pl.ds(16 * g, 16), LANES : 2 * LANES] = cand_ref[
                half, pl.ds(16 * g + 8, 16), :
            ].astype(jnp.bfloat16)

        spectrum = query_ref[touch // touches].astype(jnp.float32)
        zero = jnp.zeros((8, LANES), jnp.float32)
        before = (zero, zero)
        before_shifted = jnp.zeros((16, LANES), jnp.bfloat16)
        for b in range(blocks + 1):
            if b < blocks:
                wide = jnp.broadcast_to(spectrum[b : b + 1, :], (8, LANES))
                now = tuple(
                    pltpu.roll(wide, 1 + 8 * h, 1, stride=1, stride_axis=0) for h in range(2)
                )
            else:
                now = (zero, zero)
            shifted = jnp.concatenate(
                [jnp.where(lane > row + 8 * h, now[h], before[h]) for h in range(2)], axis=0
            ).astype(jnp.bfloat16)
            for a in range(8):
                if a == 0:
                    tile = shifted
                else:
                    tile = pltpu.roll(
                        jnp.where(lane16 < LANES - 16 * a, shifted, before_shifted), 16 * a, 1
                    )
                right_ref[
                    pl.ds((blocks - b) * LANES + 16 * a, 16), half * LANES : (half + 1) * LANES
                ] = tile
            before, before_shifted = now, shifted
        return scale

    def part_of_sum(low, high):
        left = jnp.concatenate(
            [
                jnp.concatenate(
                    [left_ref[half, pl.ds(16 * u, 8 * offsets), :] for u in range(low, high)],
                    axis=1,
                )
                for half in range(2)
            ],
            axis=0,
        )
        right = right_ref[pl.ds(2 * LANES * low, 2 * LANES * (high - low)), :]
        return jnp.dot(left, right, preferred_element_type=jnp.float32)

    cuts = [tiles * c // CHAINS for c in range(CHAINS + 1)]

    @pl.loop(0, part_slots // 2)
    def _(pair):
        scales = [one(2 * pair, 0), one(2 * pair + 1, 1)]
        product = part_of_sum(cuts[0], cuts[1])
        for c in range(1, CHAINS):
            product = product + part_of_sum(cuts[c], cuts[c + 1])
        for o in range(offsets):
            both = [
                product[
                    (half * offsets + o) * 8 : (half * offsets + o + 1) * 8,
                    half * LANES : (half + 1) * LANES,
                ]
                * scales[half]
                for half in range(2)
            ]
            out_ref[pl.ds(pl.multiple_of(16 * pair, 16), 16), o * LANES : (o + 1) * LANES] = (
                jnp.concatenate(both, axis=0).astype(jnp.bfloat16)
            )


def profile(part, depth, touches, devices, slots, local, queries, library):
    blocks = queries.shape[1]
    offsets = SHIFTS // LANES
    part_slots = devices * depth // PARTS
    rows = (blocks + offsets + 2) * 8
    smem = pl.BlockSpec(memory_space=pltpu.SMEM)
    vmem = pl.BlockSpec(memory_space=pltpu.VMEM)
    flops = part_slots * 2 * 8 * offsets * (blocks + 2) * LANES * LANES
    return pl.pallas_call(
        functools.partial(profile_kernel, part, depth, touches),
        out_shape=jax.ShapeDtypeStruct((part_slots * 8, SHIFTS), jnp.bfloat16),
        in_specs=[smem, smem, vmem, vmem],
        out_specs=vmem,
        scratch_shapes=[
            pltpu.VMEM((2, rows, LANES), jnp.float32),
            pltpu.VMEM((2, (blocks + offsets) * 8, 2 * LANES), jnp.bfloat16),
            pltpu.VMEM(((blocks + 2) * LANES, 2 * LANES), jnp.bfloat16),
        ],
        compiler_params=pltpu.CompilerParams(vmem_limit_bytes=VMEM_LIMIT),
        cost_estimate=pl.CostEstimate(
            flops=8 * flops, bytes_accessed=8 * 1024 * 1024, transcendentals=0
        ),
        name=f"profile_{part}",
    )(slots, local, queries, library)


def unpack_kernel(part, depth, returns_ref, got_ref, *rest):
    out_ref, stage_ref, sem_ref = rest[-3:]
    part_depth = depth // PARTS
    slots = got_ref.shape[0]

    def copy(slot, touch):
        return pltpu.make_async_copy(stage_ref.at[slot], out_ref.at[touch], sem_ref.at[slot])

    def touch_of(slot):
        return returns_ref[slot // part_depth * depth + part * part_depth + slot % part_depth]

    @pl.loop(0, slots)
    def _(slot):
        touch = touch_of(slot)

        @pl.when(touch >= 0)
        def _():
            stage_ref[slot] = got_ref[slot].astype(jnp.float32)
            copy(slot, touch).start()

    @pl.loop(0, slots)
    def _(slot):
        touch = touch_of(slot)

        @pl.when(touch >= 0)
        def _():
            copy(slot, touch).wait()


def unpack(part, depth, touched, returns, got, out):
    slots, per_touch, shifts = got.shape
    smem = pl.BlockSpec(memory_space=pltpu.SMEM)
    vmem = pl.BlockSpec(memory_space=pltpu.VMEM)
    hbm = pl.BlockSpec(memory_space=pl.ANY)
    more = () if out is None else (out,)
    return pl.pallas_call(
        functools.partial(unpack_kernel, part, depth),
        out_shape=jax.ShapeDtypeStruct((touched, per_touch, shifts), jnp.float32),
        in_specs=[smem, vmem] + [hbm] * len(more),
        out_specs=hbm,
        scratch_shapes=[
            pltpu.VMEM((slots, per_touch, shifts), jnp.float32),
            pltpu.SemaphoreType.DMA((slots,)),
        ],
        input_output_aliases={2: 0} if more else {},
        compiler_params=pltpu.CompilerParams(vmem_limit_bytes=VMEM_LIMIT),
        cost_estimate=pl.CostEstimate(
            flops=0, bytes_accessed=got.size * 6, transcendentals=0
        ),
        name=f"unpack_{part}",
    )(returns, got, *more)


def local(spectra, library, cand_block, cand_local):
    devices = lax.axis_size("lib")
    num_query, num_bins = spectra.shape
    touches, per_touch = cand_local.shape[1], cand_local.shape[2]
    depth = depth_of(num_query, touches, devices)
    blocks = num_bins // LANES
    me = lax.axis_index("lib").astype(jnp.int32).reshape(1)

    own = cand_block.reshape(-1)
    named = lax.all_gather(
        jnp.concatenate([own, cand_local.reshape(-1)]), "lib", axis=0, tiled=False
    )
    named, wanted = named[:, : own.shape[0]], named[:, own.shape[0] :]
    queries = lax.all_gather(prepare(spectra), "lib", axis=0, tiled=True)
    rows = library.reshape(-1, blocks, LANES)
    slots, returns = route(me, named.reshape(-1), own, num_query, touches, depth)

    out = None
    for part in range(PARTS):
        answer = profile(
            part, depth, touches, devices, slots, wanted.reshape(-1), queries, rows
        )
        answer = answer.reshape(devices, depth // PARTS * per_touch, SHIFTS)
        got = lax.all_to_all(answer, "lib", split_axis=0, concat_axis=0, tiled=True)
        got = got.reshape(-1, per_touch, SHIFTS)
        out = unpack(part, depth, num_query * touches, returns, got, out)
    return out.reshape(num_query, touches * per_touch, SHIFTS)


def solution(mesh):
    placed = (
        P(("groups", "lib"), None),
        P("lib", None),
        P(("groups", "lib"), None),
        P(("groups", "lib"), None, None),
    )
    return jax.shard_map(
        local,
        mesh=mesh,
        in_specs=placed,
        out_specs=P(("groups", "lib"), None, None),
        check_vma=False,
    )
```

```python
import functools

import jax
import jax.numpy as jnp
from jax import lax
from jax.experimental import pallas as pl
from jax.experimental.pallas import tpu as pltpu
from jax.sharding import PartitionSpec as P

SHIFTS = 1024
BG = 32
EPSILON = 1e-06
LANES = 128
VMEM_LIMIT = 48 * 1024 * 1024
PARTS = 3
CHAINS = 4


def depth_of(num_query, touches, devices):
    return min(num_query, max(3, 3 * num_query * touches // (2 * devices)))


def prepare_kernel(spectra_ref, out_ref, rows_ref):
    num_query, num_bins = spectra_ref.shape
    blocks = num_bins // LANES
    values = spectra_ref[...].astype(jnp.float32)
    zeros = jnp.zeros((num_query, LANES), jnp.float32)
    wide = jnp.concatenate([values, zeros], axis=1)
    total, length = wide, 1
    while length < 2 * BG:
        total = total + pltpu.roll(total, length, 1)
        length *= 2
    total = total + pltpu.roll(wide, length, 1)
    total = pltpu.roll(total, total.shape[1] - BG, 1)[:, :num_bins]
    centered = values - total / (2 * BG + 1)
    factor = lax.rsqrt(jnp.mean(centered * centered, axis=1, keepdims=True) + EPSILON)
    prepared = (centered * factor).astype(jnp.bfloat16)
    row = lax.broadcasted_iota(jnp.int32, (LANES, LANES), 0)
    col = lax.broadcasted_iota(jnp.int32, (LANES, LANES), 1)
    flip = jnp.where(row + col == LANES - 1, 1.0, 0.0).astype(jnp.bfloat16)
    for block in range(blocks):
        piece = prepared[:, block * LANES : (block + 1) * LANES]
        turned = jnp.dot(piece, flip, preferred_element_type=jnp.float32)
        rows_ref[pl.ds(blocks - 1 - block, num_query, stride=blocks), :] = turned
    out_ref[...] = rows_ref[...].reshape(out_ref.shape).astype(jnp.bfloat16)


def prepare(spectra):
    num_query, num_bins = spectra.shape
    blocks = num_bins // LANES
    return pl.pallas_call(
        prepare_kernel,
        out_shape=jax.ShapeDtypeStruct((num_query, blocks, LANES), jnp.bfloat16),
        scratch_shapes=[pltpu.VMEM((num_query * blocks, LANES), jnp.float32)],
        compiler_params=pltpu.CompilerParams(vmem_limit_bytes=VMEM_LIMIT),
        name="prepare",
    )(spectra)


def route_kernel(num_query, touches, depth, me_ref, named_ref, own_ref, slots_ref, returns_ref):
    me = me_ref[0]
    slots = slots_ref.shape[0] - 1
    devices = slots // depth

    @pl.loop(0, slots + 1)
    def _(i):
        slots_ref[i] = -1
        returns_ref[i] = -1

    @pl.loop(0, devices)
    def _(device):
        first = device * num_query

        def query(q, place):
            for t in range(touches):
                touch = (first + q) * touches + t
                hit = named_ref[touch] == me
                slots_ref[place] = jnp.where(hit, touch, -1)
                place = place + hit.astype(jnp.int32)
            return place

        lax.fori_loop(0, num_query, query, device * depth)

    @pl.loop(0, num_query)
    def _(q):
        for t in range(touches):
            touch = q * touches + t
            base = own_ref[touch] * depth
            taken = jnp.int32(0)
            for s in range(depth):
                taken = taken + (returns_ref[base + s] >= 0).astype(jnp.int32)
            returns_ref[base + taken] = touch


def route(me, named, own, num_query, touches, depth):
    devices = named.shape[0] // (num_query * touches)
    smem = pl.BlockSpec(memory_space=pltpu.SMEM)
    table = jax.ShapeDtypeStruct((devices * depth + 1,), jnp.int32)
    return pl.pallas_call(
        functools.partial(route_kernel, num_query, touches, depth),
        out_shape=(table, table),
        in_specs=[smem] * 3,
        out_specs=(smem, smem),
        name="route",
    )(me, named, own)


def profile_kernel(
    part, depth, touches, slots_ref, local_ref, query_ref, library_ref, out_ref,
    cand_ref, left_ref, right_ref,
):
    per_touch = 8
    blocks = query_ref.shape[1]
    offsets = SHIFTS // LANES
    edge = offsets // 2
    part_depth = depth // PARTS
    part_slots = out_ref.shape[0] // per_touch
    tiles = (blocks + 2) // 2
    row = lax.broadcasted_iota(jnp.int32, (8, LANES), 0)
    lane = lax.broadcasted_iota(jnp.int32, (8, LANES), 1)

    cand_ref[...] = jnp.zeros(cand_ref.shape, cand_ref.dtype)
    right_ref[...] = jnp.zeros(right_ref.shape, right_ref.dtype)

    def one(slot, half):
        place = slot // part_depth * depth + part * part_depth + slot % part_depth
        touch = jnp.maximum(slots_ref[place], 0)
        square = jnp.zeros((per_touch, LANES), jnp.float32)
        for k in range(per_touch):
            wanted = local_ref[touch * per_touch + k]
            cand_ref[half, pl.ds(edge * per_touch + k, blocks, stride=per_touch), :] = (
                library_ref[wanted].astype(jnp.float32)
            )
        for b in range(blocks):
            piece = cand_ref[half, pl.ds((edge + b) * per_touch, per_touch), :]
            square = square + piece * piece
        mean = jnp.sum(square, axis=1, keepdims=True) / (blocks * LANES)
        scale = lax.rsqrt(mean + EPSILON)
        for g in range((blocks + offsets) // 2):
            left_ref[half, pl.ds(16 * g, 16), 0:LANES] = cand_ref[
                half, pl.ds(16 * g, 16), :
            ].astype(jnp.bfloat16)
            left_ref[half, pl.ds(16 * g, 16), LANES : 2 * LANES] = cand_ref[
                half, pl.ds(16 * g + 8, 16), :
            ].astype(jnp.bfloat16)

        spectrum = query_ref[touch // touches].astype(jnp.float32)
        before = before_shifted = jnp.zeros((8, LANES), jnp.float32)
        for b in range(blocks + 1):
            if b < blocks:
                wide = jnp.broadcast_to(spectrum[b : b + 1, :], (8, LANES))
                now = pltpu.roll(wide, 1, 1, stride=1, stride_axis=0)
            else:
                now = jnp.zeros((8, LANES), jnp.float32)
            shifted = jnp.where(lane > row, now, before)
            for a in range(0, LANES, 16):
                tile = jnp.concatenate(
                    [
                        pltpu.roll(
                            jnp.where(lane < LANES - c, shifted, before_shifted), c, 1
                        )
                        if c
                        else shifted
                        for c in (a, a + 8)
                    ],
                    axis=0,
                )
                right_ref[
                    pl.ds((blocks - b) * LANES + a, 16), half * LANES : (half + 1) * LANES
                ] = tile.astype(jnp.bfloat16)
            before, before_shifted = now, shifted
        return scale

    def part_of_sum(low, high):
        left = jnp.concatenate(
            [
                jnp.concatenate(
                    [left_ref[half, pl.ds(16 * u, 8 * offsets), :] for u in range(low, high)],
                    axis=1,
                )
                for half in range(2)
            ],
            axis=0,
        )
        right = right_ref[pl.ds(2 * LANES * low, 2 * LANES * (high - low)), :]
        return jnp.dot(left, right, preferred_element_type=jnp.float32)

    cuts = [tiles * c // CHAINS for c in range(CHAINS + 1)]

    @pl.loop(0, part_slots // 2)
    def _(pair):
        scales = [one(2 * pair, 0), one(2 * pair + 1, 1)]
        product = part_of_sum(cuts[0], cuts[1])
        for c in range(1, CHAINS):
            product = product + part_of_sum(cuts[c], cuts[c + 1])
        for o in range(offsets):
            both = [
                product[
                    (half * offsets + o) * 8 : (half * offsets + o + 1) * 8,
                    half * LANES : (half + 1) * LANES,
                ]
                * scales[half]
                for half in range(2)
            ]
            out_ref[pl.ds(pl.multiple_of(16 * pair, 16), 16), o * LANES : (o + 1) * LANES] = (
                jnp.concatenate(both, axis=0).astype(jnp.bfloat16)
            )


def profile(part, depth, touches, devices, slots, local, queries, library):
    blocks = queries.shape[1]
    offsets = SHIFTS // LANES
    part_slots = devices * depth // PARTS
    rows = (blocks + offsets + 2) * 8
    smem = pl.BlockSpec(memory_space=pltpu.SMEM)
    vmem = pl.BlockSpec(memory_space=pltpu.VMEM)
    flops = part_slots * 2 * 8 * offsets * (blocks + 2) * LANES * LANES
    return pl.pallas_call(
        functools.partial(profile_kernel, part, depth, touches),
        out_shape=jax.ShapeDtypeStruct((part_slots * 8, SHIFTS), jnp.bfloat16),
        in_specs=[smem, smem, vmem, vmem],
        out_specs=vmem,
        scratch_shapes=[
            pltpu.VMEM((2, rows, LANES), jnp.float32),
            pltpu.VMEM((2, (blocks + offsets) * 8, 2 * LANES), jnp.bfloat16),
            pltpu.VMEM(((blocks + 2) * LANES, 2 * LANES), jnp.bfloat16),
        ],
        compiler_params=pltpu.CompilerParams(vmem_limit_bytes=VMEM_LIMIT),
        cost_estimate=pl.CostEstimate(
            flops=8 * flops, bytes_accessed=8 * 1024 * 1024, transcendentals=0
        ),
        name=f"profile_{part}",
    )(slots, local, queries, library)


def unpack_kernel(part, depth, returns_ref, got_ref, *rest):
    out_ref, stage_ref, sem_ref = rest[-3:]
    part_depth = depth // PARTS
    slots = got_ref.shape[0]

    def copy(slot, touch):
        return pltpu.make_async_copy(stage_ref.at[slot], out_ref.at[touch], sem_ref.at[slot])

    def touch_of(slot):
        return returns_ref[slot // part_depth * depth + part * part_depth + slot % part_depth]

    @pl.loop(0, slots)
    def _(slot):
        touch = touch_of(slot)

        @pl.when(touch >= 0)
        def _():
            stage_ref[slot] = got_ref[slot].astype(jnp.float32)
            copy(slot, touch).start()

    @pl.loop(0, slots)
    def _(slot):
        touch = touch_of(slot)

        @pl.when(touch >= 0)
        def _():
            copy(slot, touch).wait()


def unpack(part, depth, touched, returns, got, out):
    slots, per_touch, shifts = got.shape
    smem = pl.BlockSpec(memory_space=pltpu.SMEM)
    vmem = pl.BlockSpec(memory_space=pltpu.VMEM)
    hbm = pl.BlockSpec(memory_space=pl.ANY)
    more = () if out is None else (out,)
    return pl.pallas_call(
        functools.partial(unpack_kernel, part, depth),
        out_shape=jax.ShapeDtypeStruct((touched, per_touch, shifts), jnp.float32),
        in_specs=[smem, vmem] + [hbm] * len(more),
        out_specs=hbm,
        scratch_shapes=[
            pltpu.VMEM((slots, per_touch, shifts), jnp.float32),
            pltpu.SemaphoreType.DMA((slots,)),
        ],
        input_output_aliases={2: 0} if more else {},
        compiler_params=pltpu.CompilerParams(vmem_limit_bytes=VMEM_LIMIT),
        cost_estimate=pl.CostEstimate(
            flops=0, bytes_accessed=got.size * 6, transcendentals=0
        ),
        name=f"unpack_{part}",
    )(returns, got, *more)


def local(spectra, library, cand_block, cand_local):
    devices = lax.axis_size("lib")
    num_query, num_bins = spectra.shape
    touches, per_touch = cand_local.shape[1], cand_local.shape[2]
    depth = depth_of(num_query, touches, devices)
    blocks = num_bins // LANES
    me = lax.axis_index("lib").astype(jnp.int32).reshape(1)

    own = cand_block.reshape(-1)
    named = lax.all_gather(
        jnp.concatenate([own, cand_local.reshape(-1)]), "lib", axis=0, tiled=False
    )
    named, wanted = named[:, : own.shape[0]], named[:, own.shape[0] :]
    queries = lax.all_gather(prepare(spectra), "lib", axis=0, tiled=True)
    rows = library.reshape(-1, blocks, LANES)
    slots, returns = route(me, named.reshape(-1), own, num_query, touches, depth)

    out = None
    for part in range(PARTS):
        answer = profile(
            part, depth, touches, devices, slots, wanted.reshape(-1), queries, rows
        )
        answer = answer.reshape(devices, depth // PARTS * per_touch, SHIFTS)
        got = lax.all_to_all(answer, "lib", split_axis=0, concat_axis=0, tiled=True)
        got = got.reshape(-1, per_touch, SHIFTS)
        out = unpack(part, depth, num_query * touches, returns, got, out)
    return out.reshape(num_query, touches * per_touch, SHIFTS)


def solution(mesh):
    placed = (
        P(("groups", "lib"), None),
        P("lib", None),
        P(("groups", "lib"), None),
        P(("groups", "lib"), None, None),
    )
    return jax.shard_map(
        local,
        mesh=mesh,
        in_specs=placed,
        out_specs=P(("groups", "lib"), None, None),
        check_vma=False,
    )
```

```python
import functools

import jax
import jax.numpy as jnp
from jax import lax
from jax.experimental import pallas as pl
from jax.experimental.pallas import tpu as pltpu
from jax.sharding import PartitionSpec as P

SHIFTS = 1024
BG = 32
EPSILON = 1e-06
LANES = 128
VMEM_LIMIT = 48 * 1024 * 1024
PARTS = 3
CHAINS = 2
GROUPS = 4
WIDTH = LANES // GROUPS


def depth_of(num_query, touches, devices):
    return min(num_query, max(3, 3 * num_query * touches // (2 * devices)))


def prepare_kernel(spectra_ref, out_ref, rows_ref):
    num_query, num_bins = spectra_ref.shape
    blocks = num_bins // LANES
    values = spectra_ref[...].astype(jnp.float32)
    zeros = jnp.zeros((num_query, LANES), jnp.float32)
    wide = jnp.concatenate([values, zeros], axis=1)
    total, length = wide, 1
    while length < 2 * BG:
        total = total + pltpu.roll(total, length, 1)
        length *= 2
    total = total + pltpu.roll(wide, length, 1)
    total = pltpu.roll(total, total.shape[1] - BG, 1)[:, :num_bins]
    centered = values - total / (2 * BG + 1)
    factor = lax.rsqrt(jnp.mean(centered * centered, axis=1, keepdims=True) + EPSILON)
    prepared = (centered * factor).astype(jnp.bfloat16)
    row = lax.broadcasted_iota(jnp.int32, (LANES, LANES), 0)
    col = lax.broadcasted_iota(jnp.int32, (LANES, LANES), 1)
    flip = jnp.where(row + col == LANES - 1, 1.0, 0.0).astype(jnp.bfloat16)
    for block in range(blocks):
        piece = prepared[:, block * LANES : (block + 1) * LANES]
        turned = jnp.dot(piece, flip, preferred_element_type=jnp.float32)
        rows_ref[pl.ds(blocks - 1 - block, num_query, stride=blocks), :] = turned
    out_ref[...] = rows_ref[...].reshape(out_ref.shape).astype(jnp.bfloat16)


def prepare(spectra):
    num_query, num_bins = spectra.shape
    blocks = num_bins // LANES
    return pl.pallas_call(
        prepare_kernel,
        out_shape=jax.ShapeDtypeStruct((num_query, blocks, LANES), jnp.bfloat16),
        scratch_shapes=[pltpu.VMEM((num_query * blocks, LANES), jnp.float32)],
        compiler_params=pltpu.CompilerParams(vmem_limit_bytes=VMEM_LIMIT),
        name="prepare",
    )(spectra)


def route_kernel(num_query, touches, depth, me_ref, named_ref, own_ref, slots_ref, returns_ref):
    me = me_ref[0]
    slots = slots_ref.shape[0] - 1
    devices = slots // depth

    @pl.loop(0, slots + 1)
    def _(i):
        slots_ref[i] = -1
        returns_ref[i] = -1

    @pl.loop(0, devices)
    def _(device):
        first = device * num_query

        def query(q, place):
            for t in range(touches):
                touch = (first + q) * touches + t
                hit = named_ref[touch] == me
                slots_ref[place] = jnp.where(hit, touch, -1)
                place = place + hit.astype(jnp.int32)
            return place

        lax.fori_loop(0, num_query, query, device * depth)

    @pl.loop(0, num_query)
    def _(q):
        for t in range(touches):
            touch = q * touches + t
            base = own_ref[touch] * depth
            taken = jnp.int32(0)
            for s in range(depth):
                taken = taken + (returns_ref[base + s] >= 0).astype(jnp.int32)
            returns_ref[base + taken] = touch


def route(me, named, own, num_query, touches, depth):
    devices = named.shape[0] // (num_query * touches)
    smem = pl.BlockSpec(memory_space=pltpu.SMEM)
    table = jax.ShapeDtypeStruct((devices * depth + 1,), jnp.int32)
    return pl.pallas_call(
        functools.partial(route_kernel, num_query, touches, depth),
        out_shape=(table, table),
        in_specs=[smem] * 3,
        out_specs=(smem, smem),
        name="route",
    )(me, named, own)


def profile_kernel(
    part, depth, touches, slots_ref, local_ref, query_ref, library_ref, out_ref,
    cand_ref, spectrum_ref, left_ref, right_ref,
):
    per_touch = 8
    rows = 2 * per_touch
    blocks = query_ref.shape[1]
    offsets = SHIFTS // LANES
    first = offsets // 2 + 1
    part_depth = depth // PARTS
    part_slots = out_ref.shape[0] // per_touch
    tiles = blocks // GROUPS
    row = lax.broadcasted_iota(jnp.int32, (8, LANES), 0)
    lane = lax.broadcasted_iota(jnp.int32, (8, LANES), 1)
    lane16 = lax.broadcasted_iota(jnp.int32, (rows, LANES), 1)

    cand_ref[...] = jnp.zeros(cand_ref.shape, cand_ref.dtype)
    right_ref[...] = jnp.zeros(right_ref.shape, right_ref.dtype)

    def choose(pieces):
        value = pieces[0]
        for group in range(1, GROUPS):
            value = jnp.where(lane16 < group * WIDTH, value, pieces[group])
        return value

    def gather(slot, half):
        place = slot // part_depth * depth + part * part_depth + slot % part_depth
        touch = jnp.maximum(slots_ref[place], 0)
        for k in range(per_touch):
            wanted = local_ref[touch * per_touch + k]
            cand_ref[pl.ds(first * rows + half * per_touch + k, blocks, stride=rows), :] = (
                library_ref[wanted].astype(jnp.float32)
            )
        square = jnp.zeros((per_touch, LANES), jnp.float32)
        for b in range(blocks):
            piece = cand_ref[pl.ds((first + b) * rows + half * per_touch, per_touch), :]
            square = square + piece * piece
        mean = jnp.sum(square, axis=1, keepdims=True) / (blocks * LANES)
        return touch // touches, lax.rsqrt(mean + EPSILON)

    def make_left():
        pieces = [
            cand_ref[pl.ds(rows * b, rows), :].astype(jnp.bfloat16)
            for b in range(blocks + offsets + 1)
        ]
        for t in range(tiles + offsets + 1):
            given = [pieces[t + tiles * g] for g in range(GROUPS)]
            turned = []
            for c in range(GROUPS):
                mixed = choose([given[(a + c) % GROUPS] for a in range(GROUPS)])
                turned.append(pltpu.roll(mixed, WIDTH * c, 1) if c else mixed)
            for a in range(GROUPS):
                left_ref[a, pl.ds(rows * t, rows), :] = choose(
                    [turned[(g - a) % GROUPS] for g in range(GROUPS)]
                )

    def make_right(query, half):
        spectrum_ref[half] = query_ref[query].astype(jnp.float32)
        zero = jnp.zeros((8, LANES), jnp.float32)
        before = (zero, zero)
        before_shifted = jnp.zeros((16, LANES), jnp.bfloat16)
        columns = slice(half * LANES, (half + 1) * LANES)
        for b in range(blocks + 1):
            if b < blocks:
                wide = jnp.broadcast_to(spectrum_ref[half, pl.ds(b, 1), :], (8, LANES))
                now = tuple(
                    pltpu.roll(wide, 1 + 8 * h, 1, stride=1, stride_axis=0) for h in range(2)
                )
            else:
                now = (zero, zero)
            shifted = jnp.concatenate(
                [jnp.where(lane > row + 8 * h, now[h], before[h]) for h in range(2)], axis=0
            ).astype(jnp.bfloat16)
            j = blocks - 1 - b
            place = 0 if j < 0 else (j % tiles + 1) * LANES + j // tiles * WIDTH
            right_ref[pl.ds(place, 16), columns] = shifted
            for c in range(16, WIDTH, 16):
                right_ref[pl.ds(place + c, 16), columns] = pltpu.roll(
                    jnp.where(lane16 < LANES - c, shifted, before_shifted), c, 1
                )
            before, before_shifted = now, shifted

    def sums(low, high):
        left = jnp.concatenate(
            [
                jnp.concatenate(
                    [
                        left_ref[a, pl.ds(rows * t, rows * (offsets + 1)), :]
                        for t in range(tiles + 1)
                    ],
                    axis=1,
                )
                for a in range(low, high)
            ],
            axis=0,
        )
        return jnp.dot(left, right_ref[...], preferred_element_type=jnp.float32)

    @pl.loop(0, part_slots // 2)
    def _(pair):
        queries, scales = zip(*[gather(2 * pair + half, half) for half in range(2)])
        make_left()
        for half in range(2):
            make_right(queries[half], half)
        step = GROUPS // CHAINS
        products = [sums(step * c, step * (c + 1)) for c in range(CHAINS)]

        def found(a, o, half):
            at = ((a % step) * (offsets + 1) + o) * rows + half * per_touch
            return products[a // step][at : at + per_touch, half * LANES : (half + 1) * LANES]

        for o in range(offsets):
            both = []
            for half in range(2):
                total = found(0, o + 1, half)
                for a in range(1, GROUPS):
                    shift = WIDTH * a
                    total = total + pltpu.roll(
                        jnp.where(
                            lane < LANES - shift, found(a, o + 1, half), found(a, o, half)
                        ),
                        shift,
                        1,
                    )
                both.append(total * scales[half])
            out_ref[pl.ds(pl.multiple_of(16 * pair, 16), 16), o * LANES : (o + 1) * LANES] = (
                jnp.concatenate(both, axis=0).astype(jnp.bfloat16)
            )


def profile(part, depth, touches, devices, slots, local, queries, library):
    blocks = queries.shape[1]
    offsets = SHIFTS // LANES
    part_slots = devices * depth // PARTS
    tiles = blocks // GROUPS
    smem = pl.BlockSpec(memory_space=pltpu.SMEM)
    vmem = pl.BlockSpec(memory_space=pltpu.VMEM)
    flops = part_slots * 2 * 8 * (offsets + 1) * (blocks + 4) * LANES * LANES
    return pl.pallas_call(
        functools.partial(profile_kernel, part, depth, touches),
        out_shape=jax.ShapeDtypeStruct((part_slots * 8, SHIFTS), jnp.bfloat16),
        in_specs=[smem, smem, vmem, vmem],
        out_specs=vmem,
        scratch_shapes=[
            pltpu.VMEM(((blocks + offsets + 1) * 16, LANES), jnp.float32),
            pltpu.VMEM((2, blocks, LANES), jnp.float32),
            pltpu.VMEM((GROUPS, (tiles + offsets + 1) * 16, LANES), jnp.bfloat16),
            pltpu.VMEM(((tiles + 1) * LANES, 2 * LANES), jnp.bfloat16),
        ],
        compiler_params=pltpu.CompilerParams(vmem_limit_bytes=VMEM_LIMIT),
        cost_estimate=pl.CostEstimate(
            flops=8 * flops, bytes_accessed=8 * 1024 * 1024, transcendentals=0
        ),
        name=f"profile_{part}",
    )(slots, local, queries, library)


def unpack_kernel(part, depth, returns_ref, got_ref, *rest):
    out_ref, stage_ref, sem_ref = rest[-3:]
    part_depth = depth // PARTS
    slots = got_ref.shape[0]

    def copy(slot, touch):
        return pltpu.make_async_copy(stage_ref.at[slot], out_ref.at[touch], sem_ref.at[slot])

    def touch_of(slot):
        return returns_ref[slot // part_depth * depth + part * part_depth + slot % part_depth]

    @pl.loop(0, slots)
    def _(slot):
        touch = touch_of(slot)

        @pl.when(touch >= 0)
        def _():
            stage_ref[slot] = got_ref[slot].astype(jnp.float32)
            copy(slot, touch).start()

    @pl.loop(0, slots)
    def _(slot):
        touch = touch_of(slot)

        @pl.when(touch >= 0)
        def _():
            copy(slot, touch).wait()


def unpack(part, depth, touched, returns, got, out):
    slots, per_touch, shifts = got.shape
    smem = pl.BlockSpec(memory_space=pltpu.SMEM)
    vmem = pl.BlockSpec(memory_space=pltpu.VMEM)
    hbm = pl.BlockSpec(memory_space=pl.ANY)
    more = () if out is None else (out,)
    return pl.pallas_call(
        functools.partial(unpack_kernel, part, depth),
        out_shape=jax.ShapeDtypeStruct((touched, per_touch, shifts), jnp.float32),
        in_specs=[smem, vmem] + [hbm] * len(more),
        out_specs=hbm,
        scratch_shapes=[
            pltpu.VMEM((slots, per_touch, shifts), jnp.float32),
            pltpu.SemaphoreType.DMA((slots,)),
        ],
        input_output_aliases={2: 0} if more else {},
        compiler_params=pltpu.CompilerParams(vmem_limit_bytes=VMEM_LIMIT),
        cost_estimate=pl.CostEstimate(
            flops=0, bytes_accessed=got.size * 6, transcendentals=0
        ),
        name=f"unpack_{part}",
    )(returns, got, *more)


def local(spectra, library, cand_block, cand_local):
    devices = lax.axis_size("lib")
    num_query, num_bins = spectra.shape
    touches, per_touch = cand_local.shape[1], cand_local.shape[2]
    depth = depth_of(num_query, touches, devices)
    blocks = num_bins // LANES
    me = lax.axis_index("lib").astype(jnp.int32).reshape(1)

    own = cand_block.reshape(-1)
    named = lax.all_gather(
        jnp.concatenate([own, cand_local.reshape(-1)]), "lib", axis=0, tiled=False
    )
    named, wanted = named[:, : own.shape[0]], named[:, own.shape[0] :]
    queries = lax.all_gather(prepare(spectra), "lib", axis=0, tiled=True)
    rows = library.reshape(-1, blocks, LANES)
    slots, returns = route(me, named.reshape(-1), own, num_query, touches, depth)

    out = None
    for part in range(PARTS):
        answer = profile(
            part, depth, touches, devices, slots, wanted.reshape(-1), queries, rows
        )
        answer = answer.reshape(devices, depth // PARTS * per_touch, SHIFTS)
        got = lax.all_to_all(answer, "lib", split_axis=0, concat_axis=0, tiled=True)
        got = got.reshape(-1, per_touch, SHIFTS)
        out = unpack(part, depth, num_query * touches, returns, got, out)
    return out.reshape(num_query, touches * per_touch, SHIFTS)


def solution(mesh):
    placed = (
        P(("groups", "lib"), None),
        P("lib", None),
        P(("groups", "lib"), None),
        P(("groups", "lib"), None, None),
    )
    return jax.shard_map(
        local,
        mesh=mesh,
        in_specs=placed,
        out_specs=P(("groups", "lib"), None, None),
        check_vma=False,
    )
```

```python
import functools

import jax
import jax.numpy as jnp
from jax import lax
from jax.experimental import pallas as pl
from jax.experimental.pallas import tpu as pltpu
from jax.sharding import PartitionSpec as P

SHIFTS = 1024
BG = 32
EPSILON = 1e-06
LANES = 128
VMEM_LIMIT = 48 * 1024 * 1024
PARTS = 3
CHAINS = 2
GROUPS = 4
WIDTH = LANES // GROUPS


def depth_of(num_query, touches, devices):
    return min(num_query, max(3, 3 * num_query * touches // (2 * devices)))


def prepare_kernel(spectra_ref, out_ref, rows_ref):
    num_query, num_bins = spectra_ref.shape
    blocks = num_bins // LANES
    values = spectra_ref[...].astype(jnp.float32)
    zeros = jnp.zeros((num_query, LANES), jnp.float32)
    wide = jnp.concatenate([values, zeros], axis=1)
    total, length = wide, 1
    while length < 2 * BG:
        total = total + pltpu.roll(total, length, 1)
        length *= 2
    total = total + pltpu.roll(wide, length, 1)
    total = pltpu.roll(total, total.shape[1] - BG, 1)[:, :num_bins]
    centered = values - total / (2 * BG + 1)
    factor = lax.rsqrt(jnp.mean(centered * centered, axis=1, keepdims=True) + EPSILON)
    prepared = (centered * factor).astype(jnp.bfloat16)
    row = lax.broadcasted_iota(jnp.int32, (LANES, LANES), 0)
    col = lax.broadcasted_iota(jnp.int32, (LANES, LANES), 1)
    flip = jnp.where(row + col == LANES - 1, 1.0, 0.0).astype(jnp.bfloat16)
    for block in range(blocks):
        piece = prepared[:, block * LANES : (block + 1) * LANES]
        turned = jnp.dot(piece, flip, preferred_element_type=jnp.float32)
        rows_ref[pl.ds(blocks - 1 - block, num_query, stride=blocks), :] = turned
    out_ref[...] = rows_ref[...].reshape(out_ref.shape).astype(jnp.bfloat16)


def prepare(spectra):
    num_query, num_bins = spectra.shape
    blocks = num_bins // LANES
    return pl.pallas_call(
        prepare_kernel,
        out_shape=jax.ShapeDtypeStruct((num_query, blocks, LANES), jnp.bfloat16),
        scratch_shapes=[pltpu.VMEM((num_query * blocks, LANES), jnp.float32)],
        compiler_params=pltpu.CompilerParams(vmem_limit_bytes=VMEM_LIMIT),
        name="prepare",
    )(spectra)


def route_kernel(num_query, touches, depth, me_ref, named_ref, own_ref, slots_ref, returns_ref):
    me = me_ref[0]
    slots = slots_ref.shape[0] - 1
    devices = slots // depth

    @pl.loop(0, slots + 1)
    def _(i):
        slots_ref[i] = -1
        returns_ref[i] = -1

    @pl.loop(0, devices)
    def _(device):
        first = device * num_query

        def query(q, place):
            for t in range(touches):
                touch = (first + q) * touches + t
                hit = named_ref[touch] == me
                slots_ref[place] = jnp.where(hit, touch, -1)
                place = place + hit.astype(jnp.int32)
            return place

        lax.fori_loop(0, num_query, query, device * depth)

    @pl.loop(0, num_query)
    def _(q):
        for t in range(touches):
            touch = q * touches + t
            base = own_ref[touch] * depth
            taken = jnp.int32(0)
            for s in range(depth):
                taken = taken + (returns_ref[base + s] >= 0).astype(jnp.int32)
            returns_ref[base + taken] = touch


def route(me, named, own, num_query, touches, depth):
    devices = named.shape[0] // (num_query * touches)
    smem = pl.BlockSpec(memory_space=pltpu.SMEM)
    table = jax.ShapeDtypeStruct((devices * depth + 1,), jnp.int32)
    return pl.pallas_call(
        functools.partial(route_kernel, num_query, touches, depth),
        out_shape=(table, table),
        in_specs=[smem] * 3,
        out_specs=(smem, smem),
        name="route",
    )(me, named, own)


def profile_kernel(
    part, depth, touches, slots_ref, local_ref, query_ref, library_ref, out_ref, *scratch
):
    per_touch = 8
    sets = [scratch[i::2] for i in range(2)]
    rows = 2 * per_touch
    blocks = query_ref.shape[1]
    offsets = SHIFTS // LANES
    first = offsets // 2 + 1
    part_depth = depth // PARTS
    part_slots = out_ref.shape[0] // per_touch
    tiles = blocks // GROUPS
    row = lax.broadcasted_iota(jnp.int32, (8, LANES), 0)
    lane = lax.broadcasted_iota(jnp.int32, (8, LANES), 1)
    lane16 = lax.broadcasted_iota(jnp.int32, (rows, LANES), 1)

    for cand_ref, _, _, right_ref in sets:
        cand_ref[...] = jnp.zeros(cand_ref.shape, cand_ref.dtype)
        right_ref[...] = jnp.zeros(right_ref.shape, right_ref.dtype)

    def choose(pieces):
        value = pieces[0]
        for group in range(1, GROUPS):
            value = jnp.where(lane16 < group * WIDTH, value, pieces[group])
        return value

    def gather(cand_ref, slot, half):
        place = slot // part_depth * depth + part * part_depth + slot % part_depth
        touch = jnp.maximum(slots_ref[place], 0)
        for k in range(per_touch):
            wanted = local_ref[touch * per_touch + k]
            cand_ref[pl.ds(first * rows + half * per_touch + k, blocks, stride=rows), :] = (
                library_ref[wanted].astype(jnp.float32)
            )
        square = jnp.zeros((per_touch, LANES), jnp.float32)
        for b in range(blocks):
            piece = cand_ref[pl.ds((first + b) * rows + half * per_touch, per_touch), :]
            square = square + piece * piece
        mean = jnp.sum(square, axis=1, keepdims=True) / (blocks * LANES)
        return touch // touches, lax.rsqrt(mean + EPSILON)

    def make_left(cand_ref, left_ref):
        pieces = [
            cand_ref[pl.ds(rows * b, rows), :].astype(jnp.bfloat16)
            for b in range(blocks + offsets + 1)
        ]
        for t in range(tiles + offsets + 1):
            given = [pieces[t + tiles * g] for g in range(GROUPS)]
            turned = []
            for c in range(GROUPS):
                mixed = choose([given[(a + c) % GROUPS] for a in range(GROUPS)])
                turned.append(pltpu.roll(mixed, WIDTH * c, 1) if c else mixed)
            for a in range(GROUPS):
                left_ref[a, pl.ds(rows * t, rows), :] = choose(
                    [turned[(g - a) % GROUPS] for g in range(GROUPS)]
                )

    def make_right(spectrum_ref, right_ref, query, half):
        spectrum_ref[half] = query_ref[query].astype(jnp.float32)
        zero = jnp.zeros((8, LANES), jnp.float32)
        before = (zero, zero)
        before_shifted = jnp.zeros((16, LANES), jnp.bfloat16)
        columns = slice(half * LANES, (half + 1) * LANES)
        for b in range(blocks + 1):
            if b < blocks:
                wide = jnp.broadcast_to(spectrum_ref[half, pl.ds(b, 1), :], (8, LANES))
                now = tuple(
                    pltpu.roll(wide, 1 + 8 * h, 1, stride=1, stride_axis=0) for h in range(2)
                )
            else:
                now = (zero, zero)
            shifted = jnp.concatenate(
                [jnp.where(lane > row + 8 * h, now[h], before[h]) for h in range(2)], axis=0
            ).astype(jnp.bfloat16)
            j = blocks - 1 - b
            place = 0 if j < 0 else (j % tiles + 1) * LANES + j // tiles * WIDTH
            right_ref[pl.ds(place, 16), columns] = shifted
            for c in range(16, WIDTH, 16):
                right_ref[pl.ds(place + c, 16), columns] = pltpu.roll(
                    jnp.where(lane16 < LANES - c, shifted, before_shifted), c, 1
                )
            before, before_shifted = now, shifted

    def sums(left_ref, right_ref, low, high):
        left = jnp.concatenate(
            [
                jnp.concatenate(
                    [
                        left_ref[a, pl.ds(rows * t, rows * (offsets + 1)), :]
                        for t in range(tiles + 1)
                    ],
                    axis=1,
                )
                for a in range(low, high)
            ],
            axis=0,
        )
        return jnp.dot(left, right_ref[...], preferred_element_type=jnp.float32)

    def make(pair, refs):
        cand_ref, spectrum_ref, left_ref, right_ref = refs
        found = [gather(cand_ref, 2 * pair + half, half) for half in range(2)]
        make_left(cand_ref, left_ref)
        for half in range(2):
            make_right(spectrum_ref, right_ref, found[half][0], half)
        return tuple(scale for _, scale in found)

    def finish(pair, scales, refs):
        left_ref, right_ref = refs[2:]
        step = GROUPS // CHAINS
        products = [
            sums(left_ref, right_ref, step * c, step * (c + 1)) for c in range(CHAINS)
        ]

        def found(a, o, half):
            at = ((a % step) * (offsets + 1) + o) * rows + half * per_touch
            return products[a // step][at : at + per_touch, half * LANES : (half + 1) * LANES]

        for o in range(offsets):
            both = []
            for half in range(2):
                total = found(0, o + 1, half)
                for a in range(1, GROUPS):
                    shift = WIDTH * a
                    total = total + pltpu.roll(
                        jnp.where(
                            lane < LANES - shift, found(a, o + 1, half), found(a, o, half)
                        ),
                        shift,
                        1,
                    )
                both.append(total * scales[half])
            out_ref[pl.ds(pl.multiple_of(16 * pair, 16), 16), o * LANES : (o + 1) * LANES] = (
                jnp.concatenate(both, axis=0).astype(jnp.bfloat16)
            )

    pairs = part_slots // 2

    def two(i, scales):
        following = make(2 * i + 1, sets[1])
        finish(2 * i, scales, sets[0])
        scales = make(jnp.minimum(2 * i + 2, pairs - 1), sets[0])
        finish(2 * i + 1, following, sets[1])
        return scales

    lax.fori_loop(0, pairs // 2, two, make(0, sets[0]))


def profile(part, depth, touches, devices, slots, local, queries, library):
    blocks = queries.shape[1]
    offsets = SHIFTS // LANES
    part_slots = devices * depth // PARTS
    tiles = blocks // GROUPS
    smem = pl.BlockSpec(memory_space=pltpu.SMEM)
    vmem = pl.BlockSpec(memory_space=pltpu.VMEM)
    flops = part_slots * 2 * 8 * (offsets + 1) * (blocks + 4) * LANES * LANES
    return pl.pallas_call(
        functools.partial(profile_kernel, part, depth, touches),
        out_shape=jax.ShapeDtypeStruct((part_slots * 8, SHIFTS), jnp.bfloat16),
        in_specs=[smem, smem, vmem, vmem],
        out_specs=vmem,
        scratch_shapes=[
            buffer
            for buffer in (
                pltpu.VMEM(((blocks + offsets + 1) * 16, LANES), jnp.float32),
                pltpu.VMEM((2, blocks, LANES), jnp.float32),
                pltpu.VMEM((GROUPS, (tiles + offsets + 1) * 16, LANES), jnp.bfloat16),
                pltpu.VMEM(((tiles + 1) * LANES, 2 * LANES), jnp.bfloat16),
            )
            for _ in range(2)
        ],
        compiler_params=pltpu.CompilerParams(vmem_limit_bytes=VMEM_LIMIT),
        cost_estimate=pl.CostEstimate(
            flops=8 * flops, bytes_accessed=8 * 1024 * 1024, transcendentals=0
        ),
        name=f"profile_{part}",
    )(slots, local, queries, library)


def unpack_kernel(part, depth, returns_ref, got_ref, *rest):
    out_ref, stage_ref, sem_ref = rest[-3:]
    part_depth = depth // PARTS
    slots = got_ref.shape[0]

    def copy(slot, touch):
        return pltpu.make_async_copy(stage_ref.at[slot], out_ref.at[touch], sem_ref.at[slot])

    def touch_of(slot):
        return returns_ref[slot // part_depth * depth + part * part_depth + slot % part_depth]

    @pl.loop(0, slots)
    def _(slot):
        touch = touch_of(slot)

        @pl.when(touch >= 0)
        def _():
            stage_ref[slot] = got_ref[slot].astype(jnp.float32)
            copy(slot, touch).start()

    @pl.loop(0, slots)
    def _(slot):
        touch = touch_of(slot)

        @pl.when(touch >= 0)
        def _():
            copy(slot, touch).wait()


def unpack(part, depth, touched, returns, got, out):
    slots, per_touch, shifts = got.shape
    smem = pl.BlockSpec(memory_space=pltpu.SMEM)
    vmem = pl.BlockSpec(memory_space=pltpu.VMEM)
    hbm = pl.BlockSpec(memory_space=pl.ANY)
    more = () if out is None else (out,)
    return pl.pallas_call(
        functools.partial(unpack_kernel, part, depth),
        out_shape=jax.ShapeDtypeStruct((touched, per_touch, shifts), jnp.float32),
        in_specs=[smem, vmem] + [hbm] * len(more),
        out_specs=hbm,
        scratch_shapes=[
            pltpu.VMEM((slots, per_touch, shifts), jnp.float32),
            pltpu.SemaphoreType.DMA((slots,)),
        ],
        input_output_aliases={2: 0} if more else {},
        compiler_params=pltpu.CompilerParams(vmem_limit_bytes=VMEM_LIMIT),
        cost_estimate=pl.CostEstimate(
            flops=0, bytes_accessed=got.size * 6, transcendentals=0
        ),
        name=f"unpack_{part}",
    )(returns, got, *more)


def local(spectra, library, cand_block, cand_local):
    devices = lax.axis_size("lib")
    num_query, num_bins = spectra.shape
    touches, per_touch = cand_local.shape[1], cand_local.shape[2]
    depth = depth_of(num_query, touches, devices)
    blocks = num_bins // LANES
    me = lax.axis_index("lib").astype(jnp.int32).reshape(1)

    own = cand_block.reshape(-1)
    named = lax.all_gather(
        jnp.concatenate([own, cand_local.reshape(-1)]), "lib", axis=0, tiled=False
    )
    named, wanted = named[:, : own.shape[0]], named[:, own.shape[0] :]
    queries = lax.all_gather(prepare(spectra), "lib", axis=0, tiled=True)
    rows = library.reshape(-1, blocks, LANES)
    slots, returns = route(me, named.reshape(-1), own, num_query, touches, depth)

    out = None
    for part in range(PARTS):
        answer = profile(
            part, depth, touches, devices, slots, wanted.reshape(-1), queries, rows
        )
        answer = answer.reshape(devices, depth // PARTS * per_touch, SHIFTS)
        got = lax.all_to_all(answer, "lib", split_axis=0, concat_axis=0, tiled=True)
        got = got.reshape(-1, per_touch, SHIFTS)
        out = unpack(part, depth, num_query * touches, returns, got, out)
    return out.reshape(num_query, touches * per_touch, SHIFTS)


def solution(mesh):
    placed = (
        P(("groups", "lib"), None),
        P("lib", None),
        P(("groups", "lib"), None),
        P(("groups", "lib"), None, None),
    )
    return jax.shard_map(
        local,
        mesh=mesh,
        in_specs=placed,
        out_specs=P(("groups", "lib"), None, None),
        check_vma=False,
    )
```

```python
import functools

import jax
import jax.numpy as jnp
from jax import lax
from jax.experimental import pallas as pl
from jax.experimental.pallas import tpu as pltpu
from jax.sharding import PartitionSpec as P

SHIFTS = 1024
BG = 32
EPSILON = 1e-06
LANES = 128
VMEM_LIMIT = 48 * 1024 * 1024
NEAR = 4
ROW_SLOTS = 4
SLOT_LANES = LANES // ROW_SLOTS
PER_TOUCH = 8
CHAINS = 2
GROUPS = 4
WIDTH = LANES // GROUPS


def rounded(value, unit):
    return -(-value // unit) * unit


def depth_of(num_query, touches, devices):
    return min(num_query, max(3, 3 * num_query * touches // (2 * devices)))


def record_values(found):
    lane = lax.broadcasted_iota(jnp.int32, found.shape, 1) % SLOT_LANES
    low = pltpu.roll(found, LANES - PER_TOUCH, 1)
    return jnp.where(lane < PER_TOUCH, found * 16 + low, found).astype(jnp.int32)


def prepare_kernel(depth, spectra_ref, named_ref, wanted_ref, out_ref, table_ref, rows_ref):
    num_query, num_bins = spectra_ref.shape
    blocks = num_bins // LANES
    values = spectra_ref[...].astype(jnp.float32)
    zeros = jnp.zeros((num_query, LANES), jnp.float32)
    wide = jnp.concatenate([values, zeros], axis=1)
    total, length = wide, 1
    while length < 2 * BG:
        total = total + pltpu.roll(total, length, 1)
        length *= 2
    total = total + pltpu.roll(wide, length, 1)
    total = pltpu.roll(total, total.shape[1] - BG, 1)[:, :num_bins]
    centered = values - total / (2 * BG + 1)
    factor = lax.rsqrt(jnp.mean(centered * centered, axis=1, keepdims=True) + EPSILON)
    prepared = (centered * factor).astype(jnp.bfloat16)
    row = lax.broadcasted_iota(jnp.int32, (LANES, LANES), 0)
    col = lax.broadcasted_iota(jnp.int32, (LANES, LANES), 1)
    flip = jnp.where(row + col == LANES - 1, 1.0, 0.0).astype(jnp.bfloat16)
    for block in range(blocks):
        piece = prepared[:, block * LANES : (block + 1) * LANES]
        turned = jnp.dot(piece, flip, preferred_element_type=jnp.float32)
        rows_ref[pl.ds(blocks - 1 - block, num_query, stride=blocks), :] = turned
    out_ref[0 : num_query * blocks, :] = rows_ref[...].astype(jnp.bfloat16)

    touches = named_ref.shape[1]
    touched = num_query * touches
    records = table_ref.shape[0]
    per_block = rounded(depth, ROW_SLOTS) // ROW_SLOTS
    touch = lax.broadcasted_iota(jnp.int32, (touched, num_query), 0)
    query = lax.broadcasted_iota(jnp.int32, (touched, num_query), 1)
    owner = jnp.where(touch // touches == query, 1.0, 0.0).astype(jnp.bfloat16)
    named = named_ref[...].astype(jnp.float32).astype(jnp.bfloat16)
    spread = jnp.dot(owner, named, preferred_element_type=jnp.float32)
    touch = lax.broadcasted_iota(jnp.int32, (touched, touches), 0)
    which = lax.broadcasted_iota(jnp.int32, (touched, touches), 1)
    block_col = jnp.sum(
        jnp.where(touch % touches == which, spread, 0.0), axis=1, keepdims=True
    )
    row = lax.broadcasted_iota(jnp.int32, (touched, touched), 0)
    col = lax.broadcasted_iota(jnp.int32, (touched, touched), 1)
    block_row = jnp.sum(jnp.where(row == col, block_col, 0.0), axis=0, keepdims=True)
    earlier = (block_col == block_row) & (row < col)
    rank = jnp.sum(jnp.where(earlier, 1.0, 0.0), axis=0, keepdims=True).astype(jnp.int32)
    place = block_row.astype(jnp.int32) * per_block + rank // ROW_SLOTS
    wanted = wanted_ref[...]
    high = (wanted // 16).astype(jnp.float32).astype(jnp.bfloat16)
    low = (wanted % 16).astype(jnp.float32).astype(jnp.bfloat16)
    unit = lax.broadcasted_iota(jnp.int32, (PER_TOUCH, LANES), 0)
    lane = lax.broadcasted_iota(jnp.int32, (PER_TOUCH, LANES), 1)
    row = lax.broadcasted_iota(jnp.int32, (records, touched), 0)
    touch = lax.broadcasted_iota(jnp.int32, (touched, LANES), 0)
    wide_lane = lax.broadcasted_iota(jnp.int32, (touched, LANES), 1)
    found = jnp.zeros((records, LANES), jnp.float32)
    for group in range(ROW_SLOTS):
        start = group * SLOT_LANES
        to_high = jnp.where(lane == start + unit, 1.0, 0.0).astype(jnp.bfloat16)
        to_low = jnp.where(lane == start + PER_TOUCH + unit, 1.0, 0.0).astype(jnp.bfloat16)
        data = jnp.dot(high, to_high, preferred_element_type=jnp.float32)
        data = data + jnp.dot(low, to_low, preferred_element_type=jnp.float32)
        data = jnp.where(
            wide_lane == start + 2 * PER_TOUCH, (touch + 1).astype(jnp.float32), data
        ).astype(jnp.bfloat16)
        pick = jnp.where((row == place) & (rank % ROW_SLOTS == group), 1.0, 0.0)
        found = found + jnp.dot(
            pick.astype(jnp.bfloat16), data, preferred_element_type=jnp.float32
        )
    out_ref[num_query * blocks :, :] = found.astype(jnp.bfloat16)
    table_ref[...] = record_values(found)


def prepare(spectra, named, wanted, depth, records):
    num_query, num_bins = spectra.shape
    rows = num_query * num_bins // LANES
    return pl.pallas_call(
        functools.partial(prepare_kernel, depth),
        out_shape=(
            jax.ShapeDtypeStruct((rows + records, LANES), jnp.bfloat16),
            jax.ShapeDtypeStruct((records, LANES), jnp.int32),
        ),
        scratch_shapes=[pltpu.VMEM((rows, LANES), jnp.float32)],
        compiler_params=pltpu.CompilerParams(vmem_limit_bytes=VMEM_LIMIT),
        name="prepare",
    )(spectra, named, wanted)


def profile_kernel(depth, num_query, touches, me_ref, *refs):
    shards, library_ref, refs = refs[:NEAR], refs[NEAR], refs[NEAR + 1 :]
    outs, refs = refs[:NEAR], refs[NEAR:]
    (
        query_ref, record_ref, found_ref, table_ref, answer_ref,
        cand_ref, packed_ref, spectrum_ref, left_ref, right_ref, product_ref, sem_ref,
    ) = refs
    per_touch = PER_TOUCH
    rows = 2 * per_touch
    blocks = library_ref.shape[1]
    offsets = SHIFTS // LANES
    first = offsets // 2 + 1
    tiles = blocks // GROUPS
    query_rows = num_query * blocks
    per_block = rounded(depth, ROW_SLOTS) // ROW_SLOTS
    row = lax.broadcasted_iota(jnp.int32, (8, LANES), 0)
    lane = lax.broadcasted_iota(jnp.int32, (8, LANES), 1)
    lane16 = lax.broadcasted_iota(jnp.int32, (rows, LANES), 1)

    copies = [
        pltpu.make_async_copy(shards[e], query_ref.at[e], sem_ref.at[e]) for e in range(NEAR)
    ]
    for copy in copies:
        copy.start()
    cand_ref[...] = jnp.zeros(cand_ref.shape, cand_ref.dtype)
    right_ref[...] = jnp.zeros(right_ref.shape, right_ref.dtype)
    found_ref[...] = jnp.zeros(found_ref.shape, found_ref.dtype)
    for e in range(NEAR):
        copies[e].wait()
        record_ref[...] = query_ref[e, query_rows:, :].astype(jnp.float32)
        found_ref[e * per_block : (e + 1) * per_block, :] = record_values(
            record_ref[pl.ds(me_ref[0] * per_block, per_block), :]
        )
    to_scalars = pltpu.make_async_copy(found_ref, table_ref, sem_ref.at[NEAR])
    to_scalars.start()
    to_scalars.wait()

    def entry(slot):
        e = slot // depth
        s = slot % depth
        return e, e * per_block + s // ROW_SLOTS, s % ROW_SLOTS * SLOT_LANES

    def touch_of(slot):
        _, line, start = entry(slot)
        return table_ref[line, start + 2 * per_touch] - 1

    def choose(pieces):
        value = pieces[0]
        for group in range(1, GROUPS):
            value = jnp.where(lane16 < group * WIDTH, value, pieces[group])
        return value

    def gather(slot, half):
        _, line, start = entry(slot)
        for k in range(per_touch):
            wanted = table_ref[line, start + k]
            cand_ref[pl.ds(first * rows + half * per_touch + k, blocks, stride=rows), :] = (
                library_ref[wanted].astype(jnp.float32)
            )
        square = jnp.zeros((per_touch, LANES), jnp.float32)
        for b in range(blocks):
            piece = cand_ref[pl.ds((first + b) * rows + half * per_touch, per_touch), :]
            square = square + piece * piece
        mean = jnp.sum(square, axis=1, keepdims=True) / (blocks * LANES)
        return lax.rsqrt(mean + EPSILON)

    def make_left():
        for b in range(blocks + offsets + 1):
            packed_ref[pl.ds(rows * b, rows), :] = cand_ref[pl.ds(rows * b, rows), :].astype(
                jnp.bfloat16
            )
        for t in range(tiles + offsets + 1):
            given = [packed_ref[pl.ds(rows * (t + tiles * g), rows), :] for g in range(GROUPS)]
            turned = []
            for c in range(GROUPS):
                mixed = choose([given[(a + c) % GROUPS] for a in range(GROUPS)])
                turned.append(pltpu.roll(mixed, WIDTH * c, 1) if c else mixed)
            for a in range(GROUPS):
                left_ref[a, pl.ds(rows * t, rows), :] = choose(
                    [turned[(g - a) % GROUPS] for g in range(GROUPS)]
                )

    def make_right(slot, half):
        query = jnp.maximum(touch_of(slot), 0) // touches
        spectrum_ref[half] = query_ref[
            entry(slot)[0], pl.ds(pl.multiple_of(query * blocks, blocks), blocks), :
        ].astype(jnp.float32)
        zero = jnp.zeros((8, LANES), jnp.float32)
        before = (zero, zero)
        before_shifted = jnp.zeros((16, LANES), jnp.bfloat16)
        columns = slice(half * LANES, (half + 1) * LANES)
        for b in range(blocks + 1):
            if b < blocks:
                wide = jnp.broadcast_to(spectrum_ref[half, pl.ds(b, 1), :], (8, LANES))
                now = tuple(
                    pltpu.roll(wide, 1 + 8 * h, 1, stride=1, stride_axis=0) for h in range(2)
                )
            else:
                now = (zero, zero)
            shifted = jnp.concatenate(
                [jnp.where(lane > row + 8 * h, now[h], before[h]) for h in range(2)], axis=0
            ).astype(jnp.bfloat16)
            j = blocks - 1 - b
            place = 0 if j < 0 else (j % tiles + 1) * LANES + j // tiles * WIDTH
            right_ref[pl.ds(place, 16), columns] = shifted
            for c in range(16, WIDTH, 16):
                right_ref[pl.ds(place + c, 16), columns] = pltpu.roll(
                    jnp.where(lane16 < LANES - c, shifted, before_shifted), c, 1
                )
            before, before_shifted = now, shifted

    def sums(low, high):
        left = jnp.concatenate(
            [
                jnp.concatenate(
                    [
                        left_ref[a, pl.ds(rows * t, rows * (offsets + 1)), :]
                        for t in range(tiles + 1)
                    ],
                    axis=1,
                )
                for a in range(low, high)
            ],
            axis=0,
        )
        return jnp.dot(left, right_ref[...], preferred_element_type=jnp.float32)

    slots = NEAR * depth
    height = GROUPS // CHAINS * (offsets + 1) * rows

    @pl.loop(0, slots // 2)
    def _(pair):
        @pl.when((touch_of(2 * pair) >= 0) | (touch_of(2 * pair + 1) >= 0))
        def _():
            scales = [gather(2 * pair + half, half) for half in range(2)]
            make_left()
            for half in range(2):
                make_right(2 * pair + half, half)
            step = GROUPS // CHAINS
            for c in range(CHAINS):
                product_ref[c * height : (c + 1) * height, :] = sums(step * c, step * (c + 1))

            def found(a, o, half):
                at = (a * (offsets + 1) + o) * rows + half * per_touch
                return product_ref[at : at + per_touch, half * LANES : (half + 1) * LANES]

            for o in range(offsets):
                both = []
                for half in range(2):
                    total = found(0, o + 1, half)
                    for a in range(1, GROUPS):
                        shift = WIDTH * a
                        total = total + pltpu.roll(
                            jnp.where(
                                lane < LANES - shift, found(a, o + 1, half), found(a, o, half)
                            ),
                            shift,
                            1,
                        )
                    both.append(total * scales[half])
                answer_ref[
                    pl.ds(pl.multiple_of(16 * pair, 16), 16), o * LANES : (o + 1) * LANES
                ] = jnp.concatenate(both, axis=0).astype(jnp.bfloat16)

    back = [
        pltpu.make_async_copy(
            answer_ref.at[pl.ds(e * depth * per_touch, depth * per_touch), :],
            outs[e],
            sem_ref.at[e],
        )
        for e in range(NEAR)
    ]
    for copy in back:
        copy.start()
    for copy in back:
        copy.wait()


def profile(part, depth, num_query, touches, me, shards, library):
    blocks = library.shape[1]
    offsets = SHIFTS // LANES
    tiles = blocks // GROUPS
    records = shards[0].shape[0] - num_query * blocks
    per_block = rounded(depth, ROW_SLOTS) // ROW_SLOTS
    table = (rounded(NEAR * per_block, 8), LANES)
    smem = pl.BlockSpec(memory_space=pltpu.SMEM)
    vmem = pl.BlockSpec(memory_space=pltpu.VMEM)
    hbm = pl.BlockSpec(memory_space=pl.ANY)
    answers = NEAR * depth * PER_TOUCH
    flops = answers * 2 * (offsets + 1) * (blocks + 4) * LANES * LANES
    return pl.pallas_call(
        functools.partial(profile_kernel, depth, num_query, touches),
        out_shape=[
            jax.ShapeDtypeStruct((depth * PER_TOUCH, SHIFTS), jnp.bfloat16)
            for _ in range(NEAR)
        ],
        in_specs=[smem] + [hbm] * NEAR + [vmem],
        out_specs=[hbm] * NEAR,
        scratch_shapes=[
            pltpu.VMEM((NEAR, *shards[0].shape), jnp.bfloat16),
            pltpu.VMEM((records, LANES), jnp.float32),
            pltpu.VMEM(table, jnp.int32),
            pltpu.SMEM(table, jnp.int32),
            pltpu.VMEM((answers, SHIFTS), jnp.bfloat16),
            pltpu.VMEM(((blocks + offsets + 1) * 16, LANES), jnp.float32),
            pltpu.VMEM(((blocks + offsets + 1) * 16, LANES), jnp.bfloat16),
            pltpu.VMEM((2, blocks, LANES), jnp.float32),
            pltpu.VMEM((GROUPS, (tiles + offsets + 1) * 16, LANES), jnp.bfloat16),
            pltpu.VMEM(((tiles + 1) * LANES, 2 * LANES), jnp.bfloat16),
            pltpu.VMEM((GROUPS * (offsets + 1) * 16, 2 * LANES), jnp.float32),
            pltpu.SemaphoreType.DMA((NEAR + 1,)),
        ],
        compiler_params=pltpu.CompilerParams(vmem_limit_bytes=VMEM_LIMIT),
        cost_estimate=pl.CostEstimate(
            flops=8 * flops, bytes_accessed=8 * 1024 * 1024, transcendentals=0
        ),
        name=f"profile_{part}",
    )(me, *shards, library)


def unpack_kernel(part, depth, me_ref, table_ref, *refs):
    got, refs = refs[:NEAR], refs[-3:]
    out_ref, stage_ref, sem_ref = refs
    per_block = rounded(depth, ROW_SLOTS) // ROW_SLOTS

    def copy(slot, touch):
        return pltpu.make_async_copy(stage_ref.at[slot], out_ref.at[touch], sem_ref.at[slot])

    def touch_of(e, s):
        block = jnp.bitwise_xor(me_ref[0], NEAR * part + e)
        line = block * per_block + s // ROW_SLOTS
        return table_ref[line, s % ROW_SLOTS * SLOT_LANES + 2 * PER_TOUCH] - 1

    for e in range(NEAR):
        for s in range(depth):
            touch = touch_of(e, s)
            slot = e * depth + s

            @pl.when(touch >= 0)
            def _():
                stage_ref[slot] = got[e][s * PER_TOUCH : (s + 1) * PER_TOUCH, :].astype(
                    jnp.float32
                )
                copy(slot, touch).start()

    for e in range(NEAR):
        for s in range(depth):
            touch = touch_of(e, s)

            @pl.when(touch >= 0)
            def _():
                copy(e * depth + s, touch).wait()


def unpack(part, depth, touched, me, table, got, out):
    shifts = got[0].shape[1]
    smem = pl.BlockSpec(memory_space=pltpu.SMEM)
    vmem = pl.BlockSpec(memory_space=pltpu.VMEM)
    hbm = pl.BlockSpec(memory_space=pl.ANY)
    more = () if out is None else (out,)
    return pl.pallas_call(
        functools.partial(unpack_kernel, part, depth),
        out_shape=jax.ShapeDtypeStruct((touched, PER_TOUCH, shifts), jnp.float32),
        in_specs=[smem] * 2 + [vmem] * NEAR + [hbm] * len(more),
        out_specs=hbm,
        scratch_shapes=[
            pltpu.VMEM((NEAR * depth, PER_TOUCH, shifts), jnp.float32),
            pltpu.SemaphoreType.DMA((NEAR * depth,)),
        ],
        input_output_aliases={2 + NEAR: 0} if more else {},
        compiler_params=pltpu.CompilerParams(vmem_limit_bytes=VMEM_LIMIT),
        cost_estimate=pl.CostEstimate(
            flops=0, bytes_accessed=NEAR * got[0].size * 6, transcendentals=0
        ),
        name=f"unpack_{part}",
    )(me, table, *got, *more)


def local(spectra, library, cand_block, cand_local):
    devices = lax.axis_size("lib")
    num_query, num_bins = spectra.shape
    touches, per_touch = cand_local.shape[1], cand_local.shape[2]
    depth = rounded(depth_of(num_query, touches, devices), 2)
    blocks = num_bins // LANES
    records = rounded(devices * (rounded(depth, ROW_SLOTS) // ROW_SLOTS), 16)
    me = lax.axis_index("lib").astype(jnp.int32).reshape(1)

    def across(value, distance):
        if distance == 0:
            return value
        pairs = [(i, i ^ distance) for i in range(devices)]
        return lax.ppermute(value, "lib", pairs)

    shard, table = prepare(
        spectra, cand_block, cand_local.reshape(-1, per_touch), depth, records
    )
    far = devices // NEAR
    order = [0] + list(range(far - 1, 0, -1))
    heads = {part: across(shard, NEAR * part) for part in order}
    shards = {
        part: [across(heads[part], e) for e in range(NEAR)] for part in order
    }
    rows = library.reshape(-1, blocks, LANES)
    got = {}
    for part in order:
        answers = profile(part, depth, num_query, touches, me, shards[part], rows)
        got[part] = [across(answers[e], NEAR * part + e) for e in range(NEAR)]
    out = None
    for part in order:
        out = unpack(part, depth, num_query * touches, me, table, got[part], out)
    return out.reshape(num_query, touches * per_touch, SHIFTS)


def solution(mesh):
    placed = (
        P(("groups", "lib"), None),
        P("lib", None),
        P(("groups", "lib"), None),
        P(("groups", "lib"), None, None),
    )
    return jax.shard_map(
        local,
        mesh=mesh,
        in_specs=placed,
        out_specs=P(("groups", "lib"), None, None),
        check_vma=False,
    )
```

```python
import functools

import jax
import jax.numpy as jnp
from jax import lax
from jax.experimental import pallas as pl
from jax.experimental.pallas import tpu as pltpu
from jax.sharding import PartitionSpec as P

SHIFTS = 1024
BG = 32
EPSILON = 1e-06
LANES = 128
VMEM_LIMIT = 48 * 1024 * 1024
NEAR = 4
ROW_SLOTS = 4
SLOT_LANES = LANES // ROW_SLOTS
PER_TOUCH = 8
CHAINS = 4
GROUPS = 4
WIDTH = LANES // GROUPS


def rounded(value, unit):
    return -(-value // unit) * unit


def depth_of(num_query, touches, devices):
    return min(num_query, max(3, 3 * num_query * touches // (2 * devices)))


def record_values(found):
    lane = lax.broadcasted_iota(jnp.int32, found.shape, 1) % SLOT_LANES
    low = pltpu.roll(found, LANES - PER_TOUCH, 1)
    return jnp.where(lane < PER_TOUCH, found * 16 + low, found).astype(jnp.int32)


def prepare_kernel(depth, spectra_ref, named_ref, wanted_ref, out_ref, table_ref, rows_ref):
    num_query, num_bins = spectra_ref.shape
    blocks = num_bins // LANES
    values = spectra_ref[...].astype(jnp.float32)
    zeros = jnp.zeros((num_query, LANES), jnp.float32)
    wide = jnp.concatenate([values, zeros], axis=1)
    total, length = wide, 1
    while length < 2 * BG:
        total = total + pltpu.roll(total, length, 1)
        length *= 2
    total = total + pltpu.roll(wide, length, 1)
    total = pltpu.roll(total, total.shape[1] - BG, 1)[:, :num_bins]
    centered = values - total / (2 * BG + 1)
    factor = lax.rsqrt(jnp.mean(centered * centered, axis=1, keepdims=True) + EPSILON)
    prepared = (centered * factor).astype(jnp.bfloat16)
    row = lax.broadcasted_iota(jnp.int32, (LANES, LANES), 0)
    col = lax.broadcasted_iota(jnp.int32, (LANES, LANES), 1)
    flip = jnp.where(row + col == LANES - 1, 1.0, 0.0).astype(jnp.bfloat16)
    for block in range(blocks):
        piece = prepared[:, block * LANES : (block + 1) * LANES]
        turned = jnp.dot(piece, flip, preferred_element_type=jnp.float32)
        rows_ref[pl.ds(blocks - 1 - block, num_query, stride=blocks), :] = turned
    out_ref[0 : num_query * blocks, :] = rows_ref[...].astype(jnp.bfloat16)

    touches = named_ref.shape[1]
    touched = num_query * touches
    records = table_ref.shape[0]
    per_block = rounded(depth, ROW_SLOTS) // ROW_SLOTS
    touch = lax.broadcasted_iota(jnp.int32, (touched, num_query), 0)
    query = lax.broadcasted_iota(jnp.int32, (touched, num_query), 1)
    owner = jnp.where(touch // touches == query, 1.0, 0.0).astype(jnp.bfloat16)
    named = named_ref[...].astype(jnp.float32).astype(jnp.bfloat16)
    spread = jnp.dot(owner, named, preferred_element_type=jnp.float32)
    touch = lax.broadcasted_iota(jnp.int32, (touched, touches), 0)
    which = lax.broadcasted_iota(jnp.int32, (touched, touches), 1)
    block_col = jnp.sum(
        jnp.where(touch % touches == which, spread, 0.0), axis=1, keepdims=True
    )
    row = lax.broadcasted_iota(jnp.int32, (touched, touched), 0)
    col = lax.broadcasted_iota(jnp.int32, (touched, touched), 1)
    block_row = jnp.sum(jnp.where(row == col, block_col, 0.0), axis=0, keepdims=True)
    earlier = (block_col == block_row) & (row < col)
    rank = jnp.sum(jnp.where(earlier, 1.0, 0.0), axis=0, keepdims=True).astype(jnp.int32)
    place = block_row.astype(jnp.int32) * per_block + rank // ROW_SLOTS
    wanted = wanted_ref[...]
    high = (wanted // 16).astype(jnp.float32).astype(jnp.bfloat16)
    low = (wanted % 16).astype(jnp.float32).astype(jnp.bfloat16)
    unit = lax.broadcasted_iota(jnp.int32, (PER_TOUCH, LANES), 0)
    lane = lax.broadcasted_iota(jnp.int32, (PER_TOUCH, LANES), 1)
    row = lax.broadcasted_iota(jnp.int32, (records, touched), 0)
    touch = lax.broadcasted_iota(jnp.int32, (touched, LANES), 0)
    wide_lane = lax.broadcasted_iota(jnp.int32, (touched, LANES), 1)
    found = jnp.zeros((records, LANES), jnp.float32)
    for group in range(ROW_SLOTS):
        start = group * SLOT_LANES
        to_high = jnp.where(lane == start + unit, 1.0, 0.0).astype(jnp.bfloat16)
        to_low = jnp.where(lane == start + PER_TOUCH + unit, 1.0, 0.0).astype(jnp.bfloat16)
        data = jnp.dot(high, to_high, preferred_element_type=jnp.float32)
        data = data + jnp.dot(low, to_low, preferred_element_type=jnp.float32)
        data = jnp.where(
            wide_lane == start + 2 * PER_TOUCH, (touch + 1).astype(jnp.float32), data
        ).astype(jnp.bfloat16)
        pick = jnp.where((row == place) & (rank % ROW_SLOTS == group), 1.0, 0.0)
        found = found + jnp.dot(
            pick.astype(jnp.bfloat16), data, preferred_element_type=jnp.float32
        )
    out_ref[num_query * blocks :, :] = found.astype(jnp.bfloat16)
    table_ref[...] = record_values(found)


def prepare(spectra, named, wanted, depth, records):
    num_query, num_bins = spectra.shape
    rows = num_query * num_bins // LANES
    return pl.pallas_call(
        functools.partial(prepare_kernel, depth),
        out_shape=(
            jax.ShapeDtypeStruct((rows + records, LANES), jnp.bfloat16),
            jax.ShapeDtypeStruct((records, LANES), jnp.int32),
        ),
        scratch_shapes=[pltpu.VMEM((rows, LANES), jnp.float32)],
        compiler_params=pltpu.CompilerParams(vmem_limit_bytes=VMEM_LIMIT),
        name="prepare",
    )(spectra, named, wanted)


def profile_kernel(depth, num_query, touches, me_ref, *refs):
    shards, library_ref, refs = refs[:NEAR], refs[NEAR], refs[NEAR + 1 :]
    outs, refs = refs[:NEAR], refs[NEAR:]
    query_ref, record_ref, found_ref, table_ref, order_ref, answer_ref, sem_ref = refs[:7]
    sets = [refs[7 + i :: 2] for i in range(2)]
    per_touch = PER_TOUCH
    rows = 2 * per_touch
    blocks = library_ref.shape[1]
    offsets = SHIFTS // LANES
    first = offsets // 2 + 1
    tiles = blocks // GROUPS
    query_rows = num_query * blocks
    per_block = rounded(depth, ROW_SLOTS) // ROW_SLOTS
    row = lax.broadcasted_iota(jnp.int32, (8, LANES), 0)
    lane = lax.broadcasted_iota(jnp.int32, (8, LANES), 1)
    lane16 = lax.broadcasted_iota(jnp.int32, (rows, LANES), 1)

    copies = [
        pltpu.make_async_copy(shards[e], query_ref.at[e], sem_ref.at[e]) for e in range(NEAR)
    ]
    for copy in copies:
        copy.start()
    for cand_ref, _, _, _, right_ref, _, _ in sets:
        cand_ref[...] = jnp.zeros(cand_ref.shape, cand_ref.dtype)
        right_ref[...] = jnp.zeros(right_ref.shape, right_ref.dtype)
    found_ref[...] = jnp.zeros(found_ref.shape, found_ref.dtype)
    for e in range(NEAR):
        copies[e].wait()
        record_ref[...] = query_ref[e, query_rows:, :].astype(jnp.float32)
        found_ref[e * per_block : (e + 1) * per_block, :] = record_values(
            record_ref[pl.ds(me_ref[0] * per_block, per_block), :]
        )
    to_scalars = pltpu.make_async_copy(found_ref, table_ref, sem_ref.at[NEAR])
    to_scalars.start()
    to_scalars.wait()

    def entry(slot):
        e = slot // depth
        s = slot % depth
        return e, e * per_block + s // ROW_SLOTS, s % ROW_SLOTS * SLOT_LANES

    def touch_of(slot):
        _, line, start = entry(slot)
        return table_ref[line, start + 2 * per_touch] - 1

    def choose(pieces):
        value = pieces[0]
        for group in range(1, GROUPS):
            value = jnp.where(lane16 < group * WIDTH, value, pieces[group])
        return value

    def gather(cand_ref, slot, half):
        _, line, start = entry(slot)
        for k in range(per_touch):
            wanted = table_ref[line, start + k]
            cand_ref[pl.ds(first * rows + half * per_touch + k, blocks, stride=rows), :] = (
                library_ref[wanted].astype(jnp.float32)
            )
        square = jnp.zeros((per_touch, LANES), jnp.float32)
        for b in range(blocks):
            piece = cand_ref[pl.ds((first + b) * rows + half * per_touch, per_touch), :]
            square = square + piece * piece
        mean = jnp.sum(square, axis=1, keepdims=True) / (blocks * LANES)
        return lax.rsqrt(mean + EPSILON)

    def make_left(cand_ref, packed_ref, left_ref):
        for b in range(blocks + offsets + 1):
            packed_ref[pl.ds(rows * b, rows), :] = cand_ref[pl.ds(rows * b, rows), :].astype(
                jnp.bfloat16
            )
        for t in range(tiles + offsets + 1):
            given = [packed_ref[pl.ds(rows * (t + tiles * g), rows), :] for g in range(GROUPS)]
            turned = []
            for c in range(GROUPS):
                mixed = choose([given[(a + c) % GROUPS] for a in range(GROUPS)])
                turned.append(pltpu.roll(mixed, WIDTH * c, 1) if c else mixed)
            for a in range(GROUPS):
                left_ref[a, pl.ds(rows * t, rows), :] = choose(
                    [turned[(g - a) % GROUPS] for g in range(GROUPS)]
                )

    def make_right(spectrum_ref, right_ref, slot, half):
        query = jnp.maximum(touch_of(slot), 0) // touches
        spectrum_ref[half] = query_ref[
            entry(slot)[0], pl.ds(pl.multiple_of(query * blocks, blocks), blocks), :
        ].astype(jnp.float32)
        zero = jnp.zeros((8, LANES), jnp.float32)
        before = (zero, zero)
        before_shifted = jnp.zeros((16, LANES), jnp.bfloat16)
        columns = slice(half * LANES, (half + 1) * LANES)
        for b in range(blocks + 1):
            if b < blocks:
                wide = jnp.broadcast_to(spectrum_ref[half, pl.ds(b, 1), :], (8, LANES))
                now = tuple(
                    pltpu.roll(wide, 1 + 8 * h, 1, stride=1, stride_axis=0) for h in range(2)
                )
            else:
                now = (zero, zero)
            shifted = jnp.concatenate(
                [jnp.where(lane > row + 8 * h, now[h], before[h]) for h in range(2)], axis=0
            ).astype(jnp.bfloat16)
            j = blocks - 1 - b
            place = 0 if j < 0 else (j % tiles + 1) * LANES + j // tiles * WIDTH
            right_ref[pl.ds(place, 16), columns] = shifted
            for c in range(16, WIDTH, 16):
                right_ref[pl.ds(place + c, 16), columns] = pltpu.roll(
                    jnp.where(lane16 < LANES - c, shifted, before_shifted), c, 1
                )
            before, before_shifted = now, shifted

    def sums(left_ref, right_ref, low, high):
        left = jnp.concatenate(
            [
                jnp.concatenate(
                    [
                        left_ref[a, pl.ds(rows * t, rows * (offsets + 1)), :]
                        for t in range(tiles + 1)
                    ],
                    axis=1,
                )
                for a in range(low, high)
            ],
            axis=0,
        )
        return jnp.dot(left, right_ref[...], preferred_element_type=jnp.float32)

    slots = NEAR * depth
    height = GROUPS // CHAINS * (offsets + 1) * rows

    step = GROUPS // CHAINS

    def make(pair, refs):
        cand_ref, packed_ref, spectrum_ref, left_ref, right_ref, scale_ref, _ = refs
        for half in range(2):
            scale_ref[half] = jnp.broadcast_to(
                gather(cand_ref, 2 * pair + half, half), (per_touch, LANES)
            )
        make_left(cand_ref, packed_ref, left_ref)
        for half in range(2):
            make_right(spectrum_ref, right_ref, 2 * pair + half, half)

    def finish(pair, refs):
        _, _, _, left_ref, right_ref, scale_ref, product_ref = refs
        for c in range(CHAINS):
            product_ref[c * height : (c + 1) * height, :] = sums(
                left_ref, right_ref, step * c, step * (c + 1)
            )

        def found(a, o, half):
            at = (a * (offsets + 1) + o) * rows + half * per_touch
            return product_ref[at : at + per_touch, half * LANES : (half + 1) * LANES]

        for o in range(offsets):
            both = []
            for half in range(2):
                total = found(0, o + 1, half)
                for a in range(1, GROUPS):
                    shift = WIDTH * a
                    total = total + pltpu.roll(
                        jnp.where(
                            lane < LANES - shift, found(a, o + 1, half), found(a, o, half)
                        ),
                        shift,
                        1,
                    )
                both.append(total * scale_ref[half])
            answer_ref[
                pl.ds(pl.multiple_of(16 * pair, 16), 16), o * LANES : (o + 1) * LANES
            ] = jnp.concatenate(both, axis=0).astype(jnp.bfloat16)

    order_ref[0] = 0

    def list_pair(pair, used):
        named = (touch_of(2 * pair) >= 0) | (touch_of(2 * pair + 1) >= 0)

        @pl.when(named)
        def _():
            for ahead in range(3):
                order_ref[used + ahead] = pair

        return used + named.astype(jnp.int32)

    used = lax.fori_loop(0, slots // 2, list_pair, jnp.int32(0))
    make(order_ref[0], sets[0])

    @pl.loop(0, (used + 1) // 2)
    def _(i):
        make(order_ref[2 * i + 1], sets[1])
        finish(order_ref[2 * i], sets[0])
        make(order_ref[2 * i + 2], sets[0])
        finish(order_ref[2 * i + 1], sets[1])

    back = [
        pltpu.make_async_copy(
            answer_ref.at[pl.ds(e * depth * per_touch, depth * per_touch), :],
            outs[e],
            sem_ref.at[e],
        )
        for e in range(NEAR)
    ]
    for copy in back:
        copy.start()
    for copy in back:
        copy.wait()


def profile(part, depth, num_query, touches, me, shards, library):
    blocks = library.shape[1]
    offsets = SHIFTS // LANES
    tiles = blocks // GROUPS
    records = shards[0].shape[0] - num_query * blocks
    per_block = rounded(depth, ROW_SLOTS) // ROW_SLOTS
    table = (rounded(NEAR * per_block, 8), LANES)
    smem = pl.BlockSpec(memory_space=pltpu.SMEM)
    vmem = pl.BlockSpec(memory_space=pltpu.VMEM)
    hbm = pl.BlockSpec(memory_space=pl.ANY)
    answers = NEAR * depth * PER_TOUCH
    flops = answers * 2 * (offsets + 1) * (blocks + 4) * LANES * LANES
    return pl.pallas_call(
        functools.partial(profile_kernel, depth, num_query, touches),
        out_shape=[
            jax.ShapeDtypeStruct((depth * PER_TOUCH, SHIFTS), jnp.bfloat16)
            for _ in range(NEAR)
        ],
        in_specs=[smem] + [hbm] * NEAR + [vmem],
        out_specs=[hbm] * NEAR,
        scratch_shapes=[
            pltpu.VMEM((NEAR, *shards[0].shape), jnp.bfloat16),
            pltpu.VMEM((records, LANES), jnp.float32),
            pltpu.VMEM(table, jnp.int32),
            pltpu.SMEM(table, jnp.int32),
            pltpu.SMEM((NEAR * depth // 2 + 3,), jnp.int32),
            pltpu.VMEM((answers, SHIFTS), jnp.bfloat16),
            pltpu.SemaphoreType.DMA((NEAR + 1,)),
        ]
        + [
            buffer
            for buffer in (
                pltpu.VMEM(((blocks + offsets + 1) * 16, LANES), jnp.float32),
                pltpu.VMEM(((blocks + offsets + 1) * 16, LANES), jnp.bfloat16),
                pltpu.VMEM((2, blocks, LANES), jnp.float32),
                pltpu.VMEM((GROUPS, (tiles + offsets + 1) * 16, LANES), jnp.bfloat16),
                pltpu.VMEM(((tiles + 1) * LANES, 2 * LANES), jnp.bfloat16),
                pltpu.VMEM((2, PER_TOUCH, LANES), jnp.float32),
                pltpu.VMEM((GROUPS * (offsets + 1) * 16, 2 * LANES), jnp.float32),
            )
            for _ in range(2)
        ],
        compiler_params=pltpu.CompilerParams(vmem_limit_bytes=VMEM_LIMIT),
        cost_estimate=pl.CostEstimate(
            flops=8 * flops, bytes_accessed=8 * 1024 * 1024, transcendentals=0
        ),
        name=f"profile_{part}",
    )(me, *shards, library)


def unpack_kernel(part, depth, me_ref, table_ref, *refs):
    got, refs = refs[:NEAR], refs[-3:]
    out_ref, stage_ref, sem_ref = refs
    per_block = rounded(depth, ROW_SLOTS) // ROW_SLOTS

    def copy(slot, touch):
        return pltpu.make_async_copy(stage_ref.at[slot], out_ref.at[touch], sem_ref.at[slot])

    def touch_of(e, s):
        block = jnp.bitwise_xor(me_ref[0], NEAR * part + e)
        line = block * per_block + s // ROW_SLOTS
        return table_ref[line, s % ROW_SLOTS * SLOT_LANES + 2 * PER_TOUCH] - 1

    for e in range(NEAR):
        for s in range(depth):
            touch = touch_of(e, s)
            slot = e * depth + s

            @pl.when(touch >= 0)
            def _():
                stage_ref[slot] = got[e][s * PER_TOUCH : (s + 1) * PER_TOUCH, :].astype(
                    jnp.float32
                )
                copy(slot, touch).start()

    for e in range(NEAR):
        for s in range(depth):
            touch = touch_of(e, s)

            @pl.when(touch >= 0)
            def _():
                copy(e * depth + s, touch).wait()


def unpack(part, depth, touched, me, table, got, out):
    shifts = got[0].shape[1]
    smem = pl.BlockSpec(memory_space=pltpu.SMEM)
    vmem = pl.BlockSpec(memory_space=pltpu.VMEM)
    hbm = pl.BlockSpec(memory_space=pl.ANY)
    more = () if out is None else (out,)
    return pl.pallas_call(
        functools.partial(unpack_kernel, part, depth),
        out_shape=jax.ShapeDtypeStruct((touched, PER_TOUCH, shifts), jnp.float32),
        in_specs=[smem] * 2 + [vmem] * NEAR + [hbm] * len(more),
        out_specs=hbm,
        scratch_shapes=[
            pltpu.VMEM((NEAR * depth, PER_TOUCH, shifts), jnp.float32),
            pltpu.SemaphoreType.DMA((NEAR * depth,)),
        ],
        input_output_aliases={2 + NEAR: 0} if more else {},
        compiler_params=pltpu.CompilerParams(vmem_limit_bytes=VMEM_LIMIT),
        cost_estimate=pl.CostEstimate(
            flops=0, bytes_accessed=NEAR * got[0].size * 6, transcendentals=0
        ),
        name=f"unpack_{part}",
    )(me, table, *got, *more)


def local(spectra, library, cand_block, cand_local):
    devices = lax.axis_size("lib")
    num_query, num_bins = spectra.shape
    touches, per_touch = cand_local.shape[1], cand_local.shape[2]
    depth = rounded(depth_of(num_query, touches, devices), 2)
    blocks = num_bins // LANES
    records = rounded(devices * (rounded(depth, ROW_SLOTS) // ROW_SLOTS), 16)
    me = lax.axis_index("lib").astype(jnp.int32).reshape(1)

    def across(value, distance):
        if distance == 0:
            return value
        pairs = [(i, i ^ distance) for i in range(devices)]
        return lax.ppermute(value, "lib", pairs)

    shard, table = prepare(
        spectra, cand_block, cand_local.reshape(-1, per_touch), depth, records
    )
    far = devices // NEAR
    order = [0] + list(range(far - 1, 0, -1))
    heads = {part: across(shard, NEAR * part) for part in order}
    shards = {
        part: [across(heads[part], e) for e in range(NEAR)] for part in order
    }
    rows = library.reshape(-1, blocks, LANES)
    got = {}
    for part in order:
        answers = profile(part, depth, num_query, touches, me, shards[part], rows)
        got[part] = [across(answers[e], NEAR * part + e) for e in range(NEAR)]
    out = None
    for part in order:
        out = unpack(part, depth, num_query * touches, me, table, got[part], out)
    return out.reshape(num_query, touches * per_touch, SHIFTS)


def solution(mesh):
    placed = (
        P(("groups", "lib"), None),
        P("lib", None),
        P(("groups", "lib"), None),
        P(("groups", "lib"), None, None),
    )
    return jax.shard_map(
        local,
        mesh=mesh,
        in_specs=placed,
        out_specs=P(("groups", "lib"), None, None),
        check_vma=False,
    )
```

```python
import functools

import jax
import jax.numpy as jnp
from jax import lax
from jax.experimental import pallas as pl
from jax.experimental.pallas import tpu as pltpu
from jax.sharding import PartitionSpec as P

SHIFTS = 1024
BG = 32
EPSILON = 1e-06
LANES = 128
VMEM_LIMIT = 48 * 1024 * 1024
NEAR = 4
ROW_SLOTS = 4
SLOT_LANES = LANES // ROW_SLOTS
PER_TOUCH = 8
CHAINS = 2
GROUPS = 4
WIDTH = LANES // GROUPS


def rounded(value, unit):
    return -(-value // unit) * unit


def depth_of(num_query, touches, devices):
    return min(num_query, max(3, 3 * num_query * touches // (2 * devices)))


def record_values(found):
    lane = lax.broadcasted_iota(jnp.int32, found.shape, 1) % SLOT_LANES
    low = pltpu.roll(found, LANES - PER_TOUCH, 1)
    return jnp.where(lane < PER_TOUCH, found * 16 + low, found).astype(jnp.int32)


def prepare_kernel(depth, spectra_ref, named_ref, wanted_ref, out_ref, table_ref, rows_ref):
    num_query, num_bins = spectra_ref.shape
    blocks = num_bins // LANES
    values = spectra_ref[...].astype(jnp.float32)
    zeros = jnp.zeros((num_query, LANES), jnp.float32)
    wide = jnp.concatenate([values, zeros], axis=1)
    total, length = wide, 1
    while length < 2 * BG:
        total = total + pltpu.roll(total, length, 1)
        length *= 2
    total = total + pltpu.roll(wide, length, 1)
    total = pltpu.roll(total, total.shape[1] - BG, 1)[:, :num_bins]
    centered = values - total / (2 * BG + 1)
    factor = lax.rsqrt(jnp.mean(centered * centered, axis=1, keepdims=True) + EPSILON)
    prepared = (centered * factor).astype(jnp.bfloat16)
    row = lax.broadcasted_iota(jnp.int32, (LANES, LANES), 0)
    col = lax.broadcasted_iota(jnp.int32, (LANES, LANES), 1)
    flip = jnp.where(row + col == LANES - 1, 1.0, 0.0).astype(jnp.bfloat16)
    for block in range(blocks):
        piece = prepared[:, block * LANES : (block + 1) * LANES]
        turned = jnp.dot(piece, flip, preferred_element_type=jnp.float32)
        rows_ref[pl.ds(blocks - 1 - block, num_query, stride=blocks), :] = turned
    out_ref[0 : num_query * blocks, :] = rows_ref[...].astype(jnp.bfloat16)

    touches = named_ref.shape[1]
    touched = num_query * touches
    records = table_ref.shape[0]
    per_block = rounded(depth, ROW_SLOTS) // ROW_SLOTS
    touch = lax.broadcasted_iota(jnp.int32, (touched, num_query), 0)
    query = lax.broadcasted_iota(jnp.int32, (touched, num_query), 1)
    owner = jnp.where(touch // touches == query, 1.0, 0.0).astype(jnp.bfloat16)
    named = named_ref[...].astype(jnp.float32).astype(jnp.bfloat16)
    spread = jnp.dot(owner, named, preferred_element_type=jnp.float32)
    touch = lax.broadcasted_iota(jnp.int32, (touched, touches), 0)
    which = lax.broadcasted_iota(jnp.int32, (touched, touches), 1)
    block_col = jnp.sum(
        jnp.where(touch % touches == which, spread, 0.0), axis=1, keepdims=True
    )
    row = lax.broadcasted_iota(jnp.int32, (touched, touched), 0)
    col = lax.broadcasted_iota(jnp.int32, (touched, touched), 1)
    block_row = jnp.sum(jnp.where(row == col, block_col, 0.0), axis=0, keepdims=True)
    earlier = (block_col == block_row) & (row < col)
    rank = jnp.sum(jnp.where(earlier, 1.0, 0.0), axis=0, keepdims=True).astype(jnp.int32)
    place = block_row.astype(jnp.int32) * per_block + rank // ROW_SLOTS
    wanted = wanted_ref[...]
    high = (wanted // 16).astype(jnp.float32).astype(jnp.bfloat16)
    low = (wanted % 16).astype(jnp.float32).astype(jnp.bfloat16)
    unit = lax.broadcasted_iota(jnp.int32, (PER_TOUCH, LANES), 0)
    lane = lax.broadcasted_iota(jnp.int32, (PER_TOUCH, LANES), 1)
    row = lax.broadcasted_iota(jnp.int32, (records, touched), 0)
    touch = lax.broadcasted_iota(jnp.int32, (touched, LANES), 0)
    wide_lane = lax.broadcasted_iota(jnp.int32, (touched, LANES), 1)
    found = jnp.zeros((records, LANES), jnp.float32)
    for group in range(ROW_SLOTS):
        start = group * SLOT_LANES
        to_high = jnp.where(lane == start + unit, 1.0, 0.0).astype(jnp.bfloat16)
        to_low = jnp.where(lane == start + PER_TOUCH + unit, 1.0, 0.0).astype(jnp.bfloat16)
        data = jnp.dot(high, to_high, preferred_element_type=jnp.float32)
        data = data + jnp.dot(low, to_low, preferred_element_type=jnp.float32)
        data = jnp.where(
            wide_lane == start + 2 * PER_TOUCH, (touch + 1).astype(jnp.float32), data
        ).astype(jnp.bfloat16)
        pick = jnp.where((row == place) & (rank % ROW_SLOTS == group), 1.0, 0.0)
        found = found + jnp.dot(
            pick.astype(jnp.bfloat16), data, preferred_element_type=jnp.float32
        )
    out_ref[num_query * blocks :, :] = found.astype(jnp.bfloat16)
    table_ref[...] = record_values(found)


def prepare(spectra, named, wanted, depth, records):
    num_query, num_bins = spectra.shape
    rows = num_query * num_bins // LANES
    return pl.pallas_call(
        functools.partial(prepare_kernel, depth),
        out_shape=(
            jax.ShapeDtypeStruct((rows + records, LANES), jnp.bfloat16),
            jax.ShapeDtypeStruct((records, LANES), jnp.int32),
        ),
        scratch_shapes=[pltpu.VMEM((rows, LANES), jnp.float32)],
        compiler_params=pltpu.CompilerParams(vmem_limit_bytes=VMEM_LIMIT),
        name="prepare",
    )(spectra, named, wanted)


def profile_kernel(depth, num_query, touches, me_ref, *refs):
    shards, library_ref, refs = refs[:NEAR], refs[NEAR], refs[NEAR + 1 :]
    outs, refs = refs[:NEAR], refs[NEAR:]
    query_ref, record_ref, found_ref, table_ref, order_ref, answer_ref, sem_ref = refs[:7]
    cand_ref, packed_ref, spectrum_ref, product_ref = refs[7:11]
    made, used_now = refs[11:14], refs[14:17]
    per_touch = PER_TOUCH
    rows = 2 * per_touch
    blocks = library_ref.shape[1]
    offsets = SHIFTS // LANES
    first = offsets // 2 + 1
    tiles = blocks // GROUPS
    query_rows = num_query * blocks
    per_block = rounded(depth, ROW_SLOTS) // ROW_SLOTS
    row = lax.broadcasted_iota(jnp.int32, (8, LANES), 0)
    lane = lax.broadcasted_iota(jnp.int32, (8, LANES), 1)
    lane16 = lax.broadcasted_iota(jnp.int32, (rows, LANES), 1)

    copies = [
        pltpu.make_async_copy(shards[e], query_ref.at[e], sem_ref.at[e]) for e in range(NEAR)
    ]
    for copy in copies:
        copy.start()
    cand_ref[...] = jnp.zeros(cand_ref.shape, cand_ref.dtype)
    for ref in (*made, *used_now):
        ref[...] = jnp.zeros(ref.shape, ref.dtype)
    found_ref[...] = jnp.zeros(found_ref.shape, found_ref.dtype)
    for e in range(NEAR):
        copies[e].wait()
        record_ref[...] = query_ref[e, query_rows:, :].astype(jnp.float32)
        found_ref[e * per_block : (e + 1) * per_block, :] = record_values(
            record_ref[pl.ds(me_ref[0] * per_block, per_block), :]
        )
    to_scalars = pltpu.make_async_copy(found_ref, table_ref, sem_ref.at[NEAR])
    to_scalars.start()
    to_scalars.wait()

    def entry(slot):
        e = slot // depth
        s = slot % depth
        return e, e * per_block + s // ROW_SLOTS, s % ROW_SLOTS * SLOT_LANES

    def touch_of(slot):
        _, line, start = entry(slot)
        return table_ref[line, start + 2 * per_touch] - 1

    def choose(pieces):
        value = pieces[0]
        for group in range(1, GROUPS):
            value = jnp.where(lane16 < group * WIDTH, value, pieces[group])
        return value

    def gather(cand_ref, slot, half):
        _, line, start = entry(slot)
        for k in range(per_touch):
            wanted = table_ref[line, start + k]
            cand_ref[pl.ds(first * rows + half * per_touch + k, blocks, stride=rows), :] = (
                library_ref[wanted].astype(jnp.float32)
            )
        square = jnp.zeros((per_touch, LANES), jnp.float32)
        for b in range(blocks):
            piece = cand_ref[pl.ds((first + b) * rows + half * per_touch, per_touch), :]
            square = square + piece * piece
        mean = jnp.sum(square, axis=1, keepdims=True) / (blocks * LANES)
        return lax.rsqrt(mean + EPSILON)

    def make_left(cand_ref, packed_ref, left_ref):
        for b in range(blocks + offsets + 1):
            packed_ref[pl.ds(rows * b, rows), :] = cand_ref[pl.ds(rows * b, rows), :].astype(
                jnp.bfloat16
            )
        for t in range(tiles + offsets + 1):
            given = [packed_ref[pl.ds(rows * (t + tiles * g), rows), :] for g in range(GROUPS)]
            turned = []
            for c in range(GROUPS):
                mixed = choose([given[(a + c) % GROUPS] for a in range(GROUPS)])
                turned.append(pltpu.roll(mixed, WIDTH * c, 1) if c else mixed)
            for a in range(GROUPS):
                left_ref[a, pl.ds(rows * t, rows), :] = choose(
                    [turned[(g - a) % GROUPS] for g in range(GROUPS)]
                )

    def make_right(spectrum_ref, right_ref, slot, half):
        query = jnp.maximum(touch_of(slot), 0) // touches
        spectrum_ref[half] = query_ref[
            entry(slot)[0], pl.ds(pl.multiple_of(query * blocks, blocks), blocks), :
        ].astype(jnp.float32)
        zero = jnp.zeros((8, LANES), jnp.float32)
        before = (zero, zero)
        before_shifted = jnp.zeros((16, LANES), jnp.bfloat16)
        columns = slice(half * LANES, (half + 1) * LANES)
        for b in range(blocks + 1):
            if b < blocks:
                wide = jnp.broadcast_to(spectrum_ref[half, pl.ds(b, 1), :], (8, LANES))
                now = tuple(
                    pltpu.roll(wide, 1 + 8 * h, 1, stride=1, stride_axis=0) for h in range(2)
                )
            else:
                now = (zero, zero)
            shifted = jnp.concatenate(
                [jnp.where(lane > row + 8 * h, now[h], before[h]) for h in range(2)], axis=0
            ).astype(jnp.bfloat16)
            j = blocks - 1 - b
            place = 0 if j < 0 else (j % tiles + 1) * LANES + j // tiles * WIDTH
            right_ref[pl.ds(place, 16), columns] = shifted
            for c in range(16, WIDTH, 16):
                right_ref[pl.ds(place + c, 16), columns] = pltpu.roll(
                    jnp.where(lane16 < LANES - c, shifted, before_shifted), c, 1
                )
            before, before_shifted = now, shifted

    def sums(left_ref, right_ref, low, high):
        left = jnp.concatenate(
            [
                jnp.concatenate(
                    [
                        left_ref[a, pl.ds(rows * t, rows * (offsets + 1)), :]
                        for t in range(tiles + 1)
                    ],
                    axis=1,
                )
                for a in range(low, high)
            ],
            axis=0,
        )
        return jnp.dot(left, right_ref[...], preferred_element_type=jnp.float32)

    slots = NEAR * depth
    height = GROUPS // CHAINS * (offsets + 1) * rows

    step = GROUPS // CHAINS

    def make(pair):
        left_ref, right_ref, scale_ref = made
        for half in range(2):
            scale_ref[half] = jnp.broadcast_to(
                gather(cand_ref, 2 * pair + half, half), (per_touch, LANES)
            )
        make_left(cand_ref, packed_ref, left_ref)
        for half in range(2):
            make_right(spectrum_ref, right_ref, 2 * pair + half, half)

    def finish(pair):
        left_ref, right_ref, scale_ref = used_now
        for c in range(CHAINS):
            product_ref[c * height : (c + 1) * height, :] = sums(
                left_ref, right_ref, step * c, step * (c + 1)
            )

        def found(a, o, half):
            at = (a * (offsets + 1) + o) * rows + half * per_touch
            return product_ref[at : at + per_touch, half * LANES : (half + 1) * LANES]

        for o in range(offsets):
            both = []
            for half in range(2):
                total = found(0, o + 1, half)
                for a in range(1, GROUPS):
                    shift = WIDTH * a
                    total = total + pltpu.roll(
                        jnp.where(
                            lane < LANES - shift, found(a, o + 1, half), found(a, o, half)
                        ),
                        shift,
                        1,
                    )
                both.append(total * scale_ref[half])
            answer_ref[
                pl.ds(pl.multiple_of(16 * pair, 16), 16), o * LANES : (o + 1) * LANES
            ] = jnp.concatenate(both, axis=0).astype(jnp.bfloat16)

    order_ref[0] = 0

    def list_pair(pair, used):
        named = (touch_of(2 * pair) >= 0) | (touch_of(2 * pair + 1) >= 0)

        @pl.when(named)
        def _():
            for ahead in range(3):
                order_ref[used + ahead] = pair

        return used + named.astype(jnp.int32)

    used = lax.fori_loop(0, slots // 2, list_pair, jnp.int32(0))

    @pl.loop(0, used + 1)
    def _(i):
        for source, target in zip(made, used_now):
            target[...] = source[...]
        finish(order_ref[jnp.maximum(i - 1, 0)])
        make(order_ref[i])

    back = [
        pltpu.make_async_copy(
            answer_ref.at[pl.ds(e * depth * per_touch, depth * per_touch), :],
            outs[e],
            sem_ref.at[e],
        )
        for e in range(NEAR)
    ]
    for copy in back:
        copy.start()
    for copy in back:
        copy.wait()


def profile(part, depth, num_query, touches, me, shards, library):
    blocks = library.shape[1]
    offsets = SHIFTS // LANES
    tiles = blocks // GROUPS
    records = shards[0].shape[0] - num_query * blocks
    per_block = rounded(depth, ROW_SLOTS) // ROW_SLOTS
    table = (rounded(NEAR * per_block, 8), LANES)
    smem = pl.BlockSpec(memory_space=pltpu.SMEM)
    vmem = pl.BlockSpec(memory_space=pltpu.VMEM)
    hbm = pl.BlockSpec(memory_space=pl.ANY)
    answers = NEAR * depth * PER_TOUCH
    flops = answers * 2 * (offsets + 1) * (blocks + 4) * LANES * LANES
    return pl.pallas_call(
        functools.partial(profile_kernel, depth, num_query, touches),
        out_shape=[
            jax.ShapeDtypeStruct((depth * PER_TOUCH, SHIFTS), jnp.bfloat16)
            for _ in range(NEAR)
        ],
        in_specs=[smem] + [hbm] * NEAR + [vmem],
        out_specs=[hbm] * NEAR,
        scratch_shapes=[
            pltpu.VMEM((NEAR, *shards[0].shape), jnp.bfloat16),
            pltpu.VMEM((records, LANES), jnp.float32),
            pltpu.VMEM(table, jnp.int32),
            pltpu.SMEM(table, jnp.int32),
            pltpu.SMEM((NEAR * depth // 2 + 3,), jnp.int32),
            pltpu.VMEM((answers, SHIFTS), jnp.bfloat16),
            pltpu.SemaphoreType.DMA((NEAR + 1,)),
        ]
        + [
            pltpu.VMEM(((blocks + offsets + 1) * 16, LANES), jnp.float32),
            pltpu.VMEM(((blocks + offsets + 1) * 16, LANES), jnp.bfloat16),
            pltpu.VMEM((2, blocks, LANES), jnp.float32),
            pltpu.VMEM((GROUPS * (offsets + 1) * 16, 2 * LANES), jnp.float32),
        ]
        + [
            pltpu.VMEM((GROUPS, (tiles + offsets + 1) * 16, LANES), jnp.bfloat16),
            pltpu.VMEM(((tiles + 1) * LANES, 2 * LANES), jnp.bfloat16),
            pltpu.VMEM((2, PER_TOUCH, LANES), jnp.float32),
        ]
        * 2,
        compiler_params=pltpu.CompilerParams(vmem_limit_bytes=VMEM_LIMIT),
        cost_estimate=pl.CostEstimate(
            flops=8 * flops, bytes_accessed=8 * 1024 * 1024, transcendentals=0
        ),
        name=f"profile_{part}",
    )(me, *shards, library)


def unpack_kernel(part, depth, me_ref, table_ref, *refs):
    got, refs = refs[:NEAR], refs[-3:]
    out_ref, stage_ref, sem_ref = refs
    per_block = rounded(depth, ROW_SLOTS) // ROW_SLOTS

    def copy(slot, touch):
        return pltpu.make_async_copy(stage_ref.at[slot], out_ref.at[touch], sem_ref.at[slot])

    def touch_of(e, s):
        block = jnp.bitwise_xor(me_ref[0], NEAR * part + e)
        line = block * per_block + s // ROW_SLOTS
        return table_ref[line, s % ROW_SLOTS * SLOT_LANES + 2 * PER_TOUCH] - 1

    for e in range(NEAR):
        for s in range(depth):
            touch = touch_of(e, s)
            slot = e * depth + s

            @pl.when(touch >= 0)
            def _():
                stage_ref[slot] = got[e][s * PER_TOUCH : (s + 1) * PER_TOUCH, :].astype(
                    jnp.float32
                )
                copy(slot, touch).start()

    for e in range(NEAR):
        for s in range(depth):
            touch = touch_of(e, s)

            @pl.when(touch >= 0)
            def _():
                copy(e * depth + s, touch).wait()


def unpack(part, depth, touched, me, table, got, out):
    shifts = got[0].shape[1]
    smem = pl.BlockSpec(memory_space=pltpu.SMEM)
    vmem = pl.BlockSpec(memory_space=pltpu.VMEM)
    hbm = pl.BlockSpec(memory_space=pl.ANY)
    more = () if out is None else (out,)
    return pl.pallas_call(
        functools.partial(unpack_kernel, part, depth),
        out_shape=jax.ShapeDtypeStruct((touched, PER_TOUCH, shifts), jnp.float32),
        in_specs=[smem] * 2 + [vmem] * NEAR + [hbm] * len(more),
        out_specs=hbm,
        scratch_shapes=[
            pltpu.VMEM((NEAR * depth, PER_TOUCH, shifts), jnp.float32),
            pltpu.SemaphoreType.DMA((NEAR * depth,)),
        ],
        input_output_aliases={2 + NEAR: 0} if more else {},
        compiler_params=pltpu.CompilerParams(vmem_limit_bytes=VMEM_LIMIT),
        cost_estimate=pl.CostEstimate(
            flops=0, bytes_accessed=NEAR * got[0].size * 6, transcendentals=0
        ),
        name=f"unpack_{part}",
    )(me, table, *got, *more)


def local(spectra, library, cand_block, cand_local):
    devices = lax.axis_size("lib")
    num_query, num_bins = spectra.shape
    touches, per_touch = cand_local.shape[1], cand_local.shape[2]
    depth = rounded(depth_of(num_query, touches, devices), 2)
    blocks = num_bins // LANES
    records = rounded(devices * (rounded(depth, ROW_SLOTS) // ROW_SLOTS), 16)
    me = lax.axis_index("lib").astype(jnp.int32).reshape(1)

    def across(value, distance):
        if distance == 0:
            return value
        pairs = [(i, i ^ distance) for i in range(devices)]
        return lax.ppermute(value, "lib", pairs)

    shard, table = prepare(
        spectra, cand_block, cand_local.reshape(-1, per_touch), depth, records
    )
    far = devices // NEAR
    order = [0] + list(range(far - 1, 0, -1))
    heads = {part: across(shard, NEAR * part) for part in order}
    shards = {
        part: [across(heads[part], e) for e in range(NEAR)] for part in order
    }
    rows = library.reshape(-1, blocks, LANES)
    got = {}
    for part in order:
        answers = profile(part, depth, num_query, touches, me, shards[part], rows)
        got[part] = [across(answers[e], NEAR * part + e) for e in range(NEAR)]
    out = None
    for part in order:
        out = unpack(part, depth, num_query * touches, me, table, got[part], out)
    return out.reshape(num_query, touches * per_touch, SHIFTS)


def solution(mesh):
    placed = (
        P(("groups", "lib"), None),
        P("lib", None),
        P(("groups", "lib"), None),
        P(("groups", "lib"), None, None),
    )
    return jax.shard_map(
        local,
        mesh=mesh,
        in_specs=placed,
        out_specs=P(("groups", "lib"), None, None),
        check_vma=False,
    )
```

```python
import functools

import jax
import jax.numpy as jnp
from jax import lax
from jax.experimental import pallas as pl
from jax.experimental.pallas import tpu as pltpu
from jax.sharding import PartitionSpec as P

SHIFTS = 1024
BG = 32
EPSILON = 1e-06
LANES = 128
VMEM_LIMIT = 48 * 1024 * 1024
NEAR = 4
ROW_SLOTS = 4
SLOT_LANES = LANES // ROW_SLOTS
PER_TOUCH = 8
GROUPS = 4
WIDTH = LANES // GROUPS


def rounded(value, unit):
    return -(-value // unit) * unit


def depth_of(num_query, touches, devices):
    return min(num_query, max(3, 3 * num_query * touches // (2 * devices)))


def record_values(found):
    lane = lax.broadcasted_iota(jnp.int32, found.shape, 1) % SLOT_LANES
    low = pltpu.roll(found, LANES - PER_TOUCH, 1)
    return jnp.where(lane < PER_TOUCH, found * 16 + low, found).astype(jnp.int32)


def prepare_kernel(depth, spectra_ref, named_ref, wanted_ref, out_ref, table_ref, rows_ref):
    num_query, num_bins = spectra_ref.shape
    blocks = num_bins // LANES
    values = spectra_ref[...].astype(jnp.float32)
    zeros = jnp.zeros((num_query, LANES), jnp.float32)
    wide = jnp.concatenate([values, zeros], axis=1)
    total, length = wide, 1
    while length < 2 * BG:
        total = total + pltpu.roll(total, length, 1)
        length *= 2
    total = total + pltpu.roll(wide, length, 1)
    total = pltpu.roll(total, total.shape[1] - BG, 1)[:, :num_bins]
    centered = values - total / (2 * BG + 1)
    factor = lax.rsqrt(jnp.mean(centered * centered, axis=1, keepdims=True) + EPSILON)
    prepared = (centered * factor).astype(jnp.bfloat16)
    row = lax.broadcasted_iota(jnp.int32, (LANES, LANES), 0)
    col = lax.broadcasted_iota(jnp.int32, (LANES, LANES), 1)
    flip = jnp.where(row + col == LANES - 1, 1.0, 0.0).astype(jnp.bfloat16)
    for block in range(blocks):
        piece = prepared[:, block * LANES : (block + 1) * LANES]
        turned = jnp.dot(piece, flip, preferred_element_type=jnp.float32)
        rows_ref[pl.ds(blocks - 1 - block, num_query, stride=blocks), :] = turned
    out_ref[0 : num_query * blocks, :] = rows_ref[...].astype(jnp.bfloat16)

    touches = named_ref.shape[1]
    touched = num_query * touches
    records = table_ref.shape[0]
    per_block = rounded(depth, ROW_SLOTS) // ROW_SLOTS
    touch = lax.broadcasted_iota(jnp.int32, (touched, num_query), 0)
    query = lax.broadcasted_iota(jnp.int32, (touched, num_query), 1)
    owner = jnp.where(touch // touches == query, 1.0, 0.0).astype(jnp.bfloat16)
    named = named_ref[...].astype(jnp.float32).astype(jnp.bfloat16)
    spread = jnp.dot(owner, named, preferred_element_type=jnp.float32)
    touch = lax.broadcasted_iota(jnp.int32, (touched, touches), 0)
    which = lax.broadcasted_iota(jnp.int32, (touched, touches), 1)
    block_col = jnp.sum(
        jnp.where(touch % touches == which, spread, 0.0), axis=1, keepdims=True
    )
    row = lax.broadcasted_iota(jnp.int32, (touched, touched), 0)
    col = lax.broadcasted_iota(jnp.int32, (touched, touched), 1)
    block_row = jnp.sum(jnp.where(row == col, block_col, 0.0), axis=0, keepdims=True)
    earlier = (block_col == block_row) & (row < col)
    rank = jnp.sum(jnp.where(earlier, 1.0, 0.0), axis=0, keepdims=True).astype(jnp.int32)
    place = block_row.astype(jnp.int32) * per_block + rank // ROW_SLOTS
    wanted = wanted_ref[...]
    high = (wanted // 16).astype(jnp.float32).astype(jnp.bfloat16)
    low = (wanted % 16).astype(jnp.float32).astype(jnp.bfloat16)
    unit = lax.broadcasted_iota(jnp.int32, (PER_TOUCH, LANES), 0)
    lane = lax.broadcasted_iota(jnp.int32, (PER_TOUCH, LANES), 1)
    row = lax.broadcasted_iota(jnp.int32, (records, touched), 0)
    touch = lax.broadcasted_iota(jnp.int32, (touched, LANES), 0)
    wide_lane = lax.broadcasted_iota(jnp.int32, (touched, LANES), 1)
    found = jnp.zeros((records, LANES), jnp.float32)
    for group in range(ROW_SLOTS):
        start = group * SLOT_LANES
        to_high = jnp.where(lane == start + unit, 1.0, 0.0).astype(jnp.bfloat16)
        to_low = jnp.where(lane == start + PER_TOUCH + unit, 1.0, 0.0).astype(jnp.bfloat16)
        data = jnp.dot(high, to_high, preferred_element_type=jnp.float32)
        data = data + jnp.dot(low, to_low, preferred_element_type=jnp.float32)
        data = jnp.where(
            wide_lane == start + 2 * PER_TOUCH, (touch + 1).astype(jnp.float32), data
        ).astype(jnp.bfloat16)
        pick = jnp.where((row == place) & (rank % ROW_SLOTS == group), 1.0, 0.0)
        found = found + jnp.dot(
            pick.astype(jnp.bfloat16), data, preferred_element_type=jnp.float32
        )
    out_ref[num_query * blocks :, :] = found.astype(jnp.bfloat16)
    table_ref[...] = record_values(found)


def prepare(spectra, named, wanted, depth, records):
    num_query, num_bins = spectra.shape
    rows = num_query * num_bins // LANES
    return pl.pallas_call(
        functools.partial(prepare_kernel, depth),
        out_shape=(
            jax.ShapeDtypeStruct((rows + records, LANES), jnp.bfloat16),
            jax.ShapeDtypeStruct((records, LANES), jnp.int32),
        ),
        scratch_shapes=[pltpu.VMEM((rows, LANES), jnp.float32)],
        compiler_params=pltpu.CompilerParams(vmem_limit_bytes=VMEM_LIMIT),
        name="prepare",
    )(spectra, named, wanted)


def profile_kernel(depth, num_query, touches, me_ref, *refs):
    shards, library_ref, refs = refs[:NEAR], refs[NEAR], refs[NEAR + 1 :]
    outs, refs = refs[:NEAR], refs[NEAR:]
    (
        query_ref, record_ref, found_ref, table_ref, answer_ref,
        cand_ref, packed_ref, spectrum_ref, left_ref, right_ref, product_ref, scale_ref,
        total_ref, sem_ref,
    ) = refs
    per_touch = PER_TOUCH
    rows = 2 * per_touch
    blocks = library_ref.shape[1]
    offsets = SHIFTS // LANES
    first = offsets // 2 + 1
    tiles = blocks // GROUPS
    query_rows = num_query * blocks
    per_block = rounded(depth, ROW_SLOTS) // ROW_SLOTS
    row = lax.broadcasted_iota(jnp.int32, (8, LANES), 0)
    lane = lax.broadcasted_iota(jnp.int32, (8, LANES), 1)
    lane16 = lax.broadcasted_iota(jnp.int32, (rows, LANES), 1)

    copies = [
        pltpu.make_async_copy(shards[e], query_ref.at[e], sem_ref.at[e]) for e in range(NEAR)
    ]
    for copy in copies:
        copy.start()
    cand_ref[...] = jnp.zeros(cand_ref.shape, cand_ref.dtype)
    right_ref[...] = jnp.zeros(right_ref.shape, right_ref.dtype)
    found_ref[...] = jnp.zeros(found_ref.shape, found_ref.dtype)
    for e in range(NEAR):
        copies[e].wait()
        record_ref[...] = query_ref[e, query_rows:, :].astype(jnp.float32)
        found_ref[e * per_block : (e + 1) * per_block, :] = record_values(
            record_ref[pl.ds(me_ref[0] * per_block, per_block), :]
        )
    to_scalars = pltpu.make_async_copy(found_ref, table_ref, sem_ref.at[NEAR])
    to_scalars.start()
    to_scalars.wait()

    def entry(slot):
        e = slot // depth
        s = slot % depth
        return e, e * per_block + s // ROW_SLOTS, s % ROW_SLOTS * SLOT_LANES

    def touch_of(slot):
        _, line, start = entry(slot)
        return table_ref[line, start + 2 * per_touch] - 1

    def choose(pieces):
        value = pieces[0]
        for group in range(1, GROUPS):
            value = jnp.where(lane16 < group * WIDTH, value, pieces[group])
        return value

    def gather(slot, half):
        _, line, start = entry(slot)
        for k in range(per_touch):
            wanted = table_ref[line, start + k]
            start_row = first * rows + half * per_touch + k
            cand_ref[pl.ds(start_row, blocks, stride=rows), :] = library_ref[wanted].astype(
                jnp.float32
            )
        square = jnp.zeros((per_touch, LANES), jnp.float32)
        for b in range(blocks):
            at = pl.multiple_of((first + b) * rows + half * per_touch, per_touch)
            piece = cand_ref[pl.ds(at, per_touch), :]
            square = square + piece * piece
        mean = jnp.sum(square, axis=1, keepdims=True) / (blocks * LANES)
        scale_ref[half] = jnp.broadcast_to(
            lax.rsqrt(mean + EPSILON), (per_touch, LANES)
        )

    def make_left():
        for b in range(blocks + offsets + 1):
            packed_ref[pl.ds(rows * b, rows), :] = cand_ref[pl.ds(rows * b, rows), :].astype(
                jnp.bfloat16
            )
        for t in range(tiles + offsets + 1):
            given = [packed_ref[pl.ds(rows * (t + tiles * g), rows), :] for g in range(GROUPS)]
            turned = []
            for c in range(GROUPS):
                mixed = choose([given[(a + c) % GROUPS] for a in range(GROUPS)])
                turned.append(pltpu.roll(mixed, WIDTH * c, 1) if c else mixed)
            for a in range(GROUPS):
                left_ref[a, pl.ds(rows * t, rows), :] = choose(
                    [turned[(g - a) % GROUPS] for g in range(GROUPS)]
                )

    def make_right(slot, half):
        query = jnp.maximum(touch_of(slot), 0) // touches
        spectrum_ref[half] = query_ref[
            entry(slot)[0], pl.ds(pl.multiple_of(query * blocks, blocks), blocks), :
        ].astype(jnp.float32)
        zero = jnp.zeros((8, LANES), jnp.float32)
        before = (zero, zero)
        before_shifted = jnp.zeros((16, LANES), jnp.bfloat16)
        columns = pl.ds(pl.multiple_of(half * LANES, LANES), LANES)
        for b in range(blocks + 1):
            if b < blocks:
                wide = jnp.broadcast_to(spectrum_ref[half, pl.ds(b, 1), :], (8, LANES))
                now = tuple(
                    pltpu.roll(wide, 1 + 8 * h, 1, stride=1, stride_axis=0) for h in range(2)
                )
            else:
                now = (zero, zero)
            shifted = jnp.concatenate(
                [jnp.where(lane > row + 8 * h, now[h], before[h]) for h in range(2)], axis=0
            ).astype(jnp.bfloat16)
            j = blocks - 1 - b
            place = 0 if j < 0 else (j % tiles + 1) * LANES + j // tiles * WIDTH
            right_ref[pl.ds(place, 16), columns] = shifted
            for c in range(16, WIDTH, 16):
                right_ref[pl.ds(place + c, 16), columns] = pltpu.roll(
                    jnp.where(lane16 < LANES - c, shifted, before_shifted), c, 1
                )
            before, before_shifted = now, shifted

    slots = NEAR * depth
    height = (offsets + 1) * rows

    @pl.loop(0, slots // 2)
    def _(pair):
        @pl.when((touch_of(2 * pair) >= 0) | (touch_of(2 * pair + 1) >= 0))
        def _():
            @pl.loop(0, 2)
            def _(half):
                gather(2 * pair + half, half)

            make_left()

            @pl.loop(0, 2)
            def _(half):
                make_right(2 * pair + half, half)

            @pl.loop(0, GROUPS)
            def _(a):
                left = jnp.concatenate(
                    [left_ref[a, pl.ds(rows * t, height), :] for t in range(tiles + 1)], axis=1
                )
                product_ref[a] = jnp.dot(
                    left, right_ref[...], preferred_element_type=jnp.float32
                )

            @pl.loop(0, 2)
            def _(half):
                columns = pl.ds(pl.multiple_of(half * LANES, LANES), LANES)

                def found(a, o):
                    at = pl.multiple_of(o * rows + half * per_touch, per_touch)
                    return product_ref[a, pl.ds(at, per_touch), columns]

                for o in range(offsets):
                    total = found(0, o + 1)
                    for a in range(1, GROUPS):
                        shift = WIDTH * a
                        total = total + pltpu.roll(
                            jnp.where(lane < LANES - shift, found(a, o + 1), found(a, o)),
                            shift,
                            1,
                        )
                    total_ref[half, :, o * LANES : (o + 1) * LANES] = total * scale_ref[half]

            answer_ref[pl.ds(pl.multiple_of(16 * pair, 16), 16), :] = total_ref[...].reshape(
                rows, SHIFTS
            ).astype(jnp.bfloat16)

    back = [
        pltpu.make_async_copy(
            answer_ref.at[pl.ds(e * depth * per_touch, depth * per_touch), :],
            outs[e],
            sem_ref.at[e],
        )
        for e in range(NEAR)
    ]
    for copy in back:
        copy.start()
    for copy in back:
        copy.wait()


def profile(part, depth, num_query, touches, me, shards, library):
    blocks = library.shape[1]
    offsets = SHIFTS // LANES
    tiles = blocks // GROUPS
    records = shards[0].shape[0] - num_query * blocks
    per_block = rounded(depth, ROW_SLOTS) // ROW_SLOTS
    table = (rounded(NEAR * per_block, 8), LANES)
    smem = pl.BlockSpec(memory_space=pltpu.SMEM)
    vmem = pl.BlockSpec(memory_space=pltpu.VMEM)
    hbm = pl.BlockSpec(memory_space=pl.ANY)
    answers = NEAR * depth * PER_TOUCH
    flops = answers * 2 * (offsets + 1) * (blocks + 4) * LANES * LANES
    return pl.pallas_call(
        functools.partial(profile_kernel, depth, num_query, touches),
        out_shape=[
            jax.ShapeDtypeStruct((depth * PER_TOUCH, SHIFTS), jnp.bfloat16)
            for _ in range(NEAR)
        ],
        in_specs=[smem] + [hbm] * NEAR + [vmem],
        out_specs=[hbm] * NEAR,
        scratch_shapes=[
            pltpu.VMEM((NEAR, *shards[0].shape), jnp.bfloat16),
            pltpu.VMEM((records, LANES), jnp.float32),
            pltpu.VMEM(table, jnp.int32),
            pltpu.SMEM(table, jnp.int32),
            pltpu.VMEM((answers, SHIFTS), jnp.bfloat16),
            pltpu.VMEM(((blocks + offsets + 1) * 16, LANES), jnp.float32),
            pltpu.VMEM(((blocks + offsets + 1) * 16, LANES), jnp.bfloat16),
            pltpu.VMEM((2, blocks, LANES), jnp.float32),
            pltpu.VMEM((GROUPS, (tiles + offsets + 1) * 16, LANES), jnp.bfloat16),
            pltpu.VMEM(((tiles + 1) * LANES, 2 * LANES), jnp.bfloat16),
            pltpu.VMEM((GROUPS, (offsets + 1) * 16, 2 * LANES), jnp.float32),
            pltpu.VMEM((2, PER_TOUCH, LANES), jnp.float32),
            pltpu.VMEM((2, PER_TOUCH, SHIFTS), jnp.float32),
            pltpu.SemaphoreType.DMA((NEAR + 1,)),
        ],
        compiler_params=pltpu.CompilerParams(vmem_limit_bytes=VMEM_LIMIT),
        cost_estimate=pl.CostEstimate(
            flops=8 * flops, bytes_accessed=8 * 1024 * 1024, transcendentals=0
        ),
        name=f"profile_{part}",
    )(me, *shards, library)


def unpack_kernel(part, depth, me_ref, table_ref, *refs):
    got, refs = refs[:NEAR], refs[-3:]
    out_ref, stage_ref, sem_ref = refs
    per_block = rounded(depth, ROW_SLOTS) // ROW_SLOTS

    def copy(slot, touch):
        return pltpu.make_async_copy(stage_ref.at[slot], out_ref.at[touch], sem_ref.at[slot])

    def touch_of(e, s):
        block = jnp.bitwise_xor(me_ref[0], NEAR * part + e)
        line = block * per_block + s // ROW_SLOTS
        return table_ref[line, s % ROW_SLOTS * SLOT_LANES + 2 * PER_TOUCH] - 1

    for e in range(NEAR):
        for s in range(depth):
            touch = touch_of(e, s)
            slot = e * depth + s

            @pl.when(touch >= 0)
            def _():
                stage_ref[slot] = got[e][s * PER_TOUCH : (s + 1) * PER_TOUCH, :].astype(
                    jnp.float32
                )
                copy(slot, touch).start()

    for e in range(NEAR):
        for s in range(depth):
            touch = touch_of(e, s)

            @pl.when(touch >= 0)
            def _():
                copy(e * depth + s, touch).wait()


def unpack(part, depth, touched, me, table, got, out):
    shifts = got[0].shape[1]
    smem = pl.BlockSpec(memory_space=pltpu.SMEM)
    vmem = pl.BlockSpec(memory_space=pltpu.VMEM)
    hbm = pl.BlockSpec(memory_space=pl.ANY)
    more = () if out is None else (out,)
    return pl.pallas_call(
        functools.partial(unpack_kernel, part, depth),
        out_shape=jax.ShapeDtypeStruct((touched, PER_TOUCH, shifts), jnp.float32),
        in_specs=[smem] * 2 + [vmem] * NEAR + [hbm] * len(more),
        out_specs=hbm,
        scratch_shapes=[
            pltpu.VMEM((NEAR * depth, PER_TOUCH, shifts), jnp.float32),
            pltpu.SemaphoreType.DMA((NEAR * depth,)),
        ],
        input_output_aliases={2 + NEAR: 0} if more else {},
        compiler_params=pltpu.CompilerParams(vmem_limit_bytes=VMEM_LIMIT),
        cost_estimate=pl.CostEstimate(
            flops=0, bytes_accessed=NEAR * got[0].size * 6, transcendentals=0
        ),
        name=f"unpack_{part}",
    )(me, table, *got, *more)


def local(spectra, library, cand_block, cand_local):
    devices = lax.axis_size("lib")
    num_query, num_bins = spectra.shape
    touches, per_touch = cand_local.shape[1], cand_local.shape[2]
    depth = rounded(depth_of(num_query, touches, devices), 2)
    blocks = num_bins // LANES
    records = rounded(devices * (rounded(depth, ROW_SLOTS) // ROW_SLOTS), 16)
    me = lax.axis_index("lib").astype(jnp.int32).reshape(1)

    def across(value, distance):
        if distance == 0:
            return value
        pairs = [(i, i ^ distance) for i in range(devices)]
        return lax.ppermute(value, "lib", pairs)

    shard, table = prepare(
        spectra, cand_block, cand_local.reshape(-1, per_touch), depth, records
    )
    far = devices // NEAR
    order = [0] + list(range(far - 1, 0, -1))
    heads = {part: across(shard, NEAR * part) for part in order}
    shards = {
        part: [across(heads[part], e) for e in range(NEAR)] for part in order
    }
    rows = library.reshape(-1, blocks, LANES)
    got = {}
    for part in order:
        answers = profile(part, depth, num_query, touches, me, shards[part], rows)
        got[part] = [across(answers[e], NEAR * part + e) for e in range(NEAR)]
    out = None
    for part in order:
        out = unpack(part, depth, num_query * touches, me, table, got[part], out)
    return out.reshape(num_query, touches * per_touch, SHIFTS)


def solution(mesh):
    placed = (
        P(("groups", "lib"), None),
        P("lib", None),
        P(("groups", "lib"), None),
        P(("groups", "lib"), None, None),
    )
    return jax.shard_map(
        local,
        mesh=mesh,
        in_specs=placed,
        out_specs=P(("groups", "lib"), None, None),
        check_vma=False,
    )
```

```python
import functools

import jax
import jax.numpy as jnp
from jax import lax
from jax.experimental import pallas as pl
from jax.experimental.pallas import tpu as pltpu
from jax.sharding import PartitionSpec as P

SHIFTS = 1024
BG = 32
EPSILON = 1e-06
LANES = 128
VMEM_LIMIT = 48 * 1024 * 1024
NEAR = 4
ROW_SLOTS = 4
SLOT_LANES = LANES // ROW_SLOTS
PER_TOUCH = 8
CHAINS = 1
GROUPS = 4
WIDTH = LANES // GROUPS


def rounded(value, unit):
    return -(-value // unit) * unit


def depth_of(num_query, touches, devices):
    return min(num_query, max(3, 3 * num_query * touches // (2 * devices)))


def record_values(found):
    lane = lax.broadcasted_iota(jnp.int32, found.shape, 1) % SLOT_LANES
    low = pltpu.roll(found, LANES - PER_TOUCH, 1)
    return jnp.where(lane < PER_TOUCH, found * 16 + low, found).astype(jnp.int32)


def prepare_kernel(depth, spectra_ref, named_ref, wanted_ref, out_ref, table_ref, rows_ref):
    num_query, num_bins = spectra_ref.shape
    blocks = num_bins // LANES
    values = spectra_ref[...].astype(jnp.float32)
    zeros = jnp.zeros((num_query, LANES), jnp.float32)
    wide = jnp.concatenate([values, zeros], axis=1)
    total, length = wide, 1
    while length < 2 * BG:
        total = total + pltpu.roll(total, length, 1)
        length *= 2
    total = total + pltpu.roll(wide, length, 1)
    total = pltpu.roll(total, total.shape[1] - BG, 1)[:, :num_bins]
    centered = values - total / (2 * BG + 1)
    factor = lax.rsqrt(jnp.mean(centered * centered, axis=1, keepdims=True) + EPSILON)
    prepared = (centered * factor).astype(jnp.bfloat16)
    row = lax.broadcasted_iota(jnp.int32, (LANES, LANES), 0)
    col = lax.broadcasted_iota(jnp.int32, (LANES, LANES), 1)
    flip = jnp.where(row + col == LANES - 1, 1.0, 0.0).astype(jnp.bfloat16)
    for block in range(blocks):
        piece = prepared[:, block * LANES : (block + 1) * LANES]
        turned = jnp.dot(piece, flip, preferred_element_type=jnp.float32)
        rows_ref[pl.ds(blocks - 1 - block, num_query, stride=blocks), :] = turned
    out_ref[0 : num_query * blocks, :] = rows_ref[...].astype(jnp.bfloat16)

    touches = named_ref.shape[1]
    touched = num_query * touches
    records = table_ref.shape[0]
    per_block = rounded(depth, ROW_SLOTS) // ROW_SLOTS
    touch = lax.broadcasted_iota(jnp.int32, (touched, num_query), 0)
    query = lax.broadcasted_iota(jnp.int32, (touched, num_query), 1)
    owner = jnp.where(touch // touches == query, 1.0, 0.0).astype(jnp.bfloat16)
    named = named_ref[...].astype(jnp.float32).astype(jnp.bfloat16)
    spread = jnp.dot(owner, named, preferred_element_type=jnp.float32)
    touch = lax.broadcasted_iota(jnp.int32, (touched, touches), 0)
    which = lax.broadcasted_iota(jnp.int32, (touched, touches), 1)
    block_col = jnp.sum(
        jnp.where(touch % touches == which, spread, 0.0), axis=1, keepdims=True
    )
    row = lax.broadcasted_iota(jnp.int32, (touched, touched), 0)
    col = lax.broadcasted_iota(jnp.int32, (touched, touched), 1)
    block_row = jnp.sum(jnp.where(row == col, block_col, 0.0), axis=0, keepdims=True)
    earlier = (block_col == block_row) & (row < col)
    rank = jnp.sum(jnp.where(earlier, 1.0, 0.0), axis=0, keepdims=True).astype(jnp.int32)
    place = block_row.astype(jnp.int32) * per_block + rank // ROW_SLOTS
    wanted = wanted_ref[...]
    high = (wanted // 16).astype(jnp.float32).astype(jnp.bfloat16)
    low = (wanted % 16).astype(jnp.float32).astype(jnp.bfloat16)
    unit = lax.broadcasted_iota(jnp.int32, (PER_TOUCH, LANES), 0)
    lane = lax.broadcasted_iota(jnp.int32, (PER_TOUCH, LANES), 1)
    row = lax.broadcasted_iota(jnp.int32, (records, touched), 0)
    touch = lax.broadcasted_iota(jnp.int32, (touched, LANES), 0)
    wide_lane = lax.broadcasted_iota(jnp.int32, (touched, LANES), 1)
    found = jnp.zeros((records, LANES), jnp.float32)
    for group in range(ROW_SLOTS):
        start = group * SLOT_LANES
        to_high = jnp.where(lane == start + unit, 1.0, 0.0).astype(jnp.bfloat16)
        to_low = jnp.where(lane == start + PER_TOUCH + unit, 1.0, 0.0).astype(jnp.bfloat16)
        data = jnp.dot(high, to_high, preferred_element_type=jnp.float32)
        data = data + jnp.dot(low, to_low, preferred_element_type=jnp.float32)
        data = jnp.where(
            wide_lane == start + 2 * PER_TOUCH, (touch + 1).astype(jnp.float32), data
        ).astype(jnp.bfloat16)
        pick = jnp.where((row == place) & (rank % ROW_SLOTS == group), 1.0, 0.0)
        found = found + jnp.dot(
            pick.astype(jnp.bfloat16), data, preferred_element_type=jnp.float32
        )
    out_ref[num_query * blocks :, :] = found.astype(jnp.bfloat16)
    table_ref[...] = record_values(found)


def prepare(spectra, named, wanted, depth, records):
    num_query, num_bins = spectra.shape
    rows = num_query * num_bins // LANES
    return pl.pallas_call(
        functools.partial(prepare_kernel, depth),
        out_shape=(
            jax.ShapeDtypeStruct((rows + records, LANES), jnp.bfloat16),
            jax.ShapeDtypeStruct((records, LANES), jnp.int32),
        ),
        scratch_shapes=[pltpu.VMEM((rows, LANES), jnp.float32)],
        compiler_params=pltpu.CompilerParams(vmem_limit_bytes=VMEM_LIMIT),
        name="prepare",
    )(spectra, named, wanted)


def profile_kernel(depth, num_query, touches, me_ref, *refs):
    shards, library_ref, refs = refs[:NEAR], refs[NEAR], refs[NEAR + 1 :]
    outs, refs = refs[:NEAR], refs[NEAR:]
    (
        query_ref, record_ref, found_ref, table_ref, answer_ref,
        cand_ref, packed_ref, spectrum_ref, left_ref, right_ref, product_ref, sem_ref,
    ) = refs
    per_touch = PER_TOUCH
    rows = 2 * per_touch
    blocks = library_ref.shape[1]
    offsets = SHIFTS // LANES
    first = offsets // 2 + 1
    tiles = blocks // GROUPS
    query_rows = num_query * blocks
    per_block = rounded(depth, ROW_SLOTS) // ROW_SLOTS
    row = lax.broadcasted_iota(jnp.int32, (8, LANES), 0)
    lane = lax.broadcasted_iota(jnp.int32, (8, LANES), 1)
    lane16 = lax.broadcasted_iota(jnp.int32, (rows, LANES), 1)

    copies = [
        pltpu.make_async_copy(shards[e], query_ref.at[e], sem_ref.at[e]) for e in range(NEAR)
    ]
    for copy in copies:
        copy.start()
    cand_ref[...] = jnp.zeros(cand_ref.shape, cand_ref.dtype)
    right_ref[...] = jnp.zeros(right_ref.shape, right_ref.dtype)
    found_ref[...] = jnp.zeros(found_ref.shape, found_ref.dtype)
    for e in range(NEAR):
        copies[e].wait()
        record_ref[...] = query_ref[e, query_rows:, :].astype(jnp.float32)
        found_ref[e * per_block : (e + 1) * per_block, :] = record_values(
            record_ref[pl.ds(me_ref[0] * per_block, per_block), :]
        )
    to_scalars = pltpu.make_async_copy(found_ref, table_ref, sem_ref.at[NEAR])
    to_scalars.start()
    to_scalars.wait()

    def entry(slot):
        e = slot // depth
        s = slot % depth
        return e, e * per_block + s // ROW_SLOTS, s % ROW_SLOTS * SLOT_LANES

    def touch_of(slot):
        _, line, start = entry(slot)
        return table_ref[line, start + 2 * per_touch] - 1

    def choose(pieces):
        value = pieces[0]
        for group in range(1, GROUPS):
            value = jnp.where(lane16 < group * WIDTH, value, pieces[group])
        return value

    def gather(slot, half):
        _, line, start = entry(slot)
        for k in range(per_touch):
            wanted = table_ref[line, start + k]
            cand_ref[pl.ds(first * rows + half * per_touch + k, blocks, stride=rows), :] = (
                library_ref[wanted].astype(jnp.float32)
            )
        square = jnp.zeros((per_touch, LANES), jnp.float32)
        for b in range(blocks):
            piece = cand_ref[pl.ds((first + b) * rows + half * per_touch, per_touch), :]
            square = square + piece * piece
        mean = jnp.sum(square, axis=1, keepdims=True) / (blocks * LANES)
        return lax.rsqrt(mean + EPSILON)

    def make_left():
        for b in range(blocks + offsets + 1):
            packed_ref[pl.ds(rows * b, rows), :] = cand_ref[pl.ds(rows * b, rows), :].astype(
                jnp.bfloat16
            )
        for t in range(tiles + offsets + 1):
            given = [packed_ref[pl.ds(rows * (t + tiles * g), rows), :] for g in range(GROUPS)]
            turned = []
            for c in range(GROUPS):
                mixed = choose([given[(a + c) % GROUPS] for a in range(GROUPS)])
                turned.append(pltpu.roll(mixed, WIDTH * c, 1) if c else mixed)
            for a in range(GROUPS):
                left_ref[a, pl.ds(rows * t, rows), :] = choose(
                    [turned[(g - a) % GROUPS] for g in range(GROUPS)]
                )

    def make_right(slot, half):
        query = jnp.maximum(touch_of(slot), 0) // touches
        spectrum_ref[half] = query_ref[
            entry(slot)[0], pl.ds(pl.multiple_of(query * blocks, blocks), blocks), :
        ].astype(jnp.float32)
        zero = jnp.zeros((8, LANES), jnp.float32)
        before = (zero, zero)
        before_shifted = jnp.zeros((16, LANES), jnp.bfloat16)
        columns = slice(half * LANES, (half + 1) * LANES)
        for b in range(blocks + 1):
            if b < blocks:
                wide = jnp.broadcast_to(spectrum_ref[half, pl.ds(b, 1), :], (8, LANES))
                now = tuple(
                    pltpu.roll(wide, 1 + 8 * h, 1, stride=1, stride_axis=0) for h in range(2)
                )
            else:
                now = (zero, zero)
            shifted = jnp.concatenate(
                [jnp.where(lane > row + 8 * h, now[h], before[h]) for h in range(2)], axis=0
            ).astype(jnp.bfloat16)
            j = blocks - 1 - b
            place = 0 if j < 0 else (j % tiles + 1) * LANES + j // tiles * WIDTH
            right_ref[pl.ds(place, 16), columns] = shifted
            for c in range(16, WIDTH, 16):
                right_ref[pl.ds(place + c, 16), columns] = pltpu.roll(
                    jnp.where(lane16 < LANES - c, shifted, before_shifted), c, 1
                )
            before, before_shifted = now, shifted

    def sums(low, high):
        left = jnp.concatenate(
            [
                jnp.concatenate(
                    [
                        left_ref[a, pl.ds(rows * t, rows * (offsets + 1)), :]
                        for t in range(tiles + 1)
                    ],
                    axis=1,
                )
                for a in range(low, high)
            ],
            axis=0,
        )
        return jnp.dot(left, right_ref[...], preferred_element_type=jnp.float32)

    slots = NEAR * depth
    height = GROUPS // CHAINS * (offsets + 1) * rows

    @pl.loop(0, slots // 2)
    def _(pair):
        @pl.when((touch_of(2 * pair) >= 0) | (touch_of(2 * pair + 1) >= 0))
        def _():
            scales = [gather(2 * pair + half, half) for half in range(2)]
            make_left()
            for half in range(2):
                make_right(2 * pair + half, half)
            step = GROUPS // CHAINS
            for c in range(CHAINS):
                product_ref[c * height : (c + 1) * height, :] = sums(step * c, step * (c + 1))

            def found(a, o, half):
                at = (a * (offsets + 1) + o) * rows + half * per_touch
                return product_ref[at : at + per_touch, half * LANES : (half + 1) * LANES]

            for o in range(offsets):
                both = []
                for half in range(2):
                    total = found(0, o + 1, half)
                    for a in range(1, GROUPS):
                        shift = WIDTH * a
                        total = total + pltpu.roll(
                            jnp.where(
                                lane < LANES - shift, found(a, o + 1, half), found(a, o, half)
                            ),
                            shift,
                            1,
                        )
                    both.append(total * scales[half])
                answer_ref[
                    pl.ds(pl.multiple_of(16 * pair, 16), 16), o * LANES : (o + 1) * LANES
                ] = jnp.concatenate(both, axis=0).astype(jnp.bfloat16)

    back = [
        pltpu.make_async_copy(
            answer_ref.at[pl.ds(e * depth * per_touch, depth * per_touch), :],
            outs[e],
            sem_ref.at[e],
        )
        for e in range(NEAR)
    ]
    for copy in back:
        copy.start()
    for copy in back:
        copy.wait()


def profile(part, depth, num_query, touches, me, shards, library):
    blocks = library.shape[1]
    offsets = SHIFTS // LANES
    tiles = blocks // GROUPS
    records = shards[0].shape[0] - num_query * blocks
    per_block = rounded(depth, ROW_SLOTS) // ROW_SLOTS
    table = (rounded(NEAR * per_block, 8), LANES)
    smem = pl.BlockSpec(memory_space=pltpu.SMEM)
    vmem = pl.BlockSpec(memory_space=pltpu.VMEM)
    hbm = pl.BlockSpec(memory_space=pl.ANY)
    answers = NEAR * depth * PER_TOUCH
    flops = answers * 2 * (offsets + 1) * (blocks + 4) * LANES * LANES
    return pl.pallas_call(
        functools.partial(profile_kernel, depth, num_query, touches),
        out_shape=[
            jax.ShapeDtypeStruct((depth * PER_TOUCH, SHIFTS), jnp.bfloat16)
            for _ in range(NEAR)
        ],
        in_specs=[smem] + [hbm] * NEAR + [vmem],
        out_specs=[hbm] * NEAR,
        scratch_shapes=[
            pltpu.VMEM((NEAR, *shards[0].shape), jnp.bfloat16),
            pltpu.VMEM((records, LANES), jnp.float32),
            pltpu.VMEM(table, jnp.int32),
            pltpu.SMEM(table, jnp.int32),
            pltpu.VMEM((answers, SHIFTS), jnp.bfloat16),
            pltpu.VMEM(((blocks + offsets + 1) * 16, LANES), jnp.float32),
            pltpu.VMEM(((blocks + offsets + 1) * 16, LANES), jnp.bfloat16),
            pltpu.VMEM((2, blocks, LANES), jnp.float32),
            pltpu.VMEM((GROUPS, (tiles + offsets + 1) * 16, LANES), jnp.bfloat16),
            pltpu.VMEM(((tiles + 1) * LANES, 2 * LANES), jnp.bfloat16),
            pltpu.VMEM((GROUPS * (offsets + 1) * 16, 2 * LANES), jnp.float32),
            pltpu.SemaphoreType.DMA((NEAR + 1,)),
        ],
        compiler_params=pltpu.CompilerParams(vmem_limit_bytes=VMEM_LIMIT),
        cost_estimate=pl.CostEstimate(
            flops=8 * flops, bytes_accessed=8 * 1024 * 1024, transcendentals=0
        ),
        name=f"profile_{part}",
    )(me, *shards, library)


def unpack_kernel(part, depth, me_ref, table_ref, *refs):
    got, refs = refs[:NEAR], refs[-3:]
    out_ref, stage_ref, sem_ref = refs
    per_block = rounded(depth, ROW_SLOTS) // ROW_SLOTS

    def copy(slot, touch):
        return pltpu.make_async_copy(stage_ref.at[slot], out_ref.at[touch], sem_ref.at[slot])

    def touch_of(e, s):
        block = jnp.bitwise_xor(me_ref[0], NEAR * part + e)
        line = block * per_block + s // ROW_SLOTS
        return table_ref[line, s % ROW_SLOTS * SLOT_LANES + 2 * PER_TOUCH] - 1

    for e in range(NEAR):
        for s in range(depth):
            touch = touch_of(e, s)
            slot = e * depth + s

            @pl.when(touch >= 0)
            def _():
                stage_ref[slot] = got[e][s * PER_TOUCH : (s + 1) * PER_TOUCH, :].astype(
                    jnp.float32
                )
                copy(slot, touch).start()

    for e in range(NEAR):
        for s in range(depth):
            touch = touch_of(e, s)

            @pl.when(touch >= 0)
            def _():
                copy(e * depth + s, touch).wait()


def unpack(part, depth, touched, me, table, got, out):
    shifts = got[0].shape[1]
    smem = pl.BlockSpec(memory_space=pltpu.SMEM)
    vmem = pl.BlockSpec(memory_space=pltpu.VMEM)
    hbm = pl.BlockSpec(memory_space=pl.ANY)
    more = () if out is None else (out,)
    return pl.pallas_call(
        functools.partial(unpack_kernel, part, depth),
        out_shape=jax.ShapeDtypeStruct((touched, PER_TOUCH, shifts), jnp.float32),
        in_specs=[smem] * 2 + [vmem] * NEAR + [hbm] * len(more),
        out_specs=hbm,
        scratch_shapes=[
            pltpu.VMEM((NEAR * depth, PER_TOUCH, shifts), jnp.float32),
            pltpu.SemaphoreType.DMA((NEAR * depth,)),
        ],
        input_output_aliases={2 + NEAR: 0} if more else {},
        compiler_params=pltpu.CompilerParams(vmem_limit_bytes=VMEM_LIMIT),
        cost_estimate=pl.CostEstimate(
            flops=0, bytes_accessed=NEAR * got[0].size * 6, transcendentals=0
        ),
        name=f"unpack_{part}",
    )(me, table, *got, *more)


def local(spectra, library, cand_block, cand_local):
    devices = lax.axis_size("lib")
    num_query, num_bins = spectra.shape
    touches, per_touch = cand_local.shape[1], cand_local.shape[2]
    depth = rounded(depth_of(num_query, touches, devices), 2)
    blocks = num_bins // LANES
    records = rounded(devices * (rounded(depth, ROW_SLOTS) // ROW_SLOTS), 16)
    me = lax.axis_index("lib").astype(jnp.int32).reshape(1)

    def across(value, distance):
        if distance == 0:
            return value
        pairs = [(i, i ^ distance) for i in range(devices)]
        return lax.ppermute(value, "lib", pairs)

    shard, table = prepare(
        spectra, cand_block, cand_local.reshape(-1, per_touch), depth, records
    )
    far = devices // NEAR
    order = [0] + list(range(far - 1, 0, -1))
    heads = {part: across(shard, NEAR * part) for part in order}
    shards = {
        part: [across(heads[part], e) for e in range(NEAR)] for part in order
    }
    rows = library.reshape(-1, blocks, LANES)
    got = {}
    for part in order:
        answers = profile(part, depth, num_query, touches, me, shards[part], rows)
        got[part] = [across(answers[e], NEAR * part + e) for e in range(NEAR)]
    out = None
    for part in order:
        out = unpack(part, depth, num_query * touches, me, table, got[part], out)
    return out.reshape(num_query, touches * per_touch, SHIFTS)


def solution(mesh):
    placed = (
        P(("groups", "lib"), None),
        P("lib", None),
        P(("groups", "lib"), None),
        P(("groups", "lib"), None, None),
    )
    return jax.shard_map(
        local,
        mesh=mesh,
        in_specs=placed,
        out_specs=P(("groups", "lib"), None, None),
        check_vma=False,
    )
```

```python
import functools

import jax
import jax.numpy as jnp
from jax import lax
from jax.experimental import pallas as pl
from jax.experimental.pallas import tpu as pltpu
from jax.sharding import PartitionSpec as P

SHIFTS = 1024
BG = 32
EPSILON = 1e-06
LANES = 128
VMEM_LIMIT = 48 * 1024 * 1024
NEAR = 4
ROW_SLOTS = 4
SLOT_LANES = LANES // ROW_SLOTS
PER_TOUCH = 8
CHAINS = 1
GROUPS = 4
WIDTH = LANES // GROUPS


def rounded(value, unit):
    return -(-value // unit) * unit


def depth_of(num_query, touches, devices):
    return min(num_query, max(3, 3 * num_query * touches // (2 * devices)))


def record_values(found):
    lane = lax.broadcasted_iota(jnp.int32, found.shape, 1) % SLOT_LANES
    low = pltpu.roll(found, LANES - PER_TOUCH, 1)
    return jnp.where(lane < PER_TOUCH, found * 16 + low, found).astype(jnp.int32)


def prepare_kernel(depth, spectra_ref, named_ref, wanted_ref, out_ref, table_ref, rows_ref):
    num_query, num_bins = spectra_ref.shape
    blocks = num_bins // LANES
    values = spectra_ref[...].astype(jnp.float32)
    zeros = jnp.zeros((num_query, LANES), jnp.float32)
    wide = jnp.concatenate([values, zeros], axis=1)
    total, length = wide, 1
    while length < 2 * BG:
        total = total + pltpu.roll(total, length, 1)
        length *= 2
    total = total + pltpu.roll(wide, length, 1)
    total = pltpu.roll(total, total.shape[1] - BG, 1)[:, :num_bins]
    centered = values - total / (2 * BG + 1)
    factor = lax.rsqrt(jnp.mean(centered * centered, axis=1, keepdims=True) + EPSILON)
    prepared = (centered * factor).astype(jnp.bfloat16)
    row = lax.broadcasted_iota(jnp.int32, (LANES, LANES), 0)
    col = lax.broadcasted_iota(jnp.int32, (LANES, LANES), 1)
    flip = jnp.where(row + col == LANES - 1, 1.0, 0.0).astype(jnp.bfloat16)
    for block in range(blocks):
        piece = prepared[:, block * LANES : (block + 1) * LANES]
        turned = jnp.dot(piece, flip, preferred_element_type=jnp.float32)
        rows_ref[pl.ds(blocks - 1 - block, num_query, stride=blocks), :] = turned
    out_ref[0 : num_query * blocks, :] = rows_ref[...].astype(jnp.bfloat16)

    touches = named_ref.shape[1]
    touched = num_query * touches
    records = table_ref.shape[0]
    per_block = rounded(depth, ROW_SLOTS) // ROW_SLOTS
    touch = lax.broadcasted_iota(jnp.int32, (touched, num_query), 0)
    query = lax.broadcasted_iota(jnp.int32, (touched, num_query), 1)
    owner = jnp.where(touch // touches == query, 1.0, 0.0).astype(jnp.bfloat16)
    named = named_ref[...].astype(jnp.float32).astype(jnp.bfloat16)
    spread = jnp.dot(owner, named, preferred_element_type=jnp.float32)
    touch = lax.broadcasted_iota(jnp.int32, (touched, touches), 0)
    which = lax.broadcasted_iota(jnp.int32, (touched, touches), 1)
    block_col = jnp.sum(
        jnp.where(touch % touches == which, spread, 0.0), axis=1, keepdims=True
    )
    row = lax.broadcasted_iota(jnp.int32, (touched, touched), 0)
    col = lax.broadcasted_iota(jnp.int32, (touched, touched), 1)
    block_row = jnp.sum(jnp.where(row == col, block_col, 0.0), axis=0, keepdims=True)
    earlier = (block_col == block_row) & (row < col)
    rank = jnp.sum(jnp.where(earlier, 1.0, 0.0), axis=0, keepdims=True).astype(jnp.int32)
    place = block_row.astype(jnp.int32) * per_block + rank // ROW_SLOTS
    wanted = wanted_ref[...]
    high = (wanted // 16).astype(jnp.float32).astype(jnp.bfloat16)
    low = (wanted % 16).astype(jnp.float32).astype(jnp.bfloat16)
    unit = lax.broadcasted_iota(jnp.int32, (PER_TOUCH, LANES), 0)
    lane = lax.broadcasted_iota(jnp.int32, (PER_TOUCH, LANES), 1)
    row = lax.broadcasted_iota(jnp.int32, (records, touched), 0)
    touch = lax.broadcasted_iota(jnp.int32, (touched, LANES), 0)
    wide_lane = lax.broadcasted_iota(jnp.int32, (touched, LANES), 1)
    found = jnp.zeros((records, LANES), jnp.float32)
    for group in range(ROW_SLOTS):
        start = group * SLOT_LANES
        to_high = jnp.where(lane == start + unit, 1.0, 0.0).astype(jnp.bfloat16)
        to_low = jnp.where(lane == start + PER_TOUCH + unit, 1.0, 0.0).astype(jnp.bfloat16)
        data = jnp.dot(high, to_high, preferred_element_type=jnp.float32)
        data = data + jnp.dot(low, to_low, preferred_element_type=jnp.float32)
        data = jnp.where(
            wide_lane == start + 2 * PER_TOUCH, (touch + 1).astype(jnp.float32), data
        ).astype(jnp.bfloat16)
        pick = jnp.where((row == place) & (rank % ROW_SLOTS == group), 1.0, 0.0)
        found = found + jnp.dot(
            pick.astype(jnp.bfloat16), data, preferred_element_type=jnp.float32
        )
    out_ref[num_query * blocks :, :] = found.astype(jnp.bfloat16)
    table_ref[...] = record_values(found)


def prepare(spectra, named, wanted, depth, records):
    num_query, num_bins = spectra.shape
    rows = num_query * num_bins // LANES
    return pl.pallas_call(
        functools.partial(prepare_kernel, depth),
        out_shape=(
            jax.ShapeDtypeStruct((rows + records, LANES), jnp.bfloat16),
            jax.ShapeDtypeStruct((records, LANES), jnp.int32),
        ),
        scratch_shapes=[pltpu.VMEM((rows, LANES), jnp.float32)],
        compiler_params=pltpu.CompilerParams(vmem_limit_bytes=VMEM_LIMIT),
        name="prepare",
    )(spectra, named, wanted)


def profile_kernel(depth, num_query, touches, me_ref, *refs):
    shards, library_ref, refs = refs[:NEAR], refs[NEAR], refs[NEAR + 1 :]
    outs, refs = refs[:NEAR], refs[NEAR:]
    (
        query_ref, record_ref, found_ref, table_ref, answer_ref,
        cand_ref, packed_ref, spectrum_ref, left_ref, right_ref, product_ref, sem_ref,
    ) = refs
    per_touch = PER_TOUCH
    rows = 2 * per_touch
    blocks = library_ref.shape[1]
    offsets = SHIFTS // LANES
    first = offsets // 2 + 1
    tiles = blocks // GROUPS
    query_rows = num_query * blocks
    per_block = rounded(depth, ROW_SLOTS) // ROW_SLOTS
    row = lax.broadcasted_iota(jnp.int32, (8, LANES), 0)
    lane = lax.broadcasted_iota(jnp.int32, (8, LANES), 1)
    lane16 = lax.broadcasted_iota(jnp.int32, (rows, LANES), 1)

    copies = [
        pltpu.make_async_copy(shards[e], query_ref.at[e], sem_ref.at[e]) for e in range(NEAR)
    ]
    for copy in copies:
        copy.start()
    cand_ref[...] = jnp.zeros(cand_ref.shape, cand_ref.dtype)
    right_ref[...] = jnp.zeros(right_ref.shape, right_ref.dtype)
    found_ref[...] = jnp.zeros(found_ref.shape, found_ref.dtype)
    for e in range(NEAR):
        copies[e].wait()
        record_ref[...] = query_ref[e, query_rows:, :].astype(jnp.float32)
        found_ref[e * per_block : (e + 1) * per_block, :] = record_values(
            record_ref[pl.ds(me_ref[0] * per_block, per_block), :]
        )
    to_scalars = pltpu.make_async_copy(found_ref, table_ref, sem_ref.at[NEAR])
    to_scalars.start()
    to_scalars.wait()

    def entry(slot):
        e = slot // depth
        s = slot % depth
        return e, e * per_block + s // ROW_SLOTS, s % ROW_SLOTS * SLOT_LANES

    def touch_of(slot):
        _, line, start = entry(slot)
        return table_ref[line, start + 2 * per_touch] - 1

    def choose(pieces):
        value = pieces[0]
        for group in range(1, GROUPS):
            value = jnp.where(lane16 < group * WIDTH, value, pieces[group])
        return value

    def gather(slot, half):
        _, line, start = entry(slot)
        for k in range(per_touch):
            wanted = table_ref[line, start + k]
            cand_ref[pl.ds(first * rows + half * per_touch + k, blocks, stride=rows), :] = (
                library_ref[wanted].astype(jnp.float32)
            )
        square = jnp.zeros((per_touch, LANES), jnp.float32)
        for b in range(blocks):
            piece = cand_ref[pl.ds((first + b) * rows + half * per_touch, per_touch), :]
            square = square + piece * piece
        mean = jnp.sum(square, axis=1, keepdims=True) / (blocks * LANES)
        return lax.rsqrt(mean + EPSILON)

    def make_left():
        for b in range(blocks + offsets + 1):
            packed_ref[pl.ds(rows * b, rows), :] = cand_ref[pl.ds(rows * b, rows), :].astype(
                jnp.bfloat16
            )
        for t in range(tiles + offsets + 1):
            given = [packed_ref[pl.ds(rows * (t + tiles * g), rows), :] for g in range(GROUPS)]
            turned = []
            for c in range(GROUPS):
                mixed = choose([given[(a + c) % GROUPS] for a in range(GROUPS)])
                turned.append(pltpu.roll(mixed, WIDTH * c, 1) if c else mixed)
            for a in range(GROUPS):
                left_ref[a, pl.ds(rows * t, rows), :] = choose(
                    [turned[(g - a) % GROUPS] for g in range(GROUPS)]
                )

    def shifter(slot, half):
        query = jnp.maximum(touch_of(slot), 0) // touches
        spectrum_ref[half] = query_ref[
            entry(slot)[0], pl.ds(pl.multiple_of(query * blocks, blocks), blocks), :
        ].astype(jnp.float32)
        zero = jnp.zeros((8, LANES), jnp.float32)
        turned = {-1: (zero, zero), blocks: (zero, zero)}
        shifted = {-1: jnp.zeros((16, LANES), jnp.bfloat16)}

        def turned_of(b):
            if b not in turned:
                wide = jnp.broadcast_to(spectrum_ref[half, pl.ds(b, 1), :], (8, LANES))
                turned[b] = tuple(
                    pltpu.roll(wide, 1 + 8 * h, 1, stride=1, stride_axis=0) for h in range(2)
                )
            return turned[b]

        def shifted_of(b):
            if b not in shifted:
                now, before = turned_of(b), turned_of(b - 1)
                shifted[b] = jnp.concatenate(
                    [jnp.where(lane > row + 8 * h, now[h], before[h]) for h in range(2)], axis=0
                ).astype(jnp.bfloat16)
            return shifted[b]

        return shifted_of

    def make_right(slots):
        shifters = [shifter(slot, half) for half, slot in enumerate(slots)]
        for t in range(tiles + 1):
            for half in range(2):
                columns = slice(half * LANES, (half + 1) * LANES)
                for g in range(GROUPS if t else 1):
                    b = blocks - t - tiles * g
                    place = t * LANES + g * WIDTH
                    now, before = shifters[half](b), shifters[half](b - 1)
                    right_ref[pl.ds(place, 16), columns] = now
                    for c in range(16, WIDTH, 16):
                        right_ref[pl.ds(place + c, 16), columns] = pltpu.roll(
                            jnp.where(lane16 < LANES - c, now, before), c, 1
                        )

    def sums(low, high):
        left = jnp.concatenate(
            [
                jnp.concatenate(
                    [
                        left_ref[a, pl.ds(rows * t, rows * (offsets + 1)), :]
                        for t in range(tiles + 1)
                    ],
                    axis=1,
                )
                for a in range(low, high)
            ],
            axis=0,
        )
        return jnp.dot(left, right_ref[...], preferred_element_type=jnp.float32)

    slots = NEAR * depth
    height = GROUPS // CHAINS * (offsets + 1) * rows

    @pl.loop(0, slots // 2)
    def _(pair):
        @pl.when((touch_of(2 * pair) >= 0) | (touch_of(2 * pair + 1) >= 0))
        def _():
            scales = [gather(2 * pair + half, half) for half in range(2)]
            make_left()
            make_right([2 * pair, 2 * pair + 1])
            step = GROUPS // CHAINS
            for c in range(CHAINS):
                product_ref[c * height : (c + 1) * height, :] = sums(step * c, step * (c + 1))

            def found(a, o, half):
                at = (a * (offsets + 1) + o) * rows + half * per_touch
                return product_ref[at : at + per_touch, half * LANES : (half + 1) * LANES]

            for o in range(offsets):
                both = []
                for half in range(2):
                    total = found(0, o + 1, half)
                    for a in range(1, GROUPS):
                        shift = WIDTH * a
                        total = total + pltpu.roll(
                            jnp.where(
                                lane < LANES - shift, found(a, o + 1, half), found(a, o, half)
                            ),
                            shift,
                            1,
                        )
                    both.append(total * scales[half])
                answer_ref[
                    pl.ds(pl.multiple_of(16 * pair, 16), 16), o * LANES : (o + 1) * LANES
                ] = jnp.concatenate(both, axis=0).astype(jnp.bfloat16)

    back = [
        pltpu.make_async_copy(
            answer_ref.at[pl.ds(e * depth * per_touch, depth * per_touch), :],
            outs[e],
            sem_ref.at[e],
        )
        for e in range(NEAR)
    ]
    for copy in back:
        copy.start()
    for copy in back:
        copy.wait()


def profile(part, depth, num_query, touches, me, shards, library):
    blocks = library.shape[1]
    offsets = SHIFTS // LANES
    tiles = blocks // GROUPS
    records = shards[0].shape[0] - num_query * blocks
    per_block = rounded(depth, ROW_SLOTS) // ROW_SLOTS
    table = (rounded(NEAR * per_block, 8), LANES)
    smem = pl.BlockSpec(memory_space=pltpu.SMEM)
    vmem = pl.BlockSpec(memory_space=pltpu.VMEM)
    hbm = pl.BlockSpec(memory_space=pl.ANY)
    answers = NEAR * depth * PER_TOUCH
    flops = answers * 2 * (offsets + 1) * (blocks + 4) * LANES * LANES
    return pl.pallas_call(
        functools.partial(profile_kernel, depth, num_query, touches),
        out_shape=[
            jax.ShapeDtypeStruct((depth * PER_TOUCH, SHIFTS), jnp.bfloat16)
            for _ in range(NEAR)
        ],
        in_specs=[smem] + [hbm] * NEAR + [vmem],
        out_specs=[hbm] * NEAR,
        scratch_shapes=[
            pltpu.VMEM((NEAR, *shards[0].shape), jnp.bfloat16),
            pltpu.VMEM((records, LANES), jnp.float32),
            pltpu.VMEM(table, jnp.int32),
            pltpu.SMEM(table, jnp.int32),
            pltpu.VMEM((answers, SHIFTS), jnp.bfloat16),
            pltpu.VMEM(((blocks + offsets + 1) * 16, LANES), jnp.float32),
            pltpu.VMEM(((blocks + offsets + 1) * 16, LANES), jnp.bfloat16),
            pltpu.VMEM((2, blocks, LANES), jnp.float32),
            pltpu.VMEM((GROUPS, (tiles + offsets + 1) * 16, LANES), jnp.bfloat16),
            pltpu.VMEM(((tiles + 1) * LANES, 2 * LANES), jnp.bfloat16),
            pltpu.VMEM((GROUPS * (offsets + 1) * 16, 2 * LANES), jnp.float32),
            pltpu.SemaphoreType.DMA((NEAR + 1,)),
        ],
        compiler_params=pltpu.CompilerParams(vmem_limit_bytes=VMEM_LIMIT),
        cost_estimate=pl.CostEstimate(
            flops=8 * flops, bytes_accessed=8 * 1024 * 1024, transcendentals=0
        ),
        name=f"profile_{part}",
    )(me, *shards, library)


def unpack_kernel(part, depth, me_ref, table_ref, *refs):
    got, refs = refs[:NEAR], refs[-3:]
    out_ref, stage_ref, sem_ref = refs
    per_block = rounded(depth, ROW_SLOTS) // ROW_SLOTS

    def copy(slot, touch):
        return pltpu.make_async_copy(stage_ref.at[slot], out_ref.at[touch], sem_ref.at[slot])

    def touch_of(e, s):
        block = jnp.bitwise_xor(me_ref[0], NEAR * part + e)
        line = block * per_block + s // ROW_SLOTS
        return table_ref[line, s % ROW_SLOTS * SLOT_LANES + 2 * PER_TOUCH] - 1

    for e in range(NEAR):
        for s in range(depth):
            touch = touch_of(e, s)
            slot = e * depth + s

            @pl.when(touch >= 0)
            def _():
                stage_ref[slot] = got[e][s * PER_TOUCH : (s + 1) * PER_TOUCH, :].astype(
                    jnp.float32
                )
                copy(slot, touch).start()

    for e in range(NEAR):
        for s in range(depth):
            touch = touch_of(e, s)

            @pl.when(touch >= 0)
            def _():
                copy(e * depth + s, touch).wait()


def unpack(part, depth, touched, me, table, got, out):
    shifts = got[0].shape[1]
    smem = pl.BlockSpec(memory_space=pltpu.SMEM)
    vmem = pl.BlockSpec(memory_space=pltpu.VMEM)
    hbm = pl.BlockSpec(memory_space=pl.ANY)
    more = () if out is None else (out,)
    return pl.pallas_call(
        functools.partial(unpack_kernel, part, depth),
        out_shape=jax.ShapeDtypeStruct((touched, PER_TOUCH, shifts), jnp.float32),
        in_specs=[smem] * 2 + [vmem] * NEAR + [hbm] * len(more),
        out_specs=hbm,
        scratch_shapes=[
            pltpu.VMEM((NEAR * depth, PER_TOUCH, shifts), jnp.float32),
            pltpu.SemaphoreType.DMA((NEAR * depth,)),
        ],
        input_output_aliases={2 + NEAR: 0} if more else {},
        compiler_params=pltpu.CompilerParams(vmem_limit_bytes=VMEM_LIMIT),
        cost_estimate=pl.CostEstimate(
            flops=0, bytes_accessed=NEAR * got[0].size * 6, transcendentals=0
        ),
        name=f"unpack_{part}",
    )(me, table, *got, *more)


def local(spectra, library, cand_block, cand_local):
    devices = lax.axis_size("lib")
    num_query, num_bins = spectra.shape
    touches, per_touch = cand_local.shape[1], cand_local.shape[2]
    depth = rounded(depth_of(num_query, touches, devices), 2)
    blocks = num_bins // LANES
    records = rounded(devices * (rounded(depth, ROW_SLOTS) // ROW_SLOTS), 16)
    me = lax.axis_index("lib").astype(jnp.int32).reshape(1)

    def across(value, distance):
        if distance == 0:
            return value
        pairs = [(i, i ^ distance) for i in range(devices)]
        return lax.ppermute(value, "lib", pairs)

    shard, table = prepare(
        spectra, cand_block, cand_local.reshape(-1, per_touch), depth, records
    )
    far = devices // NEAR
    order = [0] + list(range(far - 1, 0, -1))
    heads = {part: across(shard, NEAR * part) for part in order}
    shards = {
        part: [across(heads[part], e) for e in range(NEAR)] for part in order
    }
    rows = library.reshape(-1, blocks, LANES)
    got = {}
    for part in order:
        answers = profile(part, depth, num_query, touches, me, shards[part], rows)
        got[part] = [across(answers[e], NEAR * part + e) for e in range(NEAR)]
    out = None
    for part in order:
        out = unpack(part, depth, num_query * touches, me, table, got[part], out)
    return out.reshape(num_query, touches * per_touch, SHIFTS)


def solution(mesh):
    placed = (
        P(("groups", "lib"), None),
        P("lib", None),
        P(("groups", "lib"), None),
        P(("groups", "lib"), None, None),
    )
    return jax.shard_map(
        local,
        mesh=mesh,
        in_specs=placed,
        out_specs=P(("groups", "lib"), None, None),
        check_vma=False,
    )
```

```python
import functools

import jax
import jax.numpy as jnp
from jax import lax
from jax.experimental import pallas as pl
from jax.experimental.pallas import tpu as pltpu
from jax.sharding import PartitionSpec as P

SHIFTS = 1024
BG = 32
EPSILON = 1e-06
LANES = 128
VMEM_LIMIT = 48 * 1024 * 1024
NEAR = 4
ROW_SLOTS = 4
SLOT_LANES = LANES // ROW_SLOTS
PER_TOUCH = 8
CHAINS = 1
GROUPS = 4
WIDTH = LANES // GROUPS


def rounded(value, unit):
    return -(-value // unit) * unit


def depth_of(num_query, touches, devices):
    return min(num_query, max(3, 3 * num_query * touches // (2 * devices)))


def record_values(found):
    lane = lax.broadcasted_iota(jnp.int32, found.shape, 1) % SLOT_LANES
    low = pltpu.roll(found, LANES - PER_TOUCH, 1)
    return jnp.where(lane < PER_TOUCH, found * 16 + low, found).astype(jnp.int32)


def prepare_kernel(depth, spectra_ref, named_ref, wanted_ref, out_ref, table_ref, rows_ref):
    num_query, num_bins = spectra_ref.shape
    blocks = num_bins // LANES
    values = spectra_ref[...].astype(jnp.float32)
    zeros = jnp.zeros((num_query, LANES), jnp.float32)
    wide = jnp.concatenate([values, zeros], axis=1)
    total, length = wide, 1
    while length < 2 * BG:
        total = total + pltpu.roll(total, length, 1)
        length *= 2
    total = total + pltpu.roll(wide, length, 1)
    total = pltpu.roll(total, total.shape[1] - BG, 1)[:, :num_bins]
    centered = values - total / (2 * BG + 1)
    factor = lax.rsqrt(jnp.mean(centered * centered, axis=1, keepdims=True) + EPSILON)
    prepared = (centered * factor).astype(jnp.bfloat16)
    row = lax.broadcasted_iota(jnp.int32, (LANES, LANES), 0)
    col = lax.broadcasted_iota(jnp.int32, (LANES, LANES), 1)
    flip = jnp.where(row + col == LANES - 1, 1.0, 0.0).astype(jnp.bfloat16)
    for block in range(blocks):
        piece = prepared[:, block * LANES : (block + 1) * LANES]
        turned = jnp.dot(piece, flip, preferred_element_type=jnp.float32)
        rows_ref[pl.ds(blocks - 1 - block, num_query, stride=blocks), :] = turned
    out_ref[0 : num_query * blocks, :] = rows_ref[...].astype(jnp.bfloat16)

    touches = named_ref.shape[1]
    touched = num_query * touches
    records = table_ref.shape[0]
    per_block = rounded(depth, ROW_SLOTS) // ROW_SLOTS
    touch = lax.broadcasted_iota(jnp.int32, (touched, num_query), 0)
    query = lax.broadcasted_iota(jnp.int32, (touched, num_query), 1)
    owner = jnp.where(touch // touches == query, 1.0, 0.0).astype(jnp.bfloat16)
    named = named_ref[...].astype(jnp.float32).astype(jnp.bfloat16)
    spread = jnp.dot(owner, named, preferred_element_type=jnp.float32)
    touch = lax.broadcasted_iota(jnp.int32, (touched, touches), 0)
    which = lax.broadcasted_iota(jnp.int32, (touched, touches), 1)
    block_col = jnp.sum(
        jnp.where(touch % touches == which, spread, 0.0), axis=1, keepdims=True
    )
    row = lax.broadcasted_iota(jnp.int32, (touched, touched), 0)
    col = lax.broadcasted_iota(jnp.int32, (touched, touched), 1)
    block_row = jnp.sum(jnp.where(row == col, block_col, 0.0), axis=0, keepdims=True)
    earlier = (block_col == block_row) & (row < col)
    rank = jnp.sum(jnp.where(earlier, 1.0, 0.0), axis=0, keepdims=True).astype(jnp.int32)
    place = block_row.astype(jnp.int32) * per_block + rank // ROW_SLOTS
    wanted = wanted_ref[...]
    high = (wanted // 16).astype(jnp.float32).astype(jnp.bfloat16)
    low = (wanted % 16).astype(jnp.float32).astype(jnp.bfloat16)
    unit = lax.broadcasted_iota(jnp.int32, (PER_TOUCH, LANES), 0)
    lane = lax.broadcasted_iota(jnp.int32, (PER_TOUCH, LANES), 1)
    row = lax.broadcasted_iota(jnp.int32, (records, touched), 0)
    touch = lax.broadcasted_iota(jnp.int32, (touched, LANES), 0)
    wide_lane = lax.broadcasted_iota(jnp.int32, (touched, LANES), 1)
    found = jnp.zeros((records, LANES), jnp.float32)
    for group in range(ROW_SLOTS):
        start = group * SLOT_LANES
        to_high = jnp.where(lane == start + unit, 1.0, 0.0).astype(jnp.bfloat16)
        to_low = jnp.where(lane == start + PER_TOUCH + unit, 1.0, 0.0).astype(jnp.bfloat16)
        data = jnp.dot(high, to_high, preferred_element_type=jnp.float32)
        data = data + jnp.dot(low, to_low, preferred_element_type=jnp.float32)
        data = jnp.where(
            wide_lane == start + 2 * PER_TOUCH, (touch + 1).astype(jnp.float32), data
        ).astype(jnp.bfloat16)
        pick = jnp.where((row == place) & (rank % ROW_SLOTS == group), 1.0, 0.0)
        found = found + jnp.dot(
            pick.astype(jnp.bfloat16), data, preferred_element_type=jnp.float32
        )
    out_ref[num_query * blocks :, :] = found.astype(jnp.bfloat16)
    table_ref[...] = record_values(found)


def prepare(spectra, named, wanted, depth, records):
    num_query, num_bins = spectra.shape
    rows = num_query * num_bins // LANES
    return pl.pallas_call(
        functools.partial(prepare_kernel, depth),
        out_shape=(
            jax.ShapeDtypeStruct((rows + records, LANES), jnp.bfloat16),
            jax.ShapeDtypeStruct((records, LANES), jnp.int32),
        ),
        scratch_shapes=[pltpu.VMEM((rows, LANES), jnp.float32)],
        compiler_params=pltpu.CompilerParams(vmem_limit_bytes=VMEM_LIMIT),
        name="prepare",
    )(spectra, named, wanted)


def profile_kernel(depth, num_query, touches, me_ref, *refs):
    shards, library_ref, refs = refs[:NEAR], refs[NEAR], refs[NEAR + 1 :]
    outs, refs = refs[:NEAR], refs[NEAR:]
    (
        query_ref, record_ref, line_ref, found_ref, table_ref, answer_ref,
        pick_ref, cand_ref, scale_ref, spectrum_ref, left_ref, right_ref, product_ref, sem_ref,
    ) = refs
    per_touch = PER_TOUCH
    rows = 2 * per_touch
    lines, num_bins = library_ref.shape
    blocks = num_bins // LANES
    offsets = SHIFTS // LANES
    first = offsets // 2 + 1
    tiles = blocks // GROUPS
    query_rows = num_query * blocks
    per_block = rounded(depth, ROW_SLOTS) // ROW_SLOTS
    row = lax.broadcasted_iota(jnp.int32, (8, LANES), 0)
    lane = lax.broadcasted_iota(jnp.int32, (8, LANES), 1)
    lane16 = lax.broadcasted_iota(jnp.int32, (rows, LANES), 1)

    copies = [
        pltpu.make_async_copy(shards[e], query_ref.at[e], sem_ref.at[e]) for e in range(NEAR)
    ]
    for copy in copies:
        copy.start()
    line_ref[...] = jnp.zeros(line_ref.shape, line_ref.dtype)
    scale_ref[...] = jnp.zeros(scale_ref.shape, scale_ref.dtype)
    right_ref[...] = jnp.zeros(right_ref.shape, right_ref.dtype)
    for e in range(NEAR):
        copies[e].wait()
        record_ref[...] = query_ref[e, query_rows:, :].astype(jnp.float32)
        line_ref[e * per_block : (e + 1) * per_block, :] = record_ref[
            pl.ds(me_ref[0] * per_block, per_block), :
        ]
    found_ref[...] = record_values(line_ref[...])
    to_scalars = pltpu.make_async_copy(found_ref, table_ref, sem_ref.at[NEAR])
    to_scalars.start()
    to_scalars.wait()

    picked = pick_ref.shape[0]
    at = lax.broadcasted_iota(jnp.int32, (picked, line_ref.shape[0]), 0)
    line = lax.broadcasted_iota(jnp.int32, (picked, line_ref.shape[0]), 1)
    own = jnp.where(at // (PER_TOUCH * ROW_SLOTS) == line, 1.0, 0.0).astype(jnp.bfloat16)
    spread = jnp.dot(own, line_ref[...].astype(jnp.bfloat16), preferred_element_type=jnp.float32)
    at = lax.broadcasted_iota(jnp.int32, (picked, LANES), 0)
    high = at // PER_TOUCH % ROW_SLOTS * SLOT_LANES + at % PER_TOUCH
    wide_lane = lax.broadcasted_iota(jnp.int32, (picked, LANES), 1)
    weight = jnp.where(
        wide_lane == high, 16.0, jnp.where(wide_lane == high + PER_TOUCH, 1.0, 0.0)
    )
    wanted = jnp.sum(spread * weight, axis=1, keepdims=True).astype(jnp.int32)
    which = lax.broadcasted_iota(jnp.int32, (picked, lines), 1)
    pick_ref[...] = jnp.where(which == wanted, 1.0, 0.0).astype(jnp.bfloat16)

    @pl.loop(0, num_bins // (2 * LANES))
    def _(n):
        columns = pl.ds(pl.multiple_of(n * 2 * LANES, 2 * LANES), 2 * LANES)
        piece = jnp.dot(
            pick_ref[...], library_ref[:, columns], preferred_element_type=jnp.float32
        )
        cand_ref[:, columns] = piece.astype(jnp.bfloat16)
        low, top = piece[:, :LANES], piece[:, LANES:]
        scale_ref[...] += low * low + top * top

    mean = jnp.sum(scale_ref[...], axis=1, keepdims=True) / num_bins
    scale_ref[...] = jnp.broadcast_to(lax.rsqrt(mean + EPSILON), scale_ref.shape)

    def entry(slot):
        e = slot // depth
        s = slot % depth
        return e, e * per_block + s // ROW_SLOTS, s % ROW_SLOTS * SLOT_LANES

    def touch_of(slot):
        _, line, start = entry(slot)
        return table_ref[line, start + 2 * per_touch] - 1

    def choose(pieces):
        value = pieces[0]
        for group in range(1, GROUPS):
            value = jnp.where(lane16 < group * WIDTH, value, pieces[group])
        return value

    def make_left(pair):
        def block_of(b):
            if not 0 <= b < blocks:
                return jnp.zeros((rows, LANES), jnp.bfloat16)
            return cand_ref[
                pl.ds(pl.multiple_of(rows * pair, rows), rows), b * LANES : (b + 1) * LANES
            ]

        for t in range(tiles + offsets + 1):
            given = [block_of(t + tiles * g - first) for g in range(GROUPS)]
            turned = []
            for c in range(GROUPS):
                mixed = choose([given[(a + c) % GROUPS] for a in range(GROUPS)])
                turned.append(pltpu.roll(mixed, WIDTH * c, 1) if c else mixed)
            for a in range(GROUPS):
                left_ref[a, pl.ds(rows * t, rows), :] = choose(
                    [turned[(g - a) % GROUPS] for g in range(GROUPS)]
                )

    def make_right(slot, half):
        query = jnp.maximum(touch_of(slot), 0) // touches
        spectrum_ref[half] = query_ref[
            entry(slot)[0], pl.ds(pl.multiple_of(query * blocks, blocks), blocks), :
        ].astype(jnp.float32)
        zero = jnp.zeros((8, LANES), jnp.float32)
        before = (zero, zero)
        before_shifted = jnp.zeros((16, LANES), jnp.bfloat16)
        columns = slice(half * LANES, (half + 1) * LANES)
        for b in range(blocks + 1):
            if b < blocks:
                wide = jnp.broadcast_to(spectrum_ref[half, pl.ds(b, 1), :], (8, LANES))
                now = tuple(
                    pltpu.roll(wide, 1 + 8 * h, 1, stride=1, stride_axis=0) for h in range(2)
                )
            else:
                now = (zero, zero)
            shifted = jnp.concatenate(
                [jnp.where(lane > row + 8 * h, now[h], before[h]) for h in range(2)], axis=0
            ).astype(jnp.bfloat16)
            j = blocks - 1 - b
            place = 0 if j < 0 else (j % tiles + 1) * LANES + j // tiles * WIDTH
            right_ref[pl.ds(place, 16), columns] = shifted
            for c in range(16, WIDTH, 16):
                right_ref[pl.ds(place + c, 16), columns] = pltpu.roll(
                    jnp.where(lane16 < LANES - c, shifted, before_shifted), c, 1
                )
            before, before_shifted = now, shifted

    def sums(low, high):
        left = jnp.concatenate(
            [
                jnp.concatenate(
                    [
                        left_ref[a, pl.ds(rows * t, rows * (offsets + 1)), :]
                        for t in range(tiles + 1)
                    ],
                    axis=1,
                )
                for a in range(low, high)
            ],
            axis=0,
        )
        return jnp.dot(left, right_ref[...], preferred_element_type=jnp.float32)

    slots = NEAR * depth
    height = GROUPS // CHAINS * (offsets + 1) * rows

    @pl.loop(0, slots // 2)
    def _(pair):
        @pl.when((touch_of(2 * pair) >= 0) | (touch_of(2 * pair + 1) >= 0))
        def _():
            make_left(pair)
            for half in range(2):
                make_right(2 * pair + half, half)
            step = GROUPS // CHAINS
            for c in range(CHAINS):
                product_ref[c * height : (c + 1) * height, :] = sums(step * c, step * (c + 1))

            def found(a, o, half):
                at = (a * (offsets + 1) + o) * rows + half * per_touch
                return product_ref[at : at + per_touch, half * LANES : (half + 1) * LANES]

            for o in range(offsets):
                both = []
                for half in range(2):
                    total = found(0, o + 1, half)
                    for a in range(1, GROUPS):
                        shift = WIDTH * a
                        total = total + pltpu.roll(
                            jnp.where(
                                lane < LANES - shift, found(a, o + 1, half), found(a, o, half)
                            ),
                            shift,
                            1,
                        )
                    scale_row = pl.multiple_of(rows * pair + per_touch * half, per_touch)
                    both.append(total * scale_ref[pl.ds(scale_row, per_touch), :])
                answer_ref[
                    pl.ds(pl.multiple_of(16 * pair, 16), 16), o * LANES : (o + 1) * LANES
                ] = jnp.concatenate(both, axis=0).astype(jnp.bfloat16)

    back = [
        pltpu.make_async_copy(
            answer_ref.at[pl.ds(e * depth * per_touch, depth * per_touch), :],
            outs[e],
            sem_ref.at[e],
        )
        for e in range(NEAR)
    ]
    for copy in back:
        copy.start()
    for copy in back:
        copy.wait()


def profile(part, depth, num_query, touches, me, shards, library):
    blocks = library.shape[1] // LANES
    offsets = SHIFTS // LANES
    tiles = blocks // GROUPS
    records = shards[0].shape[0] - num_query * blocks
    per_block = rounded(depth, ROW_SLOTS) // ROW_SLOTS
    table = (rounded(NEAR * per_block, 8), LANES)
    smem = pl.BlockSpec(memory_space=pltpu.SMEM)
    vmem = pl.BlockSpec(memory_space=pltpu.VMEM)
    hbm = pl.BlockSpec(memory_space=pl.ANY)
    answers = NEAR * depth * PER_TOUCH
    flops = answers * 2 * (offsets + 1) * (blocks + 4) * LANES * LANES
    return pl.pallas_call(
        functools.partial(profile_kernel, depth, num_query, touches),
        out_shape=[
            jax.ShapeDtypeStruct((depth * PER_TOUCH, SHIFTS), jnp.bfloat16)
            for _ in range(NEAR)
        ],
        in_specs=[smem] + [hbm] * NEAR + [vmem],
        out_specs=[hbm] * NEAR,
        scratch_shapes=[
            pltpu.VMEM((NEAR, *shards[0].shape), jnp.bfloat16),
            pltpu.VMEM((records, LANES), jnp.float32),
            pltpu.VMEM(table, jnp.float32),
            pltpu.VMEM(table, jnp.int32),
            pltpu.SMEM(table, jnp.int32),
            pltpu.VMEM((answers, SHIFTS), jnp.bfloat16),
            pltpu.VMEM((answers, library.shape[0]), jnp.bfloat16),
            pltpu.VMEM((answers, library.shape[1]), jnp.bfloat16),
            pltpu.VMEM((answers, LANES), jnp.float32),
            pltpu.VMEM((2, blocks, LANES), jnp.float32),
            pltpu.VMEM((GROUPS, (tiles + offsets + 1) * 16, LANES), jnp.bfloat16),
            pltpu.VMEM(((tiles + 1) * LANES, 2 * LANES), jnp.bfloat16),
            pltpu.VMEM((GROUPS * (offsets + 1) * 16, 2 * LANES), jnp.float32),
            pltpu.SemaphoreType.DMA((NEAR + 1,)),
        ],
        compiler_params=pltpu.CompilerParams(vmem_limit_bytes=VMEM_LIMIT),
        cost_estimate=pl.CostEstimate(
            flops=8 * flops, bytes_accessed=8 * 1024 * 1024, transcendentals=0
        ),
        name=f"profile_{part}",
    )(me, *shards, library)


def unpack_kernel(part, depth, me_ref, table_ref, *refs):
    got, refs = refs[:NEAR], refs[-3:]
    out_ref, stage_ref, sem_ref = refs
    per_block = rounded(depth, ROW_SLOTS) // ROW_SLOTS

    def copy(slot, touch):
        return pltpu.make_async_copy(stage_ref.at[slot], out_ref.at[touch], sem_ref.at[slot])

    def touch_of(e, s):
        block = jnp.bitwise_xor(me_ref[0], NEAR * part + e)
        line = block * per_block + s // ROW_SLOTS
        return table_ref[line, s % ROW_SLOTS * SLOT_LANES + 2 * PER_TOUCH] - 1

    for e in range(NEAR):
        for s in range(depth):
            touch = touch_of(e, s)
            slot = e * depth + s

            @pl.when(touch >= 0)
            def _():
                stage_ref[slot] = got[e][s * PER_TOUCH : (s + 1) * PER_TOUCH, :].astype(
                    jnp.float32
                )
                copy(slot, touch).start()

    for e in range(NEAR):
        for s in range(depth):
            touch = touch_of(e, s)

            @pl.when(touch >= 0)
            def _():
                copy(e * depth + s, touch).wait()


def unpack(part, depth, touched, me, table, got, out):
    shifts = got[0].shape[1]
    smem = pl.BlockSpec(memory_space=pltpu.SMEM)
    vmem = pl.BlockSpec(memory_space=pltpu.VMEM)
    hbm = pl.BlockSpec(memory_space=pl.ANY)
    more = () if out is None else (out,)
    return pl.pallas_call(
        functools.partial(unpack_kernel, part, depth),
        out_shape=jax.ShapeDtypeStruct((touched, PER_TOUCH, shifts), jnp.float32),
        in_specs=[smem] * 2 + [vmem] * NEAR + [hbm] * len(more),
        out_specs=hbm,
        scratch_shapes=[
            pltpu.VMEM((NEAR * depth, PER_TOUCH, shifts), jnp.float32),
            pltpu.SemaphoreType.DMA((NEAR * depth,)),
        ],
        input_output_aliases={2 + NEAR: 0} if more else {},
        compiler_params=pltpu.CompilerParams(vmem_limit_bytes=VMEM_LIMIT),
        cost_estimate=pl.CostEstimate(
            flops=0, bytes_accessed=NEAR * got[0].size * 6, transcendentals=0
        ),
        name=f"unpack_{part}",
    )(me, table, *got, *more)


def local(spectra, library, cand_block, cand_local):
    devices = lax.axis_size("lib")
    num_query, num_bins = spectra.shape
    touches, per_touch = cand_local.shape[1], cand_local.shape[2]
    depth = rounded(depth_of(num_query, touches, devices), ROW_SLOTS)
    records = rounded(devices * (rounded(depth, ROW_SLOTS) // ROW_SLOTS), 16)
    me = lax.axis_index("lib").astype(jnp.int32).reshape(1)

    def across(value, distance):
        if distance == 0:
            return value
        pairs = [(i, i ^ distance) for i in range(devices)]
        return lax.ppermute(value, "lib", pairs)

    shard, table = prepare(
        spectra, cand_block, cand_local.reshape(-1, per_touch), depth, records
    )
    far = devices // NEAR
    order = [0] + list(range(far - 1, 0, -1))
    heads = {part: across(shard, NEAR * part) for part in order}
    shards = {
        part: [across(heads[part], e) for e in range(NEAR)] for part in order
    }
    got = {}
    for part in order:
        answers = profile(part, depth, num_query, touches, me, shards[part], library)
        got[part] = [across(answers[e], NEAR * part + e) for e in range(NEAR)]
    out = None
    for part in order:
        out = unpack(part, depth, num_query * touches, me, table, got[part], out)
    return out.reshape(num_query, touches * per_touch, SHIFTS)


def solution(mesh):
    placed = (
        P(("groups", "lib"), None),
        P("lib", None),
        P(("groups", "lib"), None),
        P(("groups", "lib"), None, None),
    )
    return jax.shard_map(
        local,
        mesh=mesh,
        in_specs=placed,
        out_specs=P(("groups", "lib"), None, None),
        check_vma=False,
    )
```

```python
import functools

import jax
import jax.numpy as jnp
from jax import lax
from jax.experimental import pallas as pl
from jax.experimental.pallas import tpu as pltpu
from jax.sharding import PartitionSpec as P

SHIFTS = 1024
BG = 32
EPSILON = 1e-06
LANES = 128
VMEM_LIMIT = 48 * 1024 * 1024
NEAR = 4
ROW_SLOTS = 4
SLOT_LANES = LANES // ROW_SLOTS
PER_TOUCH = 8
CHAINS = 1
GROUPS = 4
WIDTH = LANES // GROUPS


def rounded(value, unit):
    return -(-value // unit) * unit


def depth_of(num_query, touches, devices):
    return min(num_query, max(3, 3 * num_query * touches // (2 * devices)))


def record_values(found):
    lane = lax.broadcasted_iota(jnp.int32, found.shape, 1) % SLOT_LANES
    low = pltpu.roll(found, LANES - PER_TOUCH, 1)
    return jnp.where(lane < PER_TOUCH, found * 16 + low, found).astype(jnp.int32)


def prepare_kernel(depth, spectra_ref, named_ref, wanted_ref, out_ref, table_ref, rows_ref):
    num_query, num_bins = spectra_ref.shape
    blocks = num_bins // LANES
    values = spectra_ref[...].astype(jnp.float32)
    zeros = jnp.zeros((num_query, LANES), jnp.float32)
    wide = jnp.concatenate([values, zeros], axis=1)
    total, length = wide, 1
    while length < 2 * BG:
        total = total + pltpu.roll(total, length, 1)
        length *= 2
    total = total + pltpu.roll(wide, length, 1)
    total = pltpu.roll(total, total.shape[1] - BG, 1)[:, :num_bins]
    centered = values - total / (2 * BG + 1)
    factor = lax.rsqrt(jnp.mean(centered * centered, axis=1, keepdims=True) + EPSILON)
    prepared = (centered * factor).astype(jnp.bfloat16)
    row = lax.broadcasted_iota(jnp.int32, (LANES, LANES), 0)
    col = lax.broadcasted_iota(jnp.int32, (LANES, LANES), 1)
    flip = jnp.where(row + col == LANES - 1, 1.0, 0.0).astype(jnp.bfloat16)
    for block in range(blocks):
        piece = prepared[:, block * LANES : (block + 1) * LANES]
        turned = jnp.dot(piece, flip, preferred_element_type=jnp.float32)
        rows_ref[pl.ds(blocks - 1 - block, num_query, stride=blocks), :] = turned
    out_ref[0 : num_query * blocks, :] = rows_ref[...].astype(jnp.bfloat16)

    touches = named_ref.shape[1]
    touched = num_query * touches
    records = table_ref.shape[0]
    per_block = rounded(depth, ROW_SLOTS) // ROW_SLOTS
    touch = lax.broadcasted_iota(jnp.int32, (touched, num_query), 0)
    query = lax.broadcasted_iota(jnp.int32, (touched, num_query), 1)
    owner = jnp.where(touch // touches == query, 1.0, 0.0).astype(jnp.bfloat16)
    named = named_ref[...].astype(jnp.float32).astype(jnp.bfloat16)
    spread = jnp.dot(owner, named, preferred_element_type=jnp.float32)
    touch = lax.broadcasted_iota(jnp.int32, (touched, touches), 0)
    which = lax.broadcasted_iota(jnp.int32, (touched, touches), 1)
    block_col = jnp.sum(
        jnp.where(touch % touches == which, spread, 0.0), axis=1, keepdims=True
    )
    row = lax.broadcasted_iota(jnp.int32, (touched, touched), 0)
    col = lax.broadcasted_iota(jnp.int32, (touched, touched), 1)
    block_row = jnp.sum(jnp.where(row == col, block_col, 0.0), axis=0, keepdims=True)
    earlier = (block_col == block_row) & (row < col)
    rank = jnp.sum(jnp.where(earlier, 1.0, 0.0), axis=0, keepdims=True).astype(jnp.int32)
    place = block_row.astype(jnp.int32) * per_block + rank // ROW_SLOTS
    wanted = wanted_ref[...]
    high = (wanted // 16).astype(jnp.float32).astype(jnp.bfloat16)
    low = (wanted % 16).astype(jnp.float32).astype(jnp.bfloat16)
    unit = lax.broadcasted_iota(jnp.int32, (PER_TOUCH, LANES), 0)
    lane = lax.broadcasted_iota(jnp.int32, (PER_TOUCH, LANES), 1)
    row = lax.broadcasted_iota(jnp.int32, (records, touched), 0)
    touch = lax.broadcasted_iota(jnp.int32, (touched, LANES), 0)
    wide_lane = lax.broadcasted_iota(jnp.int32, (touched, LANES), 1)
    found = jnp.zeros((records, LANES), jnp.float32)
    for group in range(ROW_SLOTS):
        start = group * SLOT_LANES
        to_high = jnp.where(lane == start + unit, 1.0, 0.0).astype(jnp.bfloat16)
        to_low = jnp.where(lane == start + PER_TOUCH + unit, 1.0, 0.0).astype(jnp.bfloat16)
        data = jnp.dot(high, to_high, preferred_element_type=jnp.float32)
        data = data + jnp.dot(low, to_low, preferred_element_type=jnp.float32)
        data = jnp.where(
            wide_lane == start + 2 * PER_TOUCH, (touch + 1).astype(jnp.float32), data
        ).astype(jnp.bfloat16)
        pick = jnp.where((row == place) & (rank % ROW_SLOTS == group), 1.0, 0.0)
        found = found + jnp.dot(
            pick.astype(jnp.bfloat16), data, preferred_element_type=jnp.float32
        )
    out_ref[num_query * blocks :, :] = found.astype(jnp.bfloat16)
    table_ref[...] = record_values(found)


def prepare(spectra, named, wanted, depth, records):
    num_query, num_bins = spectra.shape
    rows = num_query * num_bins // LANES
    return pl.pallas_call(
        functools.partial(prepare_kernel, depth),
        out_shape=(
            jax.ShapeDtypeStruct((rows + records, LANES), jnp.bfloat16),
            jax.ShapeDtypeStruct((records, LANES), jnp.int32),
        ),
        scratch_shapes=[pltpu.VMEM((rows, LANES), jnp.float32)],
        compiler_params=pltpu.CompilerParams(vmem_limit_bytes=VMEM_LIMIT),
        name="prepare",
    )(spectra, named, wanted)


def profile_kernel(near, depth, num_query, touches, me_ref, *refs):
    shards, library_ref, refs = refs[:near], refs[near], refs[near + 1 :]
    outs, refs = refs[:near], refs[near:]
    (
        query_ref, record_ref, found_ref, table_ref, answer_ref,
        cand_ref, packed_ref, spectrum_ref, left_ref, right_ref, product_ref, sem_ref,
    ) = refs
    per_touch = PER_TOUCH
    rows = 2 * per_touch
    blocks = library_ref.shape[1]
    offsets = SHIFTS // LANES
    first = offsets // 2 + 1
    tiles = blocks // GROUPS
    query_rows = num_query * blocks
    per_block = rounded(depth, ROW_SLOTS) // ROW_SLOTS
    row = lax.broadcasted_iota(jnp.int32, (8, LANES), 0)
    lane = lax.broadcasted_iota(jnp.int32, (8, LANES), 1)
    lane16 = lax.broadcasted_iota(jnp.int32, (rows, LANES), 1)

    copies = [
        pltpu.make_async_copy(shards[e], query_ref.at[e], sem_ref.at[e]) for e in range(near)
    ]
    for copy in copies:
        copy.start()
    cand_ref[...] = jnp.zeros(cand_ref.shape, cand_ref.dtype)
    right_ref[...] = jnp.zeros(right_ref.shape, right_ref.dtype)
    found_ref[...] = jnp.zeros(found_ref.shape, found_ref.dtype)
    for e in range(near):
        copies[e].wait()
        record_ref[...] = query_ref[e, query_rows:, :].astype(jnp.float32)
        found_ref[e * per_block : (e + 1) * per_block, :] = record_values(
            record_ref[pl.ds(me_ref[0] * per_block, per_block), :]
        )
    to_scalars = pltpu.make_async_copy(found_ref, table_ref, sem_ref.at[near])
    to_scalars.start()
    to_scalars.wait()

    def entry(slot):
        e = slot // depth
        s = slot % depth
        return e, e * per_block + s // ROW_SLOTS, s % ROW_SLOTS * SLOT_LANES

    def touch_of(slot):
        _, line, start = entry(slot)
        return table_ref[line, start + 2 * per_touch] - 1

    def choose(pieces):
        value = pieces[0]
        for group in range(1, GROUPS):
            value = jnp.where(lane16 < group * WIDTH, value, pieces[group])
        return value

    def gather(slot, half):
        _, line, start = entry(slot)
        for k in range(per_touch):
            wanted = table_ref[line, start + k]
            cand_ref[pl.ds(first * rows + half * per_touch + k, blocks, stride=rows), :] = (
                library_ref[wanted].astype(jnp.float32)
            )
        square = jnp.zeros((per_touch, LANES), jnp.float32)
        for b in range(blocks):
            piece = cand_ref[pl.ds((first + b) * rows + half * per_touch, per_touch), :]
            square = square + piece * piece
        mean = jnp.sum(square, axis=1, keepdims=True) / (blocks * LANES)
        return lax.rsqrt(mean + EPSILON)

    def make_left():
        for b in range(blocks + offsets + 1):
            packed_ref[pl.ds(rows * b, rows), :] = cand_ref[pl.ds(rows * b, rows), :].astype(
                jnp.bfloat16
            )
        for t in range(tiles + offsets + 1):
            given = [packed_ref[pl.ds(rows * (t + tiles * g), rows), :] for g in range(GROUPS)]
            turned = []
            for c in range(GROUPS):
                mixed = choose([given[(a + c) % GROUPS] for a in range(GROUPS)])
                turned.append(pltpu.roll(mixed, WIDTH * c, 1) if c else mixed)
            for a in range(GROUPS):
                left_ref[a, pl.ds(rows * t, rows), :] = choose(
                    [turned[(g - a) % GROUPS] for g in range(GROUPS)]
                )

    def make_right(slot, half):
        query = jnp.maximum(touch_of(slot), 0) // touches
        spectrum_ref[half] = query_ref[
            entry(slot)[0], pl.ds(pl.multiple_of(query * blocks, blocks), blocks), :
        ].astype(jnp.float32)
        zero = jnp.zeros((8, LANES), jnp.float32)
        before = (zero, zero)
        before_shifted = jnp.zeros((16, LANES), jnp.bfloat16)
        columns = slice(half * LANES, (half + 1) * LANES)
        for b in range(blocks + 1):
            if b < blocks:
                wide = jnp.broadcast_to(spectrum_ref[half, pl.ds(b, 1), :], (8, LANES))
                now = tuple(
                    pltpu.roll(wide, 1 + 8 * h, 1, stride=1, stride_axis=0) for h in range(2)
                )
            else:
                now = (zero, zero)
            shifted = jnp.concatenate(
                [jnp.where(lane > row + 8 * h, now[h], before[h]) for h in range(2)], axis=0
            ).astype(jnp.bfloat16)
            j = blocks - 1 - b
            place = 0 if j < 0 else (j % tiles + 1) * LANES + j // tiles * WIDTH
            right_ref[pl.ds(place, 16), columns] = shifted
            for c in range(16, WIDTH, 16):
                right_ref[pl.ds(place + c, 16), columns] = pltpu.roll(
                    jnp.where(lane16 < LANES - c, shifted, before_shifted), c, 1
                )
            before, before_shifted = now, shifted

    def sums(low, high):
        left = jnp.concatenate(
            [
                jnp.concatenate(
                    [
                        left_ref[a, pl.ds(rows * t, rows * (offsets + 1)), :]
                        for t in range(tiles + 1)
                    ],
                    axis=1,
                )
                for a in range(low, high)
            ],
            axis=0,
        )
        return jnp.dot(left, right_ref[...], preferred_element_type=jnp.float32)

    slots = near * depth
    height = GROUPS // CHAINS * (offsets + 1) * rows

    @pl.loop(0, slots // 2)
    def _(pair):
        @pl.when((touch_of(2 * pair) >= 0) | (touch_of(2 * pair + 1) >= 0))
        def _():
            scales = [gather(2 * pair + half, half) for half in range(2)]
            make_left()
            for half in range(2):
                make_right(2 * pair + half, half)
            step = GROUPS // CHAINS
            for c in range(CHAINS):
                product_ref[c * height : (c + 1) * height, :] = sums(step * c, step * (c + 1))

            def found(a, o, half):
                at = (a * (offsets + 1) + o) * rows + half * per_touch
                return product_ref[at : at + per_touch, half * LANES : (half + 1) * LANES]

            for o in range(offsets):
                both = []
                for half in range(2):
                    total = found(0, o + 1, half)
                    for a in range(1, GROUPS):
                        shift = WIDTH * a
                        total = total + pltpu.roll(
                            jnp.where(
                                lane < LANES - shift, found(a, o + 1, half), found(a, o, half)
                            ),
                            shift,
                            1,
                        )
                    both.append(total * scales[half])
                answer_ref[
                    pl.ds(pl.multiple_of(16 * pair, 16), 16), o * LANES : (o + 1) * LANES
                ] = jnp.concatenate(both, axis=0).astype(jnp.bfloat16)

    back = [
        pltpu.make_async_copy(
            answer_ref.at[pl.ds(e * depth * per_touch, depth * per_touch), :],
            outs[e],
            sem_ref.at[e],
        )
        for e in range(near)
    ]
    for copy in back:
        copy.start()
    for copy in back:
        copy.wait()


def profile(part, depth, num_query, touches, me, shards, library):
    near = len(shards)
    blocks = library.shape[1]
    offsets = SHIFTS // LANES
    tiles = blocks // GROUPS
    records = shards[0].shape[0] - num_query * blocks
    per_block = rounded(depth, ROW_SLOTS) // ROW_SLOTS
    table = (rounded(near * per_block, 8), LANES)
    smem = pl.BlockSpec(memory_space=pltpu.SMEM)
    vmem = pl.BlockSpec(memory_space=pltpu.VMEM)
    hbm = pl.BlockSpec(memory_space=pl.ANY)
    answers = near * depth * PER_TOUCH
    flops = answers * 2 * (offsets + 1) * (blocks + 4) * LANES * LANES
    return pl.pallas_call(
        functools.partial(profile_kernel, near, depth, num_query, touches),
        out_shape=[
            jax.ShapeDtypeStruct((depth * PER_TOUCH, SHIFTS), jnp.bfloat16)
            for _ in range(near)
        ],
        in_specs=[smem] + [hbm] * near + [vmem],
        out_specs=[hbm] * near,
        scratch_shapes=[
            pltpu.VMEM((near, *shards[0].shape), jnp.bfloat16),
            pltpu.VMEM((records, LANES), jnp.float32),
            pltpu.VMEM(table, jnp.int32),
            pltpu.SMEM(table, jnp.int32),
            pltpu.VMEM((answers, SHIFTS), jnp.bfloat16),
            pltpu.VMEM(((blocks + offsets + 1) * 16, LANES), jnp.float32),
            pltpu.VMEM(((blocks + offsets + 1) * 16, LANES), jnp.bfloat16),
            pltpu.VMEM((2, blocks, LANES), jnp.float32),
            pltpu.VMEM((GROUPS, (tiles + offsets + 1) * 16, LANES), jnp.bfloat16),
            pltpu.VMEM(((tiles + 1) * LANES, 2 * LANES), jnp.bfloat16),
            pltpu.VMEM((GROUPS * (offsets + 1) * 16, 2 * LANES), jnp.float32),
            pltpu.SemaphoreType.DMA((near + 1,)),
        ],
        compiler_params=pltpu.CompilerParams(vmem_limit_bytes=VMEM_LIMIT),
        cost_estimate=pl.CostEstimate(
            flops=8 * flops, bytes_accessed=8 * 1024 * 1024, transcendentals=0
        ),
        name=f"profile_{part}",
    )(me, *shards, library)


def unpack_kernel(distance, near, depth, me_ref, table_ref, *refs):
    got, refs = refs[:near], refs[-3:]
    out_ref, stage_ref, sem_ref = refs
    per_block = rounded(depth, ROW_SLOTS) // ROW_SLOTS

    def copy(slot, touch):
        return pltpu.make_async_copy(stage_ref.at[slot], out_ref.at[touch], sem_ref.at[slot])

    def touch_of(e, s):
        block = jnp.bitwise_xor(me_ref[0], distance + e)
        line = block * per_block + s // ROW_SLOTS
        return table_ref[line, s % ROW_SLOTS * SLOT_LANES + 2 * PER_TOUCH] - 1

    for e in range(near):
        for s in range(depth):
            touch = touch_of(e, s)
            slot = e * depth + s

            @pl.when(touch >= 0)
            def _():
                stage_ref[slot] = got[e][s * PER_TOUCH : (s + 1) * PER_TOUCH, :].astype(
                    jnp.float32
                )
                copy(slot, touch).start()

    for e in range(near):
        for s in range(depth):
            touch = touch_of(e, s)

            @pl.when(touch >= 0)
            def _():
                copy(e * depth + s, touch).wait()


def unpack(distance, depth, touched, me, table, got, out):
    shifts = got[0].shape[1]
    near = len(got)
    smem = pl.BlockSpec(memory_space=pltpu.SMEM)
    vmem = pl.BlockSpec(memory_space=pltpu.VMEM)
    hbm = pl.BlockSpec(memory_space=pl.ANY)
    more = () if out is None else (out,)
    return pl.pallas_call(
        functools.partial(unpack_kernel, distance, near, depth),
        out_shape=jax.ShapeDtypeStruct((touched, PER_TOUCH, shifts), jnp.float32),
        in_specs=[smem] * 2 + [vmem] * near + [hbm] * len(more),
        out_specs=hbm,
        scratch_shapes=[
            pltpu.VMEM((near * depth, PER_TOUCH, shifts), jnp.float32),
            pltpu.SemaphoreType.DMA((near * depth,)),
        ],
        input_output_aliases={2 + near: 0} if more else {},
        compiler_params=pltpu.CompilerParams(vmem_limit_bytes=VMEM_LIMIT),
        cost_estimate=pl.CostEstimate(
            flops=0, bytes_accessed=near * got[0].size * 6, transcendentals=0
        ),
        name=f"unpack_{distance}",
    )(me, table, *got, *more)


def local(spectra, library, cand_block, cand_local):
    devices = lax.axis_size("lib")
    num_query, num_bins = spectra.shape
    touches, per_touch = cand_local.shape[1], cand_local.shape[2]
    depth = rounded(depth_of(num_query, touches, devices), 2)
    blocks = num_bins // LANES
    records = rounded(devices * (rounded(depth, ROW_SLOTS) // ROW_SLOTS), 16)
    me = lax.axis_index("lib").astype(jnp.int32).reshape(1)

    def across(value, distance):
        if distance == 0:
            return value
        pairs = [(i, i ^ distance) for i in range(devices)]
        return lax.ppermute(value, "lib", pairs)

    shard, table = prepare(
        spectra, cand_block, cand_local.reshape(-1, per_touch), depth, records
    )
    far = devices // NEAR
    order = [0] + list(range(far - 1, 0, -1))
    heads = {part: across(shard, NEAR * part) for part in order}
    shards = {
        part: [across(heads[part], e) for e in range(NEAR)] for part in order
    }
    rows = library.reshape(-1, blocks, LANES)
    steps = [(part, 0, NEAR) for part in order[:-1]]
    half = NEAR // 2
    steps += [(order[-1], first, half) for first in (0, half)]
    got = {}
    for part, first, count in steps:
        distance = NEAR * part + first
        answers = profile(
            distance, depth, num_query, touches, me, shards[part][first : first + count], rows
        )
        got[distance] = [across(answer, distance + e) for e, answer in enumerate(answers)]
    out = None
    for distance, answers in got.items():
        out = unpack(distance, depth, num_query * touches, me, table, answers, out)
    return out.reshape(num_query, touches * per_touch, SHIFTS)


def solution(mesh):
    placed = (
        P(("groups", "lib"), None),
        P("lib", None),
        P(("groups", "lib"), None),
        P(("groups", "lib"), None, None),
    )
    return jax.shard_map(
        local,
        mesh=mesh,
        in_specs=placed,
        out_specs=P(("groups", "lib"), None, None),
        check_vma=False,
    )
```

```python
import functools

import jax
import jax.numpy as jnp
from jax import lax
from jax.experimental import pallas as pl
from jax.experimental.pallas import tpu as pltpu
from jax.sharding import PartitionSpec as P

SHIFTS = 1024
BG = 32
EPSILON = 1e-06
LANES = 128
VMEM_LIMIT = 48 * 1024 * 1024
NEAR = 4
ROW_SLOTS = 4
SLOT_LANES = LANES // ROW_SLOTS
PER_TOUCH = 8
CHAINS = 1
GROUPS = 4
WIDTH = LANES // GROUPS


def rounded(value, unit):
    return -(-value // unit) * unit


def depth_of(num_query, touches, devices):
    return min(num_query, max(3, 3 * num_query * touches // (2 * devices)))


def record_values(found):
    lane = lax.broadcasted_iota(jnp.int32, found.shape, 1) % SLOT_LANES
    low = pltpu.roll(found, LANES - PER_TOUCH, 1)
    return jnp.where(lane < PER_TOUCH, found * 16 + low, found).astype(jnp.int32)


def prepare_kernel(depth, spectra_ref, named_ref, wanted_ref, out_ref, table_ref, rows_ref):
    num_query, num_bins = spectra_ref.shape
    blocks = num_bins // LANES
    values = spectra_ref[...].astype(jnp.float32)
    zeros = jnp.zeros((num_query, LANES), jnp.float32)
    wide = jnp.concatenate([values, zeros], axis=1)
    total, length = wide, 1
    while length < 2 * BG:
        total = total + pltpu.roll(total, length, 1)
        length *= 2
    total = total + pltpu.roll(wide, length, 1)
    total = pltpu.roll(total, total.shape[1] - BG, 1)[:, :num_bins]
    centered = values - total / (2 * BG + 1)
    factor = lax.rsqrt(jnp.mean(centered * centered, axis=1, keepdims=True) + EPSILON)
    prepared = (centered * factor).astype(jnp.bfloat16)
    row = lax.broadcasted_iota(jnp.int32, (LANES, LANES), 0)
    col = lax.broadcasted_iota(jnp.int32, (LANES, LANES), 1)
    flip = jnp.where(row + col == LANES - 1, 1.0, 0.0).astype(jnp.bfloat16)
    for block in range(blocks):
        piece = prepared[:, block * LANES : (block + 1) * LANES]
        turned = jnp.dot(piece, flip, preferred_element_type=jnp.float32)
        rows_ref[pl.ds(blocks - 1 - block, num_query, stride=blocks), :] = turned
    out_ref[0 : num_query * blocks, :] = rows_ref[...].astype(jnp.bfloat16)

    touches = named_ref.shape[1]
    touched = num_query * touches
    records = table_ref.shape[0]
    per_block = rounded(depth, ROW_SLOTS) // ROW_SLOTS
    touch = lax.broadcasted_iota(jnp.int32, (touched, num_query), 0)
    query = lax.broadcasted_iota(jnp.int32, (touched, num_query), 1)
    owner = jnp.where(touch // touches == query, 1.0, 0.0).astype(jnp.bfloat16)
    named = named_ref[...].astype(jnp.float32).astype(jnp.bfloat16)
    spread = jnp.dot(owner, named, preferred_element_type=jnp.float32)
    touch = lax.broadcasted_iota(jnp.int32, (touched, touches), 0)
    which = lax.broadcasted_iota(jnp.int32, (touched, touches), 1)
    block_col = jnp.sum(
        jnp.where(touch % touches == which, spread, 0.0), axis=1, keepdims=True
    )
    row = lax.broadcasted_iota(jnp.int32, (touched, touched), 0)
    col = lax.broadcasted_iota(jnp.int32, (touched, touched), 1)
    block_row = jnp.sum(jnp.where(row == col, block_col, 0.0), axis=0, keepdims=True)
    earlier = (block_col == block_row) & (row < col)
    rank = jnp.sum(jnp.where(earlier, 1.0, 0.0), axis=0, keepdims=True).astype(jnp.int32)
    place = block_row.astype(jnp.int32) * per_block + rank // ROW_SLOTS
    wanted = wanted_ref[...]
    high = (wanted // 16).astype(jnp.float32).astype(jnp.bfloat16)
    low = (wanted % 16).astype(jnp.float32).astype(jnp.bfloat16)
    unit = lax.broadcasted_iota(jnp.int32, (PER_TOUCH, LANES), 0)
    lane = lax.broadcasted_iota(jnp.int32, (PER_TOUCH, LANES), 1)
    row = lax.broadcasted_iota(jnp.int32, (records, touched), 0)
    touch = lax.broadcasted_iota(jnp.int32, (touched, LANES), 0)
    wide_lane = lax.broadcasted_iota(jnp.int32, (touched, LANES), 1)
    found = jnp.zeros((records, LANES), jnp.float32)
    for group in range(ROW_SLOTS):
        start = group * SLOT_LANES
        to_high = jnp.where(lane == start + unit, 1.0, 0.0).astype(jnp.bfloat16)
        to_low = jnp.where(lane == start + PER_TOUCH + unit, 1.0, 0.0).astype(jnp.bfloat16)
        data = jnp.dot(high, to_high, preferred_element_type=jnp.float32)
        data = data + jnp.dot(low, to_low, preferred_element_type=jnp.float32)
        data = jnp.where(
            wide_lane == start + 2 * PER_TOUCH, (touch + 1).astype(jnp.float32), data
        ).astype(jnp.bfloat16)
        pick = jnp.where((row == place) & (rank % ROW_SLOTS == group), 1.0, 0.0)
        found = found + jnp.dot(
            pick.astype(jnp.bfloat16), data, preferred_element_type=jnp.float32
        )
    out_ref[num_query * blocks :, :] = found.astype(jnp.bfloat16)
    table_ref[...] = record_values(found)


def prepare(spectra, named, wanted, depth, records):
    num_query, num_bins = spectra.shape
    rows = num_query * num_bins // LANES
    return pl.pallas_call(
        functools.partial(prepare_kernel, depth),
        out_shape=(
            jax.ShapeDtypeStruct((rows + records, LANES), jnp.bfloat16),
            jax.ShapeDtypeStruct((records, LANES), jnp.int32),
        ),
        scratch_shapes=[pltpu.VMEM((rows, LANES), jnp.float32)],
        compiler_params=pltpu.CompilerParams(vmem_limit_bytes=VMEM_LIMIT),
        name="prepare",
    )(spectra, named, wanted)


def profile_kernel(depth, num_query, touches, me_ref, *refs):
    shards, library_ref, refs = refs[:NEAR], refs[NEAR], refs[NEAR + 1 :]
    outs, refs = refs[:NEAR], refs[NEAR:]
    (
        query_ref, record_ref, found_ref, table_ref, answer_ref,
        cand_ref, packed_ref, spectrum_ref, left_ref, right_ref, product_ref, sem_ref,
    ) = refs
    per_touch = PER_TOUCH
    rows = 2 * per_touch
    blocks = library_ref.shape[1]
    offsets = SHIFTS // LANES
    first = offsets // 2 + 1
    tiles = blocks // GROUPS
    query_rows = num_query * blocks
    per_block = rounded(depth, ROW_SLOTS) // ROW_SLOTS
    row = lax.broadcasted_iota(jnp.int32, (8, LANES), 0)
    lane = lax.broadcasted_iota(jnp.int32, (8, LANES), 1)
    lane16 = lax.broadcasted_iota(jnp.int32, (rows, LANES), 1)

    copies = [
        pltpu.make_async_copy(shards[e], query_ref.at[e], sem_ref.at[e]) for e in range(NEAR)
    ]
    for copy in copies:
        copy.start()
    cand_ref[...] = jnp.zeros(cand_ref.shape, cand_ref.dtype)
    right_ref[...] = jnp.zeros(right_ref.shape, right_ref.dtype)
    found_ref[...] = jnp.zeros(found_ref.shape, found_ref.dtype)
    for e in range(NEAR):
        copies[e].wait()
        record_ref[...] = query_ref[e, query_rows:, :].astype(jnp.float32)
        found_ref[e * per_block : (e + 1) * per_block, :] = record_values(
            record_ref[pl.ds(me_ref[0] * per_block, per_block), :]
        )
    to_scalars = pltpu.make_async_copy(found_ref, table_ref, sem_ref.at[NEAR])
    to_scalars.start()
    to_scalars.wait()

    def entry(slot):
        e = slot // depth
        s = slot % depth
        return e, e * per_block + s // ROW_SLOTS, s % ROW_SLOTS * SLOT_LANES

    def touch_of(slot):
        _, line, start = entry(slot)
        return table_ref[line, start + 2 * per_touch] - 1

    def choose(pieces):
        value = pieces[0]
        for group in range(1, GROUPS):
            value = jnp.where(lane16 < group * WIDTH, value, pieces[group])
        return value

    def gather(slot, half):
        _, line, start = entry(slot)
        for k in range(per_touch):
            wanted = table_ref[line, start + k]
            cand_ref[pl.ds(first * rows + half * per_touch + k, blocks, stride=rows), :] = (
                library_ref[wanted].astype(jnp.float32)
            )
        square = jnp.zeros((per_touch, LANES), jnp.float32)
        for b in range(blocks):
            piece = cand_ref[pl.ds((first + b) * rows + half * per_touch, per_touch), :]
            square = square + piece * piece
        mean = jnp.sum(square, axis=1, keepdims=True) / (blocks * LANES)
        return lax.rsqrt(mean + EPSILON)

    def make_left():
        for b in range(blocks + offsets + 1):
            packed_ref[pl.ds(rows * b, rows), :] = cand_ref[pl.ds(rows * b, rows), :].astype(
                jnp.bfloat16
            )
        for t in range(tiles + offsets + 1):
            given = [packed_ref[pl.ds(rows * (t + tiles * g), rows), :] for g in range(GROUPS)]
            turned = []
            for c in range(GROUPS):
                mixed = choose([given[(a + c) % GROUPS] for a in range(GROUPS)])
                turned.append(pltpu.roll(mixed, WIDTH * c, 1) if c else mixed)
            for a in range(GROUPS):
                left_ref[a, pl.ds(rows * t, rows), :] = choose(
                    [turned[(g - a) % GROUPS] for g in range(GROUPS)]
                )

    def make_right(slot, half):
        query = jnp.maximum(touch_of(slot), 0) // touches
        spectrum_ref[half] = query_ref[
            entry(slot)[0], pl.ds(pl.multiple_of(query * blocks, blocks), blocks), :
        ].astype(jnp.float32)
        zero = jnp.zeros((8, LANES), jnp.float32)
        columns = slice(half * LANES, (half + 1) * LANES)

        def joined(top, bottom):
            return jnp.concatenate([top, bottom], axis=0).astype(jnp.bfloat16)

        before = last = zero
        before_shifted = jnp.zeros((16, LANES), jnp.bfloat16)
        for first_b in range(0, blocks + 2, 2):
            low = []
            for b in (first_b, first_b + 1):
                if b < blocks:
                    wide = jnp.broadcast_to(spectrum_ref[half, pl.ds(b, 1), :], (8, LANES))
                    now = pltpu.roll(wide, 1, 1, stride=1, stride_axis=0)
                else:
                    now = zero
                low.append(jnp.where(lane > row, now, before))
                before = now
            more = pltpu.roll(
                jnp.where(lane16 < LANES - 8, joined(low[0], low[1]), joined(last, low[0])), 8, 1
            ).astype(jnp.float32)
            last = low[1]
            for side, b in enumerate((first_b, first_b + 1)):
                if b > blocks:
                    continue
                shifted = joined(low[side], more[8 * side : 8 * side + 8])
                j = blocks - 1 - b
                place = 0 if j < 0 else (j % tiles + 1) * LANES + j // tiles * WIDTH
                right_ref[pl.ds(place, 16), columns] = shifted
                for c in range(16, WIDTH, 16):
                    right_ref[pl.ds(place + c, 16), columns] = pltpu.roll(
                        jnp.where(lane16 < LANES - c, shifted, before_shifted), c, 1
                    )
                before_shifted = shifted

    def sums(low, high):
        left = jnp.concatenate(
            [
                jnp.concatenate(
                    [
                        left_ref[a, pl.ds(rows * t, rows * (offsets + 1)), :]
                        for t in range(tiles + 1)
                    ],
                    axis=1,
                )
                for a in range(low, high)
            ],
            axis=0,
        )
        return jnp.dot(left, right_ref[...], preferred_element_type=jnp.float32)

    slots = NEAR * depth
    height = GROUPS // CHAINS * (offsets + 1) * rows

    @pl.loop(0, slots // 2)
    def _(pair):
        @pl.when((touch_of(2 * pair) >= 0) | (touch_of(2 * pair + 1) >= 0))
        def _():
            scales = [gather(2 * pair + half, half) for half in range(2)]
            make_left()
            for half in range(2):
                make_right(2 * pair + half, half)
            step = GROUPS // CHAINS
            for c in range(CHAINS):
                product_ref[c * height : (c + 1) * height, :] = sums(step * c, step * (c + 1))

            def found(a, o, half):
                at = (a * (offsets + 1) + o) * rows + half * per_touch
                return product_ref[at : at + per_touch, half * LANES : (half + 1) * LANES]

            for o in range(offsets):
                both = []
                for half in range(2):
                    total = found(0, o + 1, half)
                    for a in range(1, GROUPS):
                        shift = WIDTH * a
                        total = total + pltpu.roll(
                            jnp.where(
                                lane < LANES - shift, found(a, o + 1, half), found(a, o, half)
                            ),
                            shift,
                            1,
                        )
                    both.append(total * scales[half])
                answer_ref[
                    pl.ds(pl.multiple_of(16 * pair, 16), 16), o * LANES : (o + 1) * LANES
                ] = jnp.concatenate(both, axis=0).astype(jnp.bfloat16)

    back = [
        pltpu.make_async_copy(
            answer_ref.at[pl.ds(e * depth * per_touch, depth * per_touch), :],
            outs[e],
            sem_ref.at[e],
        )
        for e in range(NEAR)
    ]
    for copy in back:
        copy.start()
    for copy in back:
        copy.wait()


def profile(part, depth, num_query, touches, me, shards, library):
    blocks = library.shape[1]
    offsets = SHIFTS // LANES
    tiles = blocks // GROUPS
    records = shards[0].shape[0] - num_query * blocks
    per_block = rounded(depth, ROW_SLOTS) // ROW_SLOTS
    table = (rounded(NEAR * per_block, 8), LANES)
    smem = pl.BlockSpec(memory_space=pltpu.SMEM)
    vmem = pl.BlockSpec(memory_space=pltpu.VMEM)
    hbm = pl.BlockSpec(memory_space=pl.ANY)
    answers = NEAR * depth * PER_TOUCH
    flops = answers * 2 * (offsets + 1) * (blocks + 4) * LANES * LANES
    return pl.pallas_call(
        functools.partial(profile_kernel, depth, num_query, touches),
        out_shape=[
            jax.ShapeDtypeStruct((depth * PER_TOUCH, SHIFTS), jnp.bfloat16)
            for _ in range(NEAR)
        ],
        in_specs=[smem] + [hbm] * NEAR + [vmem],
        out_specs=[hbm] * NEAR,
        scratch_shapes=[
            pltpu.VMEM((NEAR, *shards[0].shape), jnp.bfloat16),
            pltpu.VMEM((records, LANES), jnp.float32),
            pltpu.VMEM(table, jnp.int32),
            pltpu.SMEM(table, jnp.int32),
            pltpu.VMEM((answers, SHIFTS), jnp.bfloat16),
            pltpu.VMEM(((blocks + offsets + 1) * 16, LANES), jnp.float32),
            pltpu.VMEM(((blocks + offsets + 1) * 16, LANES), jnp.bfloat16),
            pltpu.VMEM((2, blocks, LANES), jnp.float32),
            pltpu.VMEM((GROUPS, (tiles + offsets + 1) * 16, LANES), jnp.bfloat16),
            pltpu.VMEM(((tiles + 1) * LANES, 2 * LANES), jnp.bfloat16),
            pltpu.VMEM((GROUPS * (offsets + 1) * 16, 2 * LANES), jnp.float32),
            pltpu.SemaphoreType.DMA((NEAR + 1,)),
        ],
        compiler_params=pltpu.CompilerParams(vmem_limit_bytes=VMEM_LIMIT),
        cost_estimate=pl.CostEstimate(
            flops=8 * flops, bytes_accessed=8 * 1024 * 1024, transcendentals=0
        ),
        name=f"profile_{part}",
    )(me, *shards, library)


def unpack_kernel(part, depth, me_ref, table_ref, *refs):
    got, refs = refs[:NEAR], refs[-3:]
    out_ref, stage_ref, sem_ref = refs
    per_block = rounded(depth, ROW_SLOTS) // ROW_SLOTS

    def copy(slot, touch):
        return pltpu.make_async_copy(stage_ref.at[slot], out_ref.at[touch], sem_ref.at[slot])

    def touch_of(e, s):
        block = jnp.bitwise_xor(me_ref[0], NEAR * part + e)
        line = block * per_block + s // ROW_SLOTS
        return table_ref[line, s % ROW_SLOTS * SLOT_LANES + 2 * PER_TOUCH] - 1

    for e in range(NEAR):
        for s in range(depth):
            touch = touch_of(e, s)
            slot = e * depth + s

            @pl.when(touch >= 0)
            def _():
                stage_ref[slot] = got[e][s * PER_TOUCH : (s + 1) * PER_TOUCH, :].astype(
                    jnp.float32
                )
                copy(slot, touch).start()

    for e in range(NEAR):
        for s in range(depth):
            touch = touch_of(e, s)

            @pl.when(touch >= 0)
            def _():
                copy(e * depth + s, touch).wait()


def unpack(part, depth, touched, me, table, got, out):
    shifts = got[0].shape[1]
    smem = pl.BlockSpec(memory_space=pltpu.SMEM)
    vmem = pl.BlockSpec(memory_space=pltpu.VMEM)
    hbm = pl.BlockSpec(memory_space=pl.ANY)
    more = () if out is None else (out,)
    return pl.pallas_call(
        functools.partial(unpack_kernel, part, depth),
        out_shape=jax.ShapeDtypeStruct((touched, PER_TOUCH, shifts), jnp.float32),
        in_specs=[smem] * 2 + [vmem] * NEAR + [hbm] * len(more),
        out_specs=hbm,
        scratch_shapes=[
            pltpu.VMEM((NEAR * depth, PER_TOUCH, shifts), jnp.float32),
            pltpu.SemaphoreType.DMA((NEAR * depth,)),
        ],
        input_output_aliases={2 + NEAR: 0} if more else {},
        compiler_params=pltpu.CompilerParams(vmem_limit_bytes=VMEM_LIMIT),
        cost_estimate=pl.CostEstimate(
            flops=0, bytes_accessed=NEAR * got[0].size * 6, transcendentals=0
        ),
        name=f"unpack_{part}",
    )(me, table, *got, *more)


def local(spectra, library, cand_block, cand_local):
    devices = lax.axis_size("lib")
    num_query, num_bins = spectra.shape
    touches, per_touch = cand_local.shape[1], cand_local.shape[2]
    depth = rounded(depth_of(num_query, touches, devices), 2)
    blocks = num_bins // LANES
    records = rounded(devices * (rounded(depth, ROW_SLOTS) // ROW_SLOTS), 16)
    me = lax.axis_index("lib").astype(jnp.int32).reshape(1)

    def across(value, distance):
        if distance == 0:
            return value
        pairs = [(i, i ^ distance) for i in range(devices)]
        return lax.ppermute(value, "lib", pairs)

    shard, table = prepare(
        spectra, cand_block, cand_local.reshape(-1, per_touch), depth, records
    )
    far = devices // NEAR
    order = [0] + list(range(far - 1, 0, -1))
    heads = {part: across(shard, NEAR * part) for part in order}
    shards = {
        part: [across(heads[part], e) for e in range(NEAR)] for part in order
    }
    rows = library.reshape(-1, blocks, LANES)
    got = {}
    for part in order:
        answers = profile(part, depth, num_query, touches, me, shards[part], rows)
        got[part] = [across(answers[e], NEAR * part + e) for e in range(NEAR)]
    out = None
    for part in order:
        out = unpack(part, depth, num_query * touches, me, table, got[part], out)
    return out.reshape(num_query, touches * per_touch, SHIFTS)


def solution(mesh):
    placed = (
        P(("groups", "lib"), None),
        P("lib", None),
        P(("groups", "lib"), None),
        P(("groups", "lib"), None, None),
    )
    return jax.shard_map(
        local,
        mesh=mesh,
        in_specs=placed,
        out_specs=P(("groups", "lib"), None, None),
        check_vma=False,
    )
```
